32 devices in a mesh: groups: 2 (over x), patch: 4 (over y, core), feat: 4 (over z).
Axes of the slice: x: 2, y: 2, z: 4, core: 2. Of those that a mesh axis runs over, the one named last changes fastest.
Arguments:
- node_lat: bfloat16 [8192, 512], P(('groups', 'patch', 'feat')), parts along dimension 0, may hold values from -6 to 6
- edge_lat: bfloat16 [8192, 8, 512], P(('groups', 'patch', 'feat')), parts along dimension 0, may hold values from -6 to 6
- neighbours: int32 [8, 4096], P(None, ('patch', 'feat')), may hold values from 0 to 1280, as said below
- send_rows: int32 [1024], P('patch'), may hold values from 0 to 1023
- coarse_of: int32 [4096], P(('patch', 'feat')), may hold values from 0 to 63
- weight_in: bfloat16 [1536, 512], replicated, may hold values from -0.15625 to 0.15625
- bias_in: float32 [512], replicated, may hold values from -3 to 3
- weight_out: bfloat16 [512, 512], replicated, may hold values from -0.25 to 0.25
- norm_gain: float32 [512], replicated, may hold values from 0.1 to 1.9
- edge_cotangent: bfloat16 [8192, 8, 512], P(('groups', 'patch', 'feat')), parts along dimension 0, may hold values from -6 to 6
- node_cotangent: bfloat16 [8192, 512], P(('groups', 'patch', 'feat')), parts along dimension 0, may hold values from -6 to 6
Outputs:
- edge_new: bfloat16 [8192, 8, 512], P(('groups', 'patch', 'feat')), parts along dimension 0
- node_new: bfloat16 [8192, 512], P(('groups', 'patch', 'feat')), parts along dimension 0
- grad_edge: bfloat16 [8192, 8, 512], P(('groups', 'patch', 'feat')), parts along dimension 0
- grad_node: bfloat16 [8192, 512], P(('groups', 'patch', 'feat')), parts along dimension 0
- grad_weight_in: float32 [3072, 512], P(('groups', 'patch'), 'feat'), parts along dimension 0
- grad_weight_out: float32 [1024, 512], P(('groups', 'patch'), 'feat'), parts along dimension 0
The draws below stay inside these ranges and needn't reach their ends.
There are 2 independent parts, one for each index of `groups`. The reference program is written for one: setup_inputs(seed, part) draws one part's arguments, and reference() takes and returns one part's arrays. A program takes and returns all parts, laid end to end along the dimension named above; an argument that names none is the same for every part. Nothing has to cross between parts.
Inputs may be any that keep to these rules, and one draw needn't show every extreme that they name: `neighbours`: value 1024 + 2 * 128 marks an empty slot; smaller values index a patch's 1024 rows, then the 128 rows from the lower patch, then the 128 rows from the upper patch.
All inputs are finite; a program needn't handle non-finite values.
Results may differ from the reference program's by a relative error of at most 0.0049.
Values may be sent and summed in bfloat16 or wider, within the bound.
No kernel may reach another device: no remote copies, remote signals or barrier semaphores. Data moves between devices by JAX's collectives and lax.ppermute only.
A program may use at most 128 MiB of HBM per device.

```python
import math
import jax
import jax.numpy as jnp
import numpy as np
from jax import lax

D = 512
H = 512
DEG = 8
NODES = 1024
TOTAL_NODES = 4096
HALO = 128
COARSE = 64
N_PATCH = 4


def draw_neighbours(key, part):
    key = jax.random.fold_in(key, 7)
    first, second = jax.random.split(key)
    table_rows = NODES + 2 * HALO
    missing = jax.random.randint(first, (TOTAL_NODES,), 0, 3)
    missing = missing.at[0].set(1)
    degree = DEG - missing
    chosen = jax.random.randint(second, (DEG, TOTAL_NODES), 0, table_rows)
    slots = jnp.arange(DEG)[:, None]
    return jnp.where(slots < degree[None, :], chosen, table_rows).astype(jnp.int32)


def place_ends(result, key, least, high):
    extent = result.shape
    index_at = [jax.random.randint(jax.random.fold_in(key, axis), (), 0, extent[axis]) for axis in range(len(extent))]
    result = result.at[tuple(index_at)].set(least)
    longest = extent.index(max(extent))
    index_at[longest] = (index_at[longest] + 1) % extent[longest]
    return result.at[tuple(index_at)].set(high)


def levels(rng, shape, cuts, smallest, high):
    loudness, own = 1.0, jax.random.fold_in(rng, 6)
    for position, shards_of in cuts:
        heights = jnp.exp(jax.random.uniform(jax.random.fold_in(own, position), (shards_of,), jnp.float32, smallest / len(cuts), high / len(cuts)))
        loudness = loudness * jnp.repeat(heights, shape[position] // shards_of).reshape([-1 if axis == position else 1 for axis in range(len(shape))])
    return loudness


def rank_table(number_of, skew):
    portions = [(1 << 20) // math.isqrt(rank ** skew) + 1 for rank in range(1, number_of + 1)]
    deviation = 1 + sum(portions) // (1 << 30)
    return np.cumsum(np.array([max(1, weight // deviation) for weight in portions]))


def ranked_ids(key, dims, count, skew):
    table = rank_table(count, skew)
    lot = jax.random.randint(jax.random.fold_in(key, 1), dims, 0, int(table[count - 1]))
    standing = jnp.searchsorted(jnp.asarray(table, jnp.int32), lot, side="right")
    return jax.random.permutation(jax.random.fold_in(key, 2), count)[standing].astype(jnp.int32)


def bell_draw(key, shape, width, bound, cuts=(), held_as=jnp.bfloat16):
    entries = jax.random.normal(key, shape, jnp.float32) * width
    if len(cuts) > 0:
        entries = levels(key, shape, cuts, -0.22, 0.18) * entries
    return jnp.clip(entries, min=-bound, max=bound).astype(held_as)


def setup_inputs(seed: int = 0, part: int = 0) -> dict:
    keys = jax.random.split(jax.random.key(seed), 12)
    own_keys = jax.random.split(jax.random.fold_in(keys[11], part), 12)
    return {
        "node_lat": bell_draw(own_keys[0], (TOTAL_NODES, D), 1.0, 6.0, ((0, 16),)),
        "edge_lat": bell_draw(own_keys[1], (TOTAL_NODES, DEG, D), 1.0, 6.0, ((0, 16),)),
        "neighbours": draw_neighbours(jax.random.fold_in(keys[11], 71), part),
        "send_rows": place_ends(jax.random.randint(keys[3], (N_PATCH * 2 * HALO,), 0, NODES), jax.random.fold_in(keys[3], 1), 0, NODES - 1).astype(jnp.int32),
        "coarse_of": place_ends(ranked_ids(keys[4], (TOTAL_NODES,), COARSE, 2), jax.random.fold_in(keys[4], 3), 0, COARSE - 1).astype(jnp.int32),
        "weight_in": bell_draw(keys[5], (3 * D, H), (3 * D) ** -0.5, 0.15625),
        "bias_in": bell_draw(keys[6], (H,), 0.5, 3.0, (), jnp.float32),
        "weight_out": bell_draw(keys[7], (H, D), H ** -0.5, 0.25),
        "norm_gain": jnp.clip(1.0 + 0.18 * jax.random.normal(keys[8], (D,), jnp.float32), 0.1, 1.9),
        "edge_cotangent": bell_draw(own_keys[9], (TOTAL_NODES, DEG, D), 1.0, 6.0, ((0, 16),)),
        "node_cotangent": bell_draw(own_keys[10], (TOTAL_NODES, D), 1.0, 6.0, ((0, 16),)),
    }


LAYER_EPS = 1e-05

def swish_terms(preact):
    sigmoid_value = jax.nn.sigmoid(preact)
    return (preact * sigmoid_value, sigmoid_value * (1.0 + preact * (1.0 - sigmoid_value)))

def edge_block(own_nodes, edge_rows, sources, live_slots, edge_cot, node_cot, weight_in, bias_in, weight_out, norm_gain):
    node_count, degree, latent = edge_rows.shape
    hidden = weight_in.shape[1]
    edge_total = node_count * degree
    flat_edges = edge_rows.reshape(edge_total, latent)
    flat_sources = sources.reshape(edge_total, latent)
    node_term = jnp.dot(own_nodes, weight_in[2 * latent:], preferred_element_type=jnp.float32)
    preact = jnp.dot(flat_edges, weight_in[:latent], preferred_element_type=jnp.float32)
    preact = preact + jnp.dot(flat_sources, weight_in[latent:2 * latent], preferred_element_type=jnp.float32)
    preact = preact.reshape(node_count, degree, hidden) + node_term[:, None, :] + bias_in
    activation, slope_term = swish_terms(preact.reshape(edge_total, hidden))
    hidden_act = activation.astype(jnp.bfloat16)
    projected = jnp.dot(hidden_act, weight_out, preferred_element_type=jnp.float32)
    centre = projected - lax.optimization_barrier(jnp.mean(projected, axis=1, keepdims=True))
    inverse = lax.rsqrt(lax.optimization_barrier(jnp.mean(centre * centre, axis=1, keepdims=True)) + LAYER_EPS)
    normed = centre * inverse
    message = (normed * norm_gain).reshape(node_count, degree, latent)
    edge_cotan = edge_cot.astype(jnp.float32)
    edge_new = (edge_rows.astype(jnp.float32) + message).astype(jnp.bfloat16)
    aggregate = lax.optimization_barrier(jnp.sum(message * live_slots[:, :, None], axis=1))
    grad_message = edge_cotan + live_slots[:, :, None] * node_cot.astype(jnp.float32)[:, None, :]
    scaled = grad_message.reshape(edge_total, latent) * norm_gain
    grad_projected = inverse * (scaled - lax.optimization_barrier(jnp.mean(scaled, axis=1, keepdims=True)) - normed * lax.optimization_barrier(jnp.mean(scaled * normed, axis=1, keepdims=True)))
    grad_projected = grad_projected.astype(jnp.bfloat16)
    contract_cols = (((1,), (1,)), ((), ()))
    contract_rows = (((0,), (0,)), ((), ()))
    grad_hidden = lax.dot_general(grad_projected, weight_out, contract_cols, preferred_element_type=jnp.float32)
    grad_preact = (grad_hidden * slope_term).astype(jnp.bfloat16)
    grad_inputs = lax.dot_general(grad_preact, weight_in, contract_cols, preferred_element_type=jnp.float32)
    grad_edge = (edge_cotan + grad_inputs[:, :latent].reshape(node_count, degree, latent)).astype(jnp.bfloat16)
    grad_sources = grad_inputs[:, latent:2 * latent]
    grad_own = lax.optimization_barrier(jnp.sum(grad_inputs[:, 2 * latent:].reshape(node_count, degree, latent), axis=1))
    preact_sum = lax.optimization_barrier(jnp.sum(grad_preact.reshape(node_count, degree, hidden), axis=1, dtype=jnp.float32))
    grad_weight_in = jnp.concatenate([lax.dot_general(flat_edges, grad_preact, contract_rows, preferred_element_type=jnp.float32), lax.dot_general(flat_sources, grad_preact, contract_rows, preferred_element_type=jnp.float32), lax.dot_general(own_nodes.astype(jnp.float32), preact_sum, contract_rows, precision=lax.Precision.HIGHEST, preferred_element_type=jnp.float32)], axis=0)
    grad_weight_out = lax.dot_general(hidden_act, grad_projected, contract_rows, preferred_element_type=jnp.float32)
    return (edge_new, aggregate, grad_edge, grad_own, grad_sources, grad_weight_in, grad_weight_out)

def reference(node_lat, edge_lat, neighbours, send_rows, coarse_of, weight_in, bias_in, weight_out, norm_gain, edge_cotangent, node_cotangent):
    latent = node_lat.shape[1]
    table_rows = NODES + 2 * HALO
    total_nodes = N_PATCH * NODES
    patch_nodes = node_lat.reshape(N_PATCH, NODES, latent)
    patch_edges = edge_lat.reshape(N_PATCH, NODES, DEG, latent)
    patch_links = neighbours.reshape(DEG, N_PATCH, NODES).transpose(1, 2, 0)
    patch_sends = send_rows.reshape(N_PATCH, 2 * HALO)
    patch_ecot = edge_cotangent.reshape(N_PATCH, NODES, DEG, latent)
    patch_ncot = node_cotangent.reshape(N_PATCH, NODES, latent)
    outgoing = jax.vmap(lambda members, chosen: members[chosen])(patch_nodes, patch_sends)
    from_lower = jnp.roll(outgoing[:, HALO:], 1, axis=0)
    from_upper = jnp.roll(outgoing[:, :HALO], -1, axis=0)
    blank_row = jnp.zeros((N_PATCH, 1, latent), node_lat.dtype)
    tables = jnp.concatenate([patch_nodes, from_lower, from_upper, blank_row], axis=1)

    def one_patch(patch_items):
        patch_table, members, edge_rows, neighbour_ids, edge_cot, node_cot = patch_items
        sources = patch_table[neighbour_ids]
        live_slots = (neighbour_ids != table_rows).astype(jnp.float32)
        results = edge_block(members, edge_rows, sources, live_slots, edge_cot, node_cot, weight_in, bias_in, weight_out, norm_gain)
        edge_new, aggregate, grad_edge, grad_own, grad_sources, grad_weight_in, grad_weight_out = results
        table_grad = jax.ops.segment_sum(grad_sources, neighbour_ids.reshape(-1), table_rows + 1)
        return (edge_new, aggregate, grad_edge, grad_own + table_grad[:NODES], table_grad[NODES:NODES + HALO], table_grad[NODES + HALO:table_rows], grad_weight_in, grad_weight_out)
    outputs = lax.map(one_patch, (tables, patch_nodes, patch_edges, patch_links, patch_ecot, patch_ncot))
    edge_new, aggregate, grad_edge, grad_patch, grad_lower, grad_upper, grad_weight_in, grad_weight_out = outputs
    returned = jnp.concatenate([jnp.roll(grad_upper, 1, axis=0), jnp.roll(grad_lower, -1, axis=0)], axis=1)
    rim_terms = jax.vmap(lambda values, chosen: jax.ops.segment_sum(values, chosen, NODES))(returned, patch_sends)
    counts = jax.ops.segment_sum(jnp.ones((total_nodes,), jnp.float32), coarse_of, COARSE)
    divisor = jnp.maximum(counts, 1.0)[:, None]
    pooled = jax.ops.segment_sum(node_lat.astype(jnp.float32), coarse_of, COARSE) / divisor
    spread = jax.ops.segment_sum(node_cotangent.astype(jnp.float32), coarse_of, COARSE) / divisor
    node_new = (node_lat.astype(jnp.float32) + aggregate.reshape(total_nodes, latent) + pooled[coarse_of]).astype(jnp.bfloat16)
    grad_node = (node_cotangent.astype(jnp.float32) + (grad_patch + rim_terms).reshape(total_nodes, latent) + spread[coarse_of]).astype(jnp.bfloat16)
    grad_scale = 1.0 / math.sqrt(total_nodes * DEG)
    return (edge_new.reshape(total_nodes, DEG, latent), node_new, grad_edge.reshape(total_nodes, DEG, latent), grad_node, lax.optimization_barrier(jnp.sum(grad_weight_in, axis=0)) * grad_scale, lax.optimization_barrier(jnp.sum(grad_weight_out, axis=0)) * grad_scale)
```

```python
import math

import jax
import jax.numpy as jnp
from jax import lax
from jax.experimental import pallas as pl
from jax.experimental.pallas import tpu as pltpu
from jax.sharding import PartitionSpec as P

COARSE_DEV = 4
LAYER_EPS = 1e-05
F32 = jnp.float32
BF16 = jnp.bfloat16
VMEM_LIMIT = 56 * 1024 * 1024
COLS = (((1,), (1,)), ((), ()))
ROWS = (((0,), (0,)), ((), ()))


def dot(a, b):
    return jnp.dot(a, b, preferred_element_type=F32)


def params():
    return pltpu.CompilerParams(vmem_limit_bytes=VMEM_LIMIT)


def cost(flops, bytes_accessed):
    return pl.CostEstimate(flops=int(flops), bytes_accessed=int(bytes_accessed), transcendentals=0)


def whole(array):
    zeros = (0,) * array.ndim
    return pl.BlockSpec(array.shape, lambda i: zeros)


def rows(array, block):
    rest = (0,) * (array.ndim - 1)
    return pl.BlockSpec((block,) + array.shape[1:], lambda i: (i,) + rest)


def one_hot(ids, first, count):
    lanes = lax.broadcasted_iota(jnp.int32, (ids.shape[0], count), 1) + first
    return jnp.where(ids == lanes, 1.0, 0.0).astype(BF16)


def base_kernel(degree, edge_ref, node_ref, ids_ref, own_ref, weight_ref, bias_ref, out_ref, table):
    latent = own_ref.shape[1]

    @pl.when(pl.program_id(0) == 0)
    def _():
        table[...] = dot(own_ref[...], weight_ref[latent : 2 * latent]).astype(BF16)

    edges = edge_ref.shape[0]
    term = dot(node_ref[...], weight_ref[2 * latent :]) + bias_ref[...]
    total = dot(edge_ref[...], weight_ref[:latent])
    total = total + dot(one_hot(ids_ref[...], 0, own_ref.shape[0]), table[...])
    hidden = total.shape[1]
    total = total.reshape(edges // degree, degree, hidden) + term[:, None, :]
    out_ref[...] = total.reshape(edges, hidden)


def base_call(edges, nodes, ids, weight_in, bias, block):
    count, latent = edges.shape
    hidden = weight_in.shape[1]
    degree = count // nodes.shape[0]
    return pl.pallas_call(
        lambda *refs: base_kernel(degree, *refs),
        grid=(count // block,),
        in_specs=[
            rows(edges, block),
            rows(nodes, block // degree),
            rows(ids, block),
            whole(nodes),
            whole(weight_in),
            whole(bias),
        ],
        out_specs=pl.BlockSpec((block, hidden), lambda i: (i, 0)),
        out_shape=jax.ShapeDtypeStruct((count, hidden), F32),
        scratch_shapes=[pltpu.VMEM(nodes.shape, BF16)],
        compiler_params=params(),
        cost_estimate=cost(2 * count * hidden * (latent + nodes.shape[0]), count * 3072),
        name="base_terms",
    )(edges, nodes, ids, nodes, weight_in, bias)


def gather_kernel(first, base_ref, ids_ref, piece_ref, weight_ref, out_ref, table):
    latent = piece_ref.shape[1]

    @pl.when(pl.program_id(0) == 0)
    def _():
        table[...] = dot(piece_ref[...], weight_ref[latent : 2 * latent]).astype(BF16)

    hot = one_hot(ids_ref[...], first, piece_ref.shape[0])
    out_ref[...] = base_ref[...] + dot(hot, table[...])


def gather_call(base, ids, piece, weight_in, first, block):
    count, hidden = base.shape
    return pl.pallas_call(
        lambda *refs: gather_kernel(first, *refs),
        grid=(count // block,),
        in_specs=[rows(base, block), rows(ids, block), whole(piece), whole(weight_in)],
        out_specs=rows(base, block),
        out_shape=jax.ShapeDtypeStruct(base.shape, F32),
        scratch_shapes=[pltpu.VMEM((piece.shape[0], hidden), BF16)],
        input_output_aliases={0: 0},
        compiler_params=params(),
        cost_estimate=cost(2 * count * hidden * piece.shape[0], count * 4096),
        name="gather_terms",
    )(base, ids, piece, weight_in)


def select_kernel(ids_ref, table_ref, out_ref):
    hot = one_hot(ids_ref[...], 0, table_ref.shape[0])
    out_ref[...] = dot(hot, table_ref[...]).astype(out_ref.dtype)


def select_call(ids, table):
    return pl.pallas_call(
        select_kernel,
        out_shape=jax.ShapeDtypeStruct((ids.shape[0], table.shape[1]), BF16),
        compiler_params=params(),
        cost_estimate=cost(2 * ids.shape[0] * table.shape[0] * table.shape[1], 1 << 21),
        name="select_rows",
    )(ids, table)


def edge_kernel(
    first,
    degree,
    base_ref,
    ids_ref,
    rim_ref,
    edge_ref,
    cot_ref,
    ncot_ref,
    weight_ref,
    out_w_ref,
    gain_ref,
    new_ref,
    agg_ref,
    hid_ref,
    gproj_ref,
    gpre_ref,
    psum_ref,
    gedge_ref,
    table,
):
    latent = rim_ref.shape[1]

    @pl.when(pl.program_id(0) == 0)
    def _():
        table[...] = dot(rim_ref[...], weight_ref[latent : 2 * latent]).astype(BF16)

    ids = ids_ref[...]
    edges = ids.shape[0]
    nodes = edges // degree
    limit = first + rim_ref.shape[0]
    live = jnp.where(ids < limit, 1.0, 0.0)
    value = base_ref[...] + dot(one_hot(ids, first, rim_ref.shape[0]), table[...])
    sig = jax.nn.sigmoid(value)
    act = value * sig
    slope = sig + act * (1.0 - sig)
    hid = act.astype(BF16)
    hid_ref[...] = hid
    projected = dot(hid, out_w_ref[...])
    centre = projected - jnp.mean(projected, axis=1, keepdims=True)
    inverse = lax.rsqrt(jnp.mean(centre * centre, axis=1, keepdims=True) + LAYER_EPS)
    normed = centre * inverse
    gain = gain_ref[...]
    message = normed * gain
    new_ref[...] = (edge_ref[...].astype(F32) + message).astype(BF16)
    agg_ref[...] = jnp.sum((message * live).reshape(nodes, degree, latent), axis=1)
    ncot = jnp.broadcast_to(ncot_ref[...].astype(F32)[:, None, :], (nodes, degree, latent))
    cot = cot_ref[...].astype(F32)
    scaled = (cot + live * ncot.reshape(edges, latent)) * gain
    mean_a = jnp.mean(scaled, axis=1, keepdims=True)
    mean_b = jnp.mean(scaled * normed, axis=1, keepdims=True)
    gproj = (inverse * (scaled - mean_a - normed * mean_b)).astype(BF16)
    gproj_ref[...] = gproj
    gpre = (lax.dot_general(gproj, out_w_ref[...], COLS, preferred_element_type=F32) * slope).astype(BF16)
    gpre_ref[...] = gpre
    psum_ref[...] = jnp.sum(gpre.astype(F32).reshape(nodes, degree, gpre.shape[1]), axis=1).astype(BF16)
    back = lax.dot_general(gpre, weight_ref[:latent], COLS, preferred_element_type=F32)
    gedge_ref[...] = (cot + back).astype(BF16)


def edge_call(base, ids, rim, edges, cots, ncot, weight_in, weight_out, gain, first, block):
    count, latent = edges.shape
    hidden = weight_in.shape[1]
    degree = count // ncot.shape[0]
    blocks = count // block
    small = block // degree

    def like(width, dtype, size, total):
        return (
            pl.BlockSpec((size, width), lambda i: (i, 0)),
            jax.ShapeDtypeStruct((total, width), dtype),
        )

    outs = [
        like(latent, BF16, block, count),
        like(latent, F32, small, count // degree),
        like(hidden, BF16, block, count),
        like(latent, BF16, block, count),
        like(hidden, BF16, block, count),
        like(hidden, BF16, small, count // degree),
        like(latent, BF16, block, count),
    ]
    return pl.pallas_call(
        lambda *refs: edge_kernel(first, degree, *refs),
        grid=(blocks,),
        in_specs=[
            rows(base, block),
            rows(ids, block),
            whole(rim),
            rows(edges, block),
            rows(cots, block),
            rows(ncot, small),
            whole(weight_in),
            whole(weight_out),
            whole(gain),
        ],
        out_specs=[spec for spec, _ in outs],
        out_shape=[shape for _, shape in outs],
        scratch_shapes=[pltpu.VMEM((rim.shape[0], hidden), BF16)],
        compiler_params=params(),
        cost_estimate=cost(2 * count * hidden * (3 * latent + rim.shape[0]), count * 10000),
        name="edge_block",
    )(base, ids, rim, edges, cots, ncot, weight_in, weight_out, gain)


def scatter_kernel(first, ids_ref, values_ref, out_ref):
    size = out_ref.shape[0]
    start = first + pl.program_id(0) * size
    places = lax.broadcasted_iota(jnp.int32, (size, ids_ref.shape[1]), 0) + start
    hot = jnp.where(places == ids_ref[...], 1.0, 0.0).astype(BF16)
    out_ref[...] = dot(hot, values_ref[...]).astype(out_ref.dtype)


def scatter_call(ids, values, first, count, block, dtype):
    width = values.shape[1]
    return pl.pallas_call(
        lambda *refs: scatter_kernel(first, *refs),
        grid=(count // block,),
        in_specs=[whole(ids), whole(values)],
        out_specs=pl.BlockSpec((block, width), lambda i: (i, 0)),
        out_shape=jax.ShapeDtypeStruct((count, width), dtype),
        compiler_params=params(),
        cost_estimate=cost(2 * count * width * values.shape[0], values.size * 2 + count * width * 4),
        name="scatter_rows",
    )(ids, values)


def scatter_more_kernel(ids_ref, values_ref, start_ref, out_ref):
    size = out_ref.shape[0]
    places = lax.broadcasted_iota(jnp.int32, (size, ids_ref.shape[1]), 0) + pl.program_id(0) * size
    hot = jnp.where(places == ids_ref[...], 1.0, 0.0).astype(BF16)
    out_ref[...] = (start_ref[...] + dot(hot, values_ref[...])).astype(out_ref.dtype)


def scatter_more_call(ids, values, start, block):
    count, width = start.shape
    return pl.pallas_call(
        scatter_more_kernel,
        grid=(count // block,),
        in_specs=[whole(ids), whole(values), rows(start, block)],
        out_specs=rows(start, block),
        out_shape=jax.ShapeDtypeStruct((count, width), BF16),
        compiler_params=params(),
        cost_estimate=cost(2 * count * width * values.shape[0], count * width * 6),
        name="scatter_more",
    )(ids, values, start)


def xor_swap(value, axis, distance):
    size = lax.axis_size(axis)
    return lax.ppermute(value, axis, [(i, i ^ distance) for i in range(size)])


def bits_of(size):
    return [1 << b for b in range(size.bit_length() - 1)]


def all_sum(value, axis):
    for distance in bits_of(lax.axis_size(axis)):
        value = value + xor_swap(value, axis, distance)
    return value


def shards(
    node_lat,
    edge_lat,
    neighbours,
    send_rows,
    coarse_of,
    weight_in,
    bias_in,
    weight_out,
    norm_gain,
    edge_cotangent,
    node_cotangent,
):
    node_count, latent = node_lat.shape
    degree = edge_lat.shape[1]
    edge_count = node_count * degree
    rim_rows = send_rows.shape[0] // 2
    feat_count = lax.axis_size("feat")
    patch_count = lax.axis_size("patch")
    patch_total = feat_count * node_count
    table_rows = patch_total + 2 * rim_rows
    coarse_total = COARSE_DEV * patch_count * feat_count
    feat = lax.axis_index("feat")
    patch = lax.axis_index("patch")
    block = min(512, edge_count)
    ring_up = [(i, (i + 1) % patch_count) for i in range(patch_count)]
    ring_down = [(j, i) for i, j in ring_up]

    def relative(ids):
        moved = ((ids // node_count) ^ feat) * node_count + ids % node_count
        return jnp.where(ids < patch_total, moved, ids)

    flat_edges = edge_lat.reshape(edge_count, latent)
    flat_cots = edge_cotangent.reshape(edge_count, latent)
    ids = relative(neighbours.T.reshape(edge_count))
    ids_col = ids[:, None]
    ids_row = ids[None, :]
    send_rel = relative(send_rows)
    bias = bias_in[None, :]
    gain = norm_gain[None, :]

    if feat_count == 4:
        far = xor_swap(node_lat, "feat", 2)
        near = xor_swap(node_lat, "feat", 1)
        last = xor_swap(far, "feat", 1)
        base = base_call(flat_edges, node_lat, ids_col, weight_in, bias, block)
        middle = jnp.concatenate([near, far], axis=0)
        table = jnp.concatenate([node_lat, near, far, last], axis=0)
        outgoing = select_call(send_rel[:, None], table)
        base = gather_call(base, ids_col, middle, weight_in, node_count, block)
        base = gather_call(base, ids_col, last, weight_in, 3 * node_count, block)
    else:
        table = node_lat
        for distance in bits_of(feat_count):
            table = jnp.concatenate([table, xor_swap(table, "feat", distance)], axis=0)
        outgoing = select_call(send_rel[:, None], table)
        base = base_call(flat_edges, node_lat, ids_col, weight_in, bias, block)
        base = gather_call(base, ids_col, table[node_count:], weight_in, node_count, block)
    from_lower = lax.ppermute(outgoing[rim_rows:], "patch", ring_up)
    from_upper = lax.ppermute(outgoing[:rim_rows], "patch", ring_down)
    rim = jnp.concatenate([from_lower, from_upper], axis=0)

    edge_new, aggregate, hidden_act, grad_proj, grad_pre, pre_sum, grad_edge = edge_call(
        base,
        ids_col,
        rim,
        flat_edges,
        flat_cots,
        node_cotangent,
        weight_in,
        weight_out,
        gain,
        patch_total,
        256,
    )

    rim_sum = scatter_call(ids_row, grad_pre, patch_total, 2 * rim_rows, 2 * rim_rows, BF16)
    back_upper = lax.ppermute(rim_sum[:rim_rows], "patch", ring_down)
    back_lower = lax.ppermute(rim_sum[rim_rows:], "patch", ring_up)
    patch_sum = scatter_call(ids_row, grad_pre, 0, patch_total, 256, F32)
    returned = jnp.concatenate([back_lower, back_upper], axis=0)
    chunks = scatter_more_call(send_rel[None, :], returned, patch_sum, node_count)
    if feat_count == 4:
        piece = [chunks[j * node_count : (j + 1) * node_count] for j in range(4)]
        relay = xor_swap(piece[3], "feat", 1)
        far_sum = (piece[2].astype(F32) + relay.astype(F32)).astype(BF16)
        got_far = xor_swap(far_sum, "feat", 2)
        got_near = xor_swap(piece[1], "feat", 1)
        own_sum = (piece[0].astype(F32) + got_far.astype(F32) + got_near.astype(F32)).astype(BF16)
    else:
        for distance in reversed(bits_of(feat_count)):
            half = distance * node_count
            got = xor_swap(chunks[half:], "feat", distance)
            chunks = (chunks[:half].astype(F32) + got.astype(F32)).astype(BF16)
        own_sum = chunks

    full_table = jnp.concatenate([table, rim], axis=0)
    full_sum = jnp.concatenate([patch_sum.astype(BF16), rim_sum], axis=0)

    def grad_dot(a, b):
        return lax.dot_general(a, b, ROWS, preferred_element_type=F32)

    in_rows = 3 * latent // patch_count
    out_rows = weight_out.shape[0] // patch_count
    hidden = weight_in.shape[1]
    grads_in = jnp.concatenate(
        [grad_dot(flat_edges, grad_pre), grad_dot(full_table, full_sum), grad_dot(node_lat, pre_sum)], axis=0
    )
    grads_out = grad_dot(hidden_act, grad_proj)
    grads = jnp.concatenate(
        [grads_in.reshape(patch_count, in_rows, hidden), grads_out.reshape(patch_count, out_rows, latent)], axis=1
    )
    span = in_rows + out_rows
    for distance in bits_of(patch_count):
        grads = grads.reshape(-1, 2, span, latent)
        bit = (patch // distance) % 2
        mine = lax.dynamic_index_in_dim(grads, bit, 1, keepdims=False)
        other = lax.dynamic_index_in_dim(grads, 1 - bit, 1, keepdims=False).astype(BF16)
        grads = mine + xor_swap(other, "patch", distance).astype(F32)
    width = latent // feat_count
    grads = grads.reshape(span, feat_count, width).transpose(1, 0, 2)
    for distance in bits_of(feat_count):
        grads = grads.reshape(-1, 2, span, width)
        bit = (feat // distance) % 2
        mine = lax.dynamic_index_in_dim(grads, bit, 1, keepdims=False)
        other = lax.dynamic_index_in_dim(grads, 1 - bit, 1, keepdims=False).astype(BF16)
        grads = mine + xor_swap(other, "feat", distance).astype(F32)
    grads = grads.reshape(span, width) * (1.0 / math.sqrt(edge_count * patch_count * feat_count))

    coarse_hot = (coarse_of[None, :] == jnp.arange(coarse_total)[:, None]).astype(BF16)
    counts = jnp.sum(coarse_hot.astype(F32), axis=1)
    sums = dot(coarse_hot, jnp.concatenate([node_lat, node_cotangent], axis=1))
    sums = jnp.concatenate([sums, jnp.broadcast_to(counts[:, None], (coarse_total, 128))], axis=1)
    sums = all_sum(all_sum(sums, "patch"), "feat")
    divisor = jnp.maximum(sums[:, 2 * latent :][:, :1], 1.0)
    means = (sums[:, : 2 * latent] / divisor).astype(BF16)
    spread = lax.dot_general(coarse_hot, means, ROWS, preferred_element_type=F32)

    node_new = (node_lat.astype(F32) + aggregate + spread[:, :latent]).astype(BF16)
    grad_node = node_cotangent.astype(F32) + spread[:, latent:]
    grad_node = grad_node + lax.dot_general(own_sum, weight_in[latent : 2 * latent], COLS, preferred_element_type=F32)
    grad_node = grad_node + lax.dot_general(pre_sum, weight_in[2 * latent :], COLS, preferred_element_type=F32)
    return (
        edge_new.reshape(edge_lat.shape),
        node_new,
        grad_edge.reshape(edge_lat.shape),
        grad_node.astype(BF16),
        grads[:in_rows],
        grads[in_rows:],
    )


def solution(mesh):
    return jax.shard_map(
        shards,
        mesh=mesh,
        in_specs=(
            P(("groups", "patch", "feat"), None),
            P(("groups", "patch", "feat"), None, None),
            P(None, ("patch", "feat")),
            P("patch"),
            P(("patch", "feat")),
            P(),
            P(),
            P(),
            P(),
            P(("groups", "patch", "feat"), None, None),
            P(("groups", "patch", "feat"), None),
        ),
        out_specs=(
            P(("groups", "patch", "feat"), None, None),
            P(("groups", "patch", "feat"), None),
            P(("groups", "patch", "feat"), None, None),
            P(("groups", "patch", "feat"), None),
            P(("groups", "patch"), "feat"),
            P(("groups", "patch"), "feat"),
        ),
        check_vma=False,
    )
```

```python
import math

import jax
import jax.numpy as jnp
from jax import lax
from jax.experimental import pallas as pl
from jax.experimental.pallas import tpu as pltpu
from jax.sharding import PartitionSpec as P

COARSE_DEV = 4
LAYER_EPS = 1e-05
F32 = jnp.float32
BF16 = jnp.bfloat16
VMEM_LIMIT = 24 * 1024 * 1024
COLS = (((1,), (1,)), ((), ()))
ROWS = (((0,), (0,)), ((), ()))


def dot(a, b):
    return jnp.dot(a, b, preferred_element_type=F32)


def params():
    return pltpu.CompilerParams(vmem_limit_bytes=VMEM_LIMIT)


def cost(micros):
    return pl.CostEstimate(flops=int(micros * 1.15e9), bytes_accessed=1 << 20, transcendentals=0)


def whole(array):
    zeros = (0,) * array.ndim
    return pl.BlockSpec(array.shape, lambda i: zeros)


def rows(array, block):
    rest = (0,) * (array.ndim - 1)
    return pl.BlockSpec((block,) + array.shape[1:], lambda i: (i,) + rest)


def one_hot(ids, first, count):
    lanes = lax.broadcasted_iota(jnp.int32, (ids.shape[0], count), 1) + first
    return jnp.where(ids == lanes, 1.0, 0.0).astype(BF16)


def fill_table(table, pieces, weight_ref):
    latent = pieces[0].shape[1]
    at = 0
    for piece in pieces:
        size = piece.shape[0]
        table[at : at + size] = dot(piece[...], weight_ref[latent : 2 * latent]).astype(BF16)
        at += size


def base_kernel(degree, edge_ref, node_ref, ids_ref, weight_ref, bias_ref, after_ref, *refs):
    pieces, (out_ref, table) = refs[:-2], refs[-2:]
    latent = edge_ref.shape[1]

    @pl.when(pl.program_id(0) == 0)
    def _():
        fill_table(table, pieces, weight_ref)

    edges = edge_ref.shape[0]
    term = dot(node_ref[...], weight_ref[2 * latent :]) + bias_ref[...]
    total = dot(edge_ref[...], weight_ref[:latent])
    total = total + dot(one_hot(ids_ref[...], 0, table.shape[0]), table[...])
    hidden = total.shape[1]
    total = total.reshape(edges // degree, degree, hidden) + term[:, None, :]
    out_ref[...] = total.reshape(edges, hidden)


def base_call(edges, nodes, ids, weight_in, bias, after, pieces, block):
    count, latent = edges.shape
    hidden = weight_in.shape[1]
    degree = count // nodes.shape[0]
    size = sum(piece.shape[0] for piece in pieces)
    return pl.pallas_call(
        lambda *refs: base_kernel(degree, *refs),
        grid=(count // block,),
        in_specs=[
            rows(edges, block),
            rows(nodes, block // degree),
            rows(ids, block),
            whole(weight_in),
            whole(bias),
            pl.BlockSpec(memory_space=pl.ANY),
        ]
        + [whole(piece) for piece in pieces],
        out_specs=pl.BlockSpec((block, hidden), lambda i: (i, 0)),
        out_shape=jax.ShapeDtypeStruct((count, hidden), F32),
        scratch_shapes=[pltpu.VMEM((size, hidden), BF16)],
        compiler_params=params(),
        cost_estimate=cost(5),
        name="base_terms",
    )(edges, nodes, ids, weight_in, bias, after, *pieces)


def edge_kernel(
    first,
    degree,
    base_ref,
    ids_ref,
    low_ref,
    high_ref,
    edge_ref,
    cot_ref,
    ncot_ref,
    weight_ref,
    out_w_ref,
    gain_ref,
    mine_ref,
    got_ref,
    new_ref,
    agg_ref,
    hid_ref,
    gproj_ref,
    gpre_ref,
    psum_ref,
    gedge_ref,
    sum_ref,
    table,
):
    latent = low_ref.shape[1]
    half = low_ref.shape[0]

    @pl.when(pl.program_id(0) == 0)
    def _():
        table[:half] = dot(low_ref[...], weight_ref[latent : 2 * latent]).astype(BF16)
        table[half:] = dot(high_ref[...], weight_ref[latent : 2 * latent]).astype(BF16)
        sum_ref[...] = mine_ref[...] + got_ref[...]

    ids = ids_ref[...]
    edges = ids.shape[0]
    nodes = edges // degree
    limit = first + 2 * half
    live = jnp.where(ids < limit, 1.0, 0.0)
    value = base_ref[...] + dot(one_hot(ids, first, 2 * half), table[...])
    sig = jax.nn.sigmoid(value)
    act = value * sig
    slope = sig + act * (1.0 - sig)
    hid = act.astype(BF16)
    hid_ref[...] = hid
    projected = dot(hid, out_w_ref[...])
    centre = projected - jnp.mean(projected, axis=1, keepdims=True)
    inverse = lax.rsqrt(jnp.mean(centre * centre, axis=1, keepdims=True) + LAYER_EPS)
    normed = centre * inverse
    gain = gain_ref[...]
    message = normed * gain
    new_ref[...] = (edge_ref[...].astype(F32) + message).astype(BF16)
    agg_ref[...] = jnp.sum((message * live).reshape(nodes, degree, latent), axis=1)
    ncot = jnp.broadcast_to(ncot_ref[...].astype(F32)[:, None, :], (nodes, degree, latent))
    cot = cot_ref[...].astype(F32)
    scaled = (cot + live * ncot.reshape(edges, latent)) * gain
    mean_a = jnp.mean(scaled, axis=1, keepdims=True)
    mean_b = jnp.mean(scaled * normed, axis=1, keepdims=True)
    gproj = (inverse * (scaled - mean_a - normed * mean_b)).astype(BF16)
    gproj_ref[...] = gproj
    gpre = (lax.dot_general(gproj, out_w_ref[...], COLS, preferred_element_type=F32) * slope).astype(BF16)
    gpre_ref[...] = gpre
    psum_ref[...] = jnp.sum(gpre.astype(F32).reshape(nodes, degree, gpre.shape[1]), axis=1).astype(BF16)
    back = lax.dot_general(gpre, weight_ref[:latent], COLS, preferred_element_type=F32)
    gedge_ref[...] = (cot + back).astype(BF16)


def edge_call(base, ids, low, high, edges, cots, ncot, weight_in, weight_out, gain, mine, got, first, block):
    count, latent = edges.shape
    hidden = weight_in.shape[1]
    degree = count // ncot.shape[0]
    blocks = count // block
    small = block // degree

    def like(width, dtype, size, total):
        return (
            pl.BlockSpec((size, width), lambda i: (i, 0)),
            jax.ShapeDtypeStruct((total, width), dtype),
        )

    outs = [
        like(latent, BF16, block, count),
        like(latent, F32, small, count // degree),
        like(hidden, BF16, block, count),
        like(latent, BF16, block, count),
        like(hidden, BF16, block, count),
        like(hidden, BF16, small, count // degree),
        like(latent, BF16, block, count),
        (whole(mine), jax.ShapeDtypeStruct(mine.shape, F32)),
    ]
    return pl.pallas_call(
        lambda *refs: edge_kernel(first, degree, *refs),
        grid=(blocks,),
        in_specs=[
            rows(base, block),
            rows(ids, block),
            whole(low),
            whole(high),
            rows(edges, block),
            rows(cots, block),
            rows(ncot, small),
            whole(weight_in),
            whole(weight_out),
            whole(gain),
            whole(mine),
            whole(got),
        ],
        out_specs=[spec for spec, _ in outs],
        out_shape=[shape for _, shape in outs],
        scratch_shapes=[pltpu.VMEM((2 * low.shape[0], hidden), BF16)],
        compiler_params=params(),
        cost_estimate=cost(12),
        name="edge_block",
    )(base, ids, low, high, edges, cots, ncot, weight_in, weight_out, gain, mine, got)


def gather_kernel(first, base_ref, ids_ref, *refs):
    pieces, (weight_ref, out_ref, table) = refs[:-3], refs[-3:]

    @pl.when(pl.program_id(0) == 0)
    def _():
        fill_table(table, pieces, weight_ref)

    hot = one_hot(ids_ref[...], first, table.shape[0])
    out_ref[...] = base_ref[...] + dot(hot, table[...])


def gather_call(base, ids, pieces, weight_in, first, block):
    count, hidden = base.shape
    size = sum(piece.shape[0] for piece in pieces)
    return pl.pallas_call(
        lambda *refs: gather_kernel(first, *refs),
        grid=(count // block,),
        in_specs=[rows(base, block), rows(ids, block)] + [whole(piece) for piece in pieces] + [whole(weight_in)],
        out_specs=rows(base, block),
        out_shape=jax.ShapeDtypeStruct(base.shape, F32),
        scratch_shapes=[pltpu.VMEM((size, hidden), BF16)],
        compiler_params=params(),
        cost_estimate=cost(2),
        name="gather_terms",
    )(base, ids, *pieces, weight_in)


def select_kernel(ids_ref, mine_ref, got_ref, after_ref, *refs):
    pieces, (low_ref, high_ref, sum_ref) = refs[:-3], refs[-3:]
    total, at = None, 0
    for piece in pieces:
        term = dot(one_hot(ids_ref[...], at, piece.shape[0]), piece[...])
        total = term if total is None else total + term
        at += piece.shape[0]
    half = low_ref.shape[0]
    low_ref[...] = total[:half].astype(BF16)
    high_ref[...] = total[half:].astype(BF16)
    sum_ref[...] = mine_ref[...] + got_ref[...]


def select_call(ids, mine, got, after, pieces):
    count, width = ids.shape[0], pieces[0].shape[1]
    half = jax.ShapeDtypeStruct((count // 2, width), BF16)
    vmem = pl.BlockSpec(memory_space=pltpu.VMEM)
    return pl.pallas_call(
        select_kernel,
        in_specs=[vmem] * 3 + [pl.BlockSpec(memory_space=pl.ANY)] + [vmem] * len(pieces),
        out_shape=[half, half, jax.ShapeDtypeStruct(mine.shape, F32)],
        compiler_params=params(),
        cost_estimate=cost(0.7),
        name="select_rows",
    )(ids, mine, got, after, *pieces)


def rim_sum_kernel(first, ids_ref, values_ref, low_ref, high_ref):
    half = low_ref.shape[0]
    places = lax.broadcasted_iota(jnp.int32, (2 * half, ids_ref.shape[1]), 0) + first
    hot = jnp.where(places == ids_ref[...], 1.0, 0.0).astype(BF16)
    total = dot(hot, values_ref[...])
    low_ref[...] = total[:half].astype(BF16)
    high_ref[...] = total[half:].astype(BF16)


def rim_sum_call(ids, values, first, count):
    half = jax.ShapeDtypeStruct((count // 2, values.shape[1]), BF16)
    return pl.pallas_call(
        lambda *refs: rim_sum_kernel(first, *refs),
        out_shape=[half, half],
        compiler_params=params(),
        cost_estimate=cost(0.7),
        name="rim_sums",
    )(ids, values)


def patch_sum_kernel(ids_ref, values_ref, out_ref):
    size = out_ref.shape[0]
    places = lax.broadcasted_iota(jnp.int32, (size, ids_ref.shape[1]), 0) + pl.program_id(0) * size
    hot = jnp.where(places == ids_ref[...], 1.0, 0.0).astype(BF16)
    out_ref[...] = dot(hot, values_ref[...])


def patch_sum_call(ids, values, count, block):
    width = values.shape[1]
    return pl.pallas_call(
        patch_sum_kernel,
        grid=(count // block,),
        in_specs=[whole(ids), whole(values)],
        out_specs=pl.BlockSpec((block, width), lambda i: (i, 0)),
        out_shape=jax.ShapeDtypeStruct((count, width), F32),
        compiler_params=params(),
        cost_estimate=cost(2.8),
        name="patch_sums",
    )(ids, values)


def add_rim_kernel(ids_ref, low_ref, high_ref, start_ref, mine_ref, got_ref, sum_ref, *outs):
    sum_ref[...] = mine_ref[...] + got_ref[...]
    half = low_ref.shape[0]
    size = outs[0].shape[0]
    for j, out in enumerate(outs):
        places = lax.broadcasted_iota(jnp.int32, (size, 2 * half), 0) + j * size
        hot = jnp.where(places == ids_ref[...], 1.0, 0.0).astype(BF16)
        total = start_ref[j * size : (j + 1) * size] + dot(hot[:, :half], low_ref[...])
        total = total + dot(hot[:, half:], high_ref[...])
        out[...] = total.astype(BF16)


def add_rim_call(ids, low, high, start, mine, got, size):
    count, width = start.shape
    piece = jax.ShapeDtypeStruct((size, width), BF16)
    return pl.pallas_call(
        add_rim_kernel,
        out_shape=[jax.ShapeDtypeStruct(mine.shape, F32)] + [piece] * (count // size),
        compiler_params=params(),
        cost_estimate=cost(0.7),
        name="add_rim_sums",
    )(ids, low, high, start, mine, got)


def edge_grads_kernel(edge_ref, gpre_ref, hid_ref, gproj_ref, in_ref, out_ref):
    in_ref[...] = lax.dot_general(edge_ref[...], gpre_ref[...], ROWS, preferred_element_type=F32)
    out_ref[...] = lax.dot_general(hid_ref[...], gproj_ref[...], ROWS, preferred_element_type=F32)


def edge_grads_call(edges, gpre, hid, gproj):
    latent, hidden = edges.shape[1], gpre.shape[1]
    return pl.pallas_call(
        edge_grads_kernel,
        out_shape=[
            jax.ShapeDtypeStruct((latent, hidden), F32),
            jax.ShapeDtypeStruct((hidden, latent), F32),
        ],
        compiler_params=params(),
        cost_estimate=cost(2.4),
        name="edge_grads",
    )(edges, gpre, hid, gproj)


def pack_kernel(pieces, bit_ref, psum_ref, edge_ref, out_ref, *refs):
    tables, sums = refs[:pieces], refs[pieces : 2 * pieces]
    keep_ref, send_ref, total = refs[2 * pieces :]
    latent = tables[0].shape[1]
    grad = None
    for table, part in zip(tables, sums):
        term = lax.dot_general(table[...], part[...], ROWS, preferred_element_type=F32)
        grad = term if grad is None else grad + term
    total[:latent] = edge_ref[...]
    total[latent : 2 * latent] = grad
    total[2 * latent : 3 * latent] = lax.dot_general(
        tables[0][...], psum_ref[...], ROWS, preferred_element_type=F32
    )
    total[3 * latent :] = out_ref[...]
    feats, pairs, span, width = keep_ref.shape
    unit = span // 4
    bit = bit_ref[0]
    for m in range(pairs):
        for slot in range(4):
            for ref, which in ((keep_ref, bit), (send_ref, 1 - bit)):
                patch = 2 * m + which
                row = (patch * 3 + slot) * unit if slot < 3 else 3 * latent + patch * unit
                block = total[pl.ds(pl.multiple_of(row, unit), unit), :]
                for f in range(feats):
                    ref[f, m, slot * unit : (slot + 1) * unit, :] = block[:, f * width : (f + 1) * width].astype(
                        ref.dtype
                    )


def pack_call(bit, psum, edge_grad, out_grad, tables, sums, feats, patches):
    latent, hidden = edge_grad.shape
    shape = (feats, patches // 2, 4 * latent // patches, hidden // feats)
    vmem = pl.BlockSpec(memory_space=pltpu.VMEM)
    return pl.pallas_call(
        lambda *refs: pack_kernel(len(tables), *refs),
        in_specs=[pl.BlockSpec(memory_space=pltpu.SMEM)] + [vmem] * (3 + 2 * len(tables)),
        out_shape=[jax.ShapeDtypeStruct(shape, F32), jax.ShapeDtypeStruct(shape, BF16)],
        scratch_shapes=[pltpu.VMEM((4 * latent, hidden), F32)],
        compiler_params=params(),
        cost_estimate=cost(3.2),
        name="pack_grads",
    )(bit, psum, edge_grad, out_grad, *tables, *sums)


def coarse_sum_kernel(ids_ref, lat_ref, cot_ref, bit_ref, mine_ref, other_ref):
    latent = lat_ref.shape[1]
    half = mine_ref.shape[0]
    for ref, bit in ((mine_ref, bit_ref[0]), (other_ref, 1 - bit_ref[0])):
        places = lax.broadcasted_iota(jnp.int32, (half, ids_ref.shape[1]), 0) + bit * half
        live = jnp.where(places == ids_ref[...], 1.0, 0.0)
        hot = live.astype(BF16)
        ref[:, :latent] = dot(hot, lat_ref[...])
        ref[:, latent : 2 * latent] = dot(hot, cot_ref[...])
        ref[:, 2 * latent :] = jnp.broadcast_to(jnp.sum(live, axis=1, keepdims=True), (half, 128))


def coarse_sum_call(ids, lat, cot, bit, coarse):
    vmem = pl.BlockSpec(memory_space=pltpu.VMEM)
    half = jax.ShapeDtypeStruct((coarse // 2, 2 * lat.shape[1] + 128), F32)
    return pl.pallas_call(
        coarse_sum_kernel,
        in_specs=[vmem, vmem, vmem, pl.BlockSpec(memory_space=pltpu.SMEM)],
        out_shape=[half, half],
        compiler_params=params(),
        cost_estimate=cost(0.3),
        name="coarse_sums",
    )(ids, lat, cot, bit)


def add_split_kernel(bit_ref, keep_ref, got_ref, mine_ref, other_ref):
    bit = bit_ref[0]
    for ref, which in ((mine_ref, bit), (other_ref, 1 - bit)):
        for a in range(keep_ref.shape[0]):
            ref[a] = (keep_ref[a, which] + got_ref[a, which].astype(F32)).astype(ref.dtype)


def add_split_call(bit, keep, got, send_type):
    vmem = pl.BlockSpec(memory_space=pltpu.VMEM)
    shape = keep.shape[:1] + keep.shape[2:]
    return pl.pallas_call(
        add_split_kernel,
        in_specs=[pl.BlockSpec(memory_space=pltpu.SMEM), vmem, vmem],
        out_shape=[jax.ShapeDtypeStruct(shape, F32), jax.ShapeDtypeStruct(shape, send_type)],
        compiler_params=params(),
        cost_estimate=cost(1),
        name="add_split",
    )(bit, keep, got)


def last_grads_kernel(scale, keep_ref, got_ref, in_ref, out_ref):
    rows_in = in_ref.shape[0]
    in_ref[...] = (keep_ref[:rows_in] + got_ref[:rows_in].astype(F32)) * scale
    out_ref[...] = (keep_ref[rows_in:] + got_ref[rows_in:].astype(F32)) * scale


def last_grads_call(scale, keep, got, rows_in):
    span, width = keep.shape
    return pl.pallas_call(
        lambda *refs: last_grads_kernel(scale, *refs),
        out_shape=[
            jax.ShapeDtypeStruct((rows_in, width), F32),
            jax.ShapeDtypeStruct((span - rows_in, width), F32),
        ],
        compiler_params=params(),
        cost_estimate=cost(0.5),
        name="last_grads",
    )(keep, got)


def node_kernel(
    place_ref, ids_ref, lat_ref, cot_ref, agg_ref, psum_ref, weight_ref, *refs
):
    pieces, (new_ref, part_ref, total) = refs[:-3], refs[-3:]
    latent = lat_ref.shape[1]
    for j, piece in enumerate(pieces):
        size = piece.shape[0]
        total[pl.ds(pl.multiple_of(place_ref[j] * size, size), size), :] = piece[...]
    sums = total[...]
    means = sums[:, : 2 * latent] / jnp.maximum(sums[:, 2 * latent : 2 * latent + 1], 1.0)
    places = lax.broadcasted_iota(jnp.int32, (sums.shape[0], ids_ref.shape[1]), 0)
    hot = jnp.where(places == ids_ref[...], 1.0, 0.0).astype(BF16)
    high = means.astype(BF16)
    low = (means - high.astype(F32)).astype(BF16)
    pooled = lax.dot_general(hot, high, ROWS, preferred_element_type=F32)
    pooled = pooled + lax.dot_general(hot, low, ROWS, preferred_element_type=F32)
    new_ref[...] = (lat_ref[...].astype(F32) + agg_ref[...] + pooled[:, :latent]).astype(BF16)
    own = lax.dot_general(psum_ref[...], weight_ref[2 * latent :], COLS, preferred_element_type=F32)
    part_ref[...] = cot_ref[...].astype(F32) + own + pooled[:, latent:]


def node_call(place, ids, lat, cot, agg, psum, weight_in, pieces):
    vmem = pl.BlockSpec(memory_space=pltpu.VMEM)
    coarse = sum(piece.shape[0] for piece in pieces)
    return pl.pallas_call(
        node_kernel,
        in_specs=[pl.BlockSpec(memory_space=pltpu.SMEM)] + [vmem] * (6 + len(pieces)),
        scratch_shapes=[pltpu.VMEM((coarse, pieces[0].shape[1]), F32)],
        out_shape=[jax.ShapeDtypeStruct(lat.shape, BF16), jax.ShapeDtypeStruct(lat.shape, F32)],
        compiler_params=params(),
        cost_estimate=cost(1.1),
        name="node_outputs",
    )(place, ids, lat, cot, agg, psum, weight_in, *pieces)


def grad_node_kernel(part_ref, own_ref, far_ref, near_ref, weight_ref, out_ref):
    latent = part_ref.shape[1]
    total = own_ref[...].astype(F32) + far_ref[...].astype(F32) + near_ref[...].astype(F32)
    back = lax.dot_general(
        total.astype(BF16), weight_ref[latent : 2 * latent], COLS, preferred_element_type=F32
    )
    out_ref[...] = (part_ref[...] + back).astype(BF16)


def grad_node_call(part, own, far, near, weight_in):
    return pl.pallas_call(
        grad_node_kernel,
        out_shape=jax.ShapeDtypeStruct(part.shape, BF16),
        compiler_params=params(),
        cost_estimate=cost(8),
        name="grad_node",
    )(part, own, far, near, weight_in)


def xor_swap(value, axis, distance):
    size = lax.axis_size(axis)
    return lax.ppermute(value, axis, [(i, i ^ distance) for i in range(size)])


def bits_of(size):
    return [1 << b for b in range(size.bit_length() - 1)]


def split(value, dim, bit):
    mine = lax.dynamic_index_in_dim(value, bit, dim, keepdims=False)
    other = lax.dynamic_index_in_dim(value, 1 - bit, dim, keepdims=False)
    return mine, other


def coarse_reduce(sums, other, patch):
    width = sums.shape[1]
    bits = bits_of(lax.axis_size("patch"))
    sums = sums + xor_swap(other, "patch", 1)
    for distance in bits[1:]:
        mine, other = split(sums.reshape(2, -1, width), 0, (patch // distance) % 2)
        sums = mine + xor_swap(other, "patch", distance)
    for distance in bits_of(lax.axis_size("feat")):
        sums = sums + xor_swap(sums, "feat", distance)
    for distance in reversed(bits):
        got = xor_swap(sums, "patch", distance)
        first = (patch // distance) % 2 == 0
        sums = jnp.concatenate([jnp.where(first, sums, got), jnp.where(first, got, sums)], axis=0)
    return sums


def shards(
    node_lat,
    edge_lat,
    neighbours,
    send_rows,
    coarse_of,
    weight_in,
    bias_in,
    weight_out,
    norm_gain,
    edge_cotangent,
    node_cotangent,
):
    node_count, latent = node_lat.shape
    degree = edge_lat.shape[1]
    edge_count = node_count * degree
    rim_rows = send_rows.shape[0] // 2
    feat_count = lax.axis_size("feat")
    patch_count = lax.axis_size("patch")
    patch_total = feat_count * node_count
    coarse_total = COARSE_DEV * patch_count * feat_count
    feat = lax.axis_index("feat")
    patch = lax.axis_index("patch")
    block = min(512, edge_count)
    ring_up = [(i, (i + 1) % patch_count) for i in range(patch_count)]
    ring_down = [(j, i) for i, j in ring_up]

    def relative(ids):
        moved = ((ids // node_count) ^ feat) * node_count + ids % node_count
        return jnp.where(ids < patch_total, moved, ids)

    flat_edges = edge_lat.reshape(edge_count, latent)
    flat_cots = edge_cotangent.reshape(edge_count, latent)
    ids = relative(neighbours).T.reshape(edge_count)
    ids_col = ids[:, None]
    ids_row = ids[None, :]
    send_rel = relative(send_rows)
    bias = bias_in[None, :]
    gain = norm_gain[None, :]
    coarse_row = coarse_of[None, :]

    core_bit = (patch % 2).astype(jnp.int32).reshape(1)
    whole_step = feat_count == 4 and patch_count == 4

    if feat_count == 4:
        far = xor_swap(node_lat, "feat", 2)
        near = xor_swap(node_lat, "feat", 1)
        last = xor_swap(far, "feat", 1)
        pieces = [node_lat, near, far, last]
    else:
        pieces = [node_lat]
        for distance in bits_of(feat_count):
            pieces = pieces + [xor_swap(piece, "feat", distance) for piece in pieces]

    coarse, coarse_other = coarse_sum_call(coarse_row, node_lat, node_cotangent, core_bit, coarse_total)
    if whole_step:
        got = xor_swap(coarse_other, "patch", 1)
        high_bit = (patch // 2).astype(jnp.int32).reshape(1)
        halves = (1, 2, coarse.shape[0] // 2, coarse.shape[1])
        coarse, coarse_other = add_split_call(high_bit, coarse.reshape(halves), got.reshape(halves), F32)
        coarse, coarse_other = coarse[0], coarse_other[0]
        got = xor_swap(coarse_other, "patch", 2)
    else:
        coarse = coarse_reduce(coarse, coarse_other, patch)
        got = jnp.zeros_like(coarse)
    base = base_call(flat_edges, node_lat, ids_col, weight_in, bias, coarse, pieces[:-1], block)
    to_lower, to_upper, coarse = select_call(send_rel[:, None], coarse, got, base, pieces)
    from_lower = lax.ppermute(to_upper, "patch", ring_up)
    from_upper = lax.ppermute(to_lower, "patch", ring_down)
    got = xor_swap(coarse, "feat", 1) if whole_step else jnp.zeros_like(coarse)
    base = gather_call(base, ids_col, pieces[-1:], weight_in, patch_total - node_count, block)

    edge_new, aggregate, hidden_act, grad_proj, grad_pre, pre_sum, grad_edge, coarse = edge_call(
        base,
        ids_col,
        from_lower,
        from_upper,
        flat_edges,
        flat_cots,
        node_cotangent,
        weight_in,
        weight_out,
        gain,
        coarse,
        got,
        patch_total,
        block,
    )

    rim_low, rim_high = rim_sum_call(ids_row, grad_pre, patch_total, 2 * rim_rows)
    back_upper = lax.ppermute(rim_low, "patch", ring_down)
    back_lower = lax.ppermute(rim_high, "patch", ring_up)
    got = xor_swap(coarse, "feat", 2) if whole_step else jnp.zeros_like(coarse)
    patch_sum = patch_sum_call(ids_row, grad_pre, patch_total, node_count)
    edge_grad, out_grad = edge_grads_call(flat_edges, grad_pre, hidden_act, grad_proj)
    coarse, *sums = add_rim_call(send_rel[None, :], back_lower, back_upper, patch_sum, coarse, got, node_count)
    if feat_count == 4:
        relay = xor_swap(sums[3], "feat", 1)
        far_sum = (sums[2].astype(F32) + relay.astype(F32)).astype(BF16)
        got_far = xor_swap(far_sum, "feat", 2)
        got_near = xor_swap(sums[1], "feat", 1)
        own = [sums[0], got_far, got_near]
    else:
        parts = sums
        for distance in reversed(bits_of(feat_count)):
            got = [xor_swap(part, "feat", distance) for part in parts[distance:]]
            parts = [(a.astype(F32) + b.astype(F32)).astype(BF16) for a, b in zip(parts[:distance], got)]
        own = [parts[0], jnp.zeros_like(parts[0]), jnp.zeros_like(parts[0])]

    keep, send = pack_call(core_bit, pre_sum, edge_grad, out_grad, pieces, sums, feat_count, patch_count)
    span, width = keep.shape[2:]
    steps = [("patch", d) for d in bits_of(patch_count)[1:]] + [("feat", d) for d in bits_of(feat_count)]
    got = xor_swap(send, "patch", 1)
    for axis, distance in steps:
        index = patch if axis == "patch" else feat
        bit = ((index // distance) % 2).astype(jnp.int32).reshape(1)
        shape = (-1, 2, span, width)
        keep, send = add_split_call(bit, keep.reshape(shape), got.reshape(shape), BF16)
        got = xor_swap(send, axis, distance)
    scale = 1.0 / math.sqrt(edge_count * patch_count * feat_count)
    in_rows = 3 * latent // patch_count
    grads_in, grads_out = last_grads_call(scale, keep.reshape(span, width), got.reshape(span, width), in_rows)

    if whole_step:
        parts = [coarse] + [xor_swap(coarse, "patch", j) for j in range(1, 4)]
        place = jnp.stack([((patch ^ j) % 2) * 2 + (patch ^ j) // 2 for j in range(4)]).astype(jnp.int32)
    else:
        parts, place = [coarse], jnp.zeros((1,), jnp.int32)
    node_new, part = node_call(
        place, coarse_row, node_lat, node_cotangent, aggregate, pre_sum, weight_in, parts
    )
    grad_node = grad_node_call(part, *own, weight_in)
    return (
        edge_new.reshape(edge_lat.shape),
        node_new,
        grad_edge.reshape(edge_lat.shape),
        grad_node,
        grads_in,
        grads_out,
    )


def solution(mesh):
    return jax.shard_map(
        shards,
        mesh=mesh,
        in_specs=(
            P(("groups", "patch", "feat"), None),
            P(("groups", "patch", "feat"), None, None),
            P(None, ("patch", "feat")),
            P("patch"),
            P(("patch", "feat")),
            P(),
            P(),
            P(),
            P(),
            P(("groups", "patch", "feat"), None, None),
            P(("groups", "patch", "feat"), None),
        ),
        out_specs=(
            P(("groups", "patch", "feat"), None, None),
            P(("groups", "patch", "feat"), None),
            P(("groups", "patch", "feat"), None, None),
            P(("groups", "patch", "feat"), None),
            P(("groups", "patch"), "feat"),
            P(("groups", "patch"), "feat"),
        ),
        check_vma=False,
    )
```

```python
import math

import jax
import jax.numpy as jnp
from jax import lax
from jax.experimental import pallas as pl
from jax.experimental.pallas import tpu as pltpu
from jax.sharding import PartitionSpec as P

COARSE_DEV = 4
LAYER_EPS = 1e-05
F32 = jnp.float32
BF16 = jnp.bfloat16
VMEM_LIMIT = 24 * 1024 * 1024
COLS = (((1,), (1,)), ((), ()))
ROWS = (((0,), (0,)), ((), ()))


def dot(a, b):
    return jnp.dot(a, b, preferred_element_type=F32)


def params():
    return pltpu.CompilerParams(vmem_limit_bytes=VMEM_LIMIT)


def cost(micros):
    return pl.CostEstimate(flops=int(micros * 1.15e9), bytes_accessed=1 << 20, transcendentals=0)


class Order:
    token = None


def launch(kernel, out_shape, in_specs=None, out_specs=None, grid=None, **settings):
    outs = list(out_shape) if isinstance(out_shape, (list, tuple)) else [out_shape]
    mark = jax.ShapeDtypeStruct((8, 128), F32)

    def call(*args):
        count = len(args)
        late = [] if Order.token is None else [Order.token]
        vmem = pl.BlockSpec(memory_space=pltpu.VMEM)
        specs = list(in_specs or [vmem] * count) + [pl.BlockSpec(memory_space=pl.ANY)] * len(late)
        end = count + len(late) + len(outs)

        def body(*refs):
            refs[end][...] = jnp.zeros((8, 128), F32)
            kernel(*refs[:count], *refs[count + len(late) : end], *refs[end + 1 :])

        if grid is None:
            places, more = [vmem] * (len(outs) + 1), {}
        else:
            places = list(out_specs) if isinstance(out_specs, (list, tuple)) else [out_specs]
            places, more = places + [pl.BlockSpec((8, 128), lambda i: (0, 0))], {"grid": grid}
        results = pl.pallas_call(
            body, out_shape=outs + [mark], in_specs=specs, out_specs=places, **more, **settings
        )(*args, *late)
        Order.token = results[-1]
        return results[:-1] if isinstance(out_shape, (list, tuple)) else results[0]

    return call


def streamed(array):
    return pltpu.with_memory_space_constraint(array, pltpu.HBM)


def held(array):
    return pltpu.with_memory_space_constraint(array, pltpu.VMEM)


def whole(array):
    zeros = (0,) * array.ndim
    return pl.BlockSpec(array.shape, lambda i: zeros)


def rows(array, block):
    rest = (0,) * (array.ndim - 1)
    return pl.BlockSpec((block,) + array.shape[1:], lambda i: (i,) + rest)


def one_hot(ids, first, count):
    lanes = lax.broadcasted_iota(jnp.int32, (ids.shape[0], count), 1) + first
    return jnp.where(ids == lanes, 1.0, 0.0).astype(BF16)


def fill_table(table, pieces, weight_ref):
    latent = pieces[0].shape[1]
    at = 0
    for piece in pieces:
        size = piece.shape[0]
        table[at : at + size] = dot(piece[...], weight_ref[latent : 2 * latent]).astype(BF16)
        at += size


def base_kernel(degree, edge_ref, node_ref, ids_ref, weight_ref, bias_ref, *refs):
    pieces, (out_ref, table) = refs[:-2], refs[-2:]
    latent = edge_ref.shape[1]

    @pl.when(pl.program_id(0) == 0)
    def _():
        fill_table(table, pieces, weight_ref)

    edges = edge_ref.shape[0]
    term = dot(node_ref[...], weight_ref[2 * latent :]) + bias_ref[...]
    total = dot(edge_ref[...], weight_ref[:latent])
    total = total + dot(one_hot(ids_ref[...], 0, table.shape[0]), table[...])
    hidden = total.shape[1]
    total = total.reshape(edges // degree, degree, hidden) + term[:, None, :]
    out_ref[...] = total.reshape(edges, hidden)


def base_call(edges, nodes, ids, weight_in, bias, pieces, block):
    count, latent = edges.shape
    hidden = weight_in.shape[1]
    degree = count // nodes.shape[0]
    size = sum(piece.shape[0] for piece in pieces)
    return launch(
        lambda *refs: base_kernel(degree, *refs),
        grid=(count // block,),
        in_specs=[
            rows(edges, block),
            rows(nodes, block // degree),
            rows(ids, block),
            whole(weight_in),
            whole(bias),
        ]
        + [whole(piece) for piece in pieces],
        out_specs=pl.BlockSpec((block, hidden), lambda i: (i, 0)),
        out_shape=jax.ShapeDtypeStruct((count, hidden), F32),
        scratch_shapes=[pltpu.VMEM((size, hidden), BF16)],
        compiler_params=params(),
        cost_estimate=cost(15),
        name="base_terms",
    )(streamed(edges), nodes, ids, weight_in, bias, *pieces)


def edge_kernel(
    first,
    degree,
    base_ref,
    ids_ref,
    last_ref,
    low_ref,
    high_ref,
    edge_ref,
    cot_ref,
    ncot_ref,
    weight_ref,
    out_w_ref,
    gain_ref,
    new_ref,
    agg_ref,
    hid_ref,
    gproj_ref,
    gpre_ref,
    psum_ref,
    gedge_ref,
    table,
):
    latent = low_ref.shape[1]

    @pl.when(pl.program_id(0) == 0)
    def _():
        fill_table(table, (last_ref, low_ref, high_ref), weight_ref)

    ids = ids_ref[...]
    edges = ids.shape[0]
    nodes = edges // degree
    limit = first + table.shape[0]
    live = jnp.where(ids < limit, 1.0, 0.0)
    value = base_ref[...] + dot(one_hot(ids, first, table.shape[0]), table[...])
    sig = jax.nn.sigmoid(value)
    act = value * sig
    slope = sig + act * (1.0 - sig)
    hid = act.astype(BF16)
    hid_ref[...] = hid
    projected = dot(hid, out_w_ref[...])
    centre = projected - jnp.mean(projected, axis=1, keepdims=True)
    inverse = lax.rsqrt(jnp.mean(centre * centre, axis=1, keepdims=True) + LAYER_EPS)
    normed = centre * inverse
    gain = gain_ref[...]
    message = normed * gain
    new_ref[...] = (edge_ref[...].astype(F32) + message).astype(BF16)
    agg_ref[...] = jnp.sum((message * live).reshape(nodes, degree, latent), axis=1)
    ncot = jnp.broadcast_to(ncot_ref[...].astype(F32)[:, None, :], (nodes, degree, latent))
    cot = cot_ref[...].astype(F32)
    scaled = (cot + live * ncot.reshape(edges, latent)) * gain
    mean_a = jnp.mean(scaled, axis=1, keepdims=True)
    mean_b = jnp.mean(scaled * normed, axis=1, keepdims=True)
    gproj = (inverse * (scaled - mean_a - normed * mean_b)).astype(BF16)
    gproj_ref[...] = gproj
    gpre = (lax.dot_general(gproj, out_w_ref[...], COLS, preferred_element_type=F32) * slope).astype(BF16)
    gpre_ref[...] = gpre
    psum_ref[...] = jnp.sum(gpre.astype(F32).reshape(nodes, degree, gpre.shape[1]), axis=1).astype(BF16)
    back = lax.dot_general(gpre, weight_ref[:latent], COLS, preferred_element_type=F32)
    gedge_ref[...] = (cot + back).astype(BF16)


def edge_call(base, ids, last, low, high, edges, cots, ncot, weight_in, weight_out, gain, first, block):
    count, latent = edges.shape
    hidden = weight_in.shape[1]
    degree = count // ncot.shape[0]
    blocks = count // block
    small = block // degree

    def like(width, dtype, size, total):
        return (
            pl.BlockSpec((size, width), lambda i: (i, 0)),
            jax.ShapeDtypeStruct((total, width), dtype),
        )

    outs = [
        like(latent, BF16, block, count),
        like(latent, F32, small, count // degree),
        like(hidden, BF16, block, count),
        like(latent, BF16, block, count),
        like(hidden, BF16, block, count),
        like(hidden, BF16, small, count // degree),
        like(latent, BF16, block, count),
    ]
    return launch(
        lambda *refs: edge_kernel(first, degree, *refs),
        grid=(blocks,),
        in_specs=[
            rows(base, block),
            rows(ids, block),
            whole(last),
            whole(low),
            whole(high),
            rows(edges, block),
            rows(cots, block),
            rows(ncot, small),
            whole(weight_in),
            whole(weight_out),
            whole(gain),
        ],
        out_specs=[spec for spec, _ in outs],
        out_shape=[shape for _, shape in outs],
        scratch_shapes=[pltpu.VMEM((last.shape[0] + 2 * low.shape[0], hidden), BF16)],
        compiler_params=params(),
        cost_estimate=cost(36),
        name="edge_block",
    )(streamed(base), ids, last, low, high, streamed(edges), streamed(cots), ncot, weight_in, weight_out, gain)


def select_kernel(ids_ref, *refs):
    pieces, (low_ref, high_ref) = refs[:-2], refs[-2:]
    total, at = None, 0
    for piece in pieces:
        term = dot(one_hot(ids_ref[...], at, piece.shape[0]), piece[...])
        total = term if total is None else total + term
        at += piece.shape[0]
    half = low_ref.shape[0]
    low_ref[...] = total[:half].astype(BF16)
    high_ref[...] = total[half:].astype(BF16)


def select_call(ids, pieces):
    count, width = ids.shape[0], pieces[0].shape[1]
    half = jax.ShapeDtypeStruct((count // 2, width), BF16)
    return launch(
        select_kernel,
        out_shape=[half, half],
        compiler_params=params(),
        cost_estimate=cost(2),
        name="select_rows",
    )(ids, *pieces)


def rim_sum_kernel(first, ids_ref, values_ref, low_ref, high_ref):
    half = low_ref.shape[0]
    places = lax.broadcasted_iota(jnp.int32, (2 * half, ids_ref.shape[1]), 0) + first
    hot = jnp.where(places == ids_ref[...], 1.0, 0.0).astype(BF16)
    total = dot(hot, values_ref[...])
    low_ref[...] = total[:half].astype(BF16)
    high_ref[...] = total[half:].astype(BF16)


def rim_sum_call(ids, values, first, count):
    half = jax.ShapeDtypeStruct((count // 2, values.shape[1]), BF16)
    return launch(
        lambda *refs: rim_sum_kernel(first, *refs),
        out_shape=[half, half],
        compiler_params=params(),
        cost_estimate=cost(2.4),
        name="rim_sums",
    )(ids, values)


def patch_sum_kernel(ids_ref, values_ref, out_ref):
    size = out_ref.shape[0]
    places = lax.broadcasted_iota(jnp.int32, (size, ids_ref.shape[1]), 0) + pl.program_id(0) * size
    hot = jnp.where(places == ids_ref[...], 1.0, 0.0).astype(BF16)
    out_ref[...] = dot(hot, values_ref[...])


def patch_sum_call(ids, values, count, block):
    width = values.shape[1]
    return launch(
        patch_sum_kernel,
        grid=(count // block,),
        in_specs=[whole(ids), whole(values)],
        out_specs=pl.BlockSpec((block, width), lambda i: (i, 0)),
        out_shape=jax.ShapeDtypeStruct((count, width), F32),
        compiler_params=params(),
        cost_estimate=cost(0.5),
        name="patch_sums",
    )(ids, values)


def add_rim_kernel(ids_ref, low_ref, high_ref, start_ref, mine_ref, got_ref, *outs):
    half = low_ref.shape[0]
    size = outs[0].shape[0]
    latent = start_ref.shape[1]
    coarse = mine_ref[...] + got_ref[...]
    few = coarse.shape[0]
    counts = coarse[:, 2 * latent :]
    high = jnp.floor(counts * (1.0 / 64.0))
    for j, out in enumerate(outs):
        places = lax.broadcasted_iota(jnp.int32, (size, 2 * half), 0) + j * size
        hot = jnp.where(places == ids_ref[...], 1.0, 0.0).astype(BF16)
        total = start_ref[j * size : (j + 1) * size] + dot(hot[:, :half], low_ref[...])
        total = total + dot(hot[:, half:], high_ref[...])
        out[:size] = total.astype(BF16)
        if out.shape[0] > size:
            out[size : size + few] = coarse[:, :latent].astype(BF16)
            out[size + few : size + 2 * few] = coarse[:, latent : 2 * latent].astype(BF16)
            out[size + 2 * few :] = jnp.zeros((few, latent), BF16)
            out[size + 2 * few :, :128] = high.astype(BF16)
            out[size + 2 * few :, 128:256] = (counts - 64.0 * high).astype(BF16)


def add_rim_call(ids, low, high, start, mine, got, size, extended):
    count, width = start.shape
    pieces = count // size
    extra = [3 * mine.shape[0] if extended and j == pieces - 1 else 0 for j in range(pieces)]
    return launch(
        add_rim_kernel,
        out_shape=[jax.ShapeDtypeStruct((size + more, width), BF16) for more in extra],
        compiler_params=params(),
        cost_estimate=cost(15.0),
        name="add_rim_sums",
    )(ids, low, high, start, mine, got)


def edge_grads_kernel(edge_ref, gpre_ref, hid_ref, gproj_ref, in_ref, out_ref):
    in_ref[...] = lax.dot_general(edge_ref[...], gpre_ref[...], ROWS, preferred_element_type=F32)
    out_ref[...] = lax.dot_general(hid_ref[...], gproj_ref[...], ROWS, preferred_element_type=F32)


def edge_grads_call(edges, gpre, hid, gproj):
    latent, hidden = edges.shape[1], gpre.shape[1]
    return launch(
        edge_grads_kernel,
        out_shape=[
            jax.ShapeDtypeStruct((latent, hidden), F32),
            jax.ShapeDtypeStruct((hidden, latent), F32),
        ],
        compiler_params=params(),
        cost_estimate=cost(0.5),
        name="edge_grads",
    )(edges, gpre, hid, gproj)


def pack_kernel(pieces, bit_ref, psum_ref, edge_ref, out_ref, patch_ref, low_ref, high_ref, *refs):
    tables = refs[:pieces]
    keep_ref, send_ref, total = refs[pieces:]
    latent = tables[0].shape[1]
    size = tables[0].shape[0]
    parts = [patch_ref[j * size : (j + 1) * size].astype(BF16) for j in range(pieces - 2)]
    grad = None
    for table, part in zip(tables, parts + [low_ref[...], high_ref[...]]):
        term = lax.dot_general(table[...], part, ROWS, preferred_element_type=F32)
        grad = term if grad is None else grad + term
    total[:latent] = edge_ref[...]
    total[latent : 2 * latent] = grad
    total[2 * latent : 3 * latent] = lax.dot_general(
        tables[0][...], psum_ref[...], ROWS, preferred_element_type=F32
    )
    total[3 * latent :] = out_ref[...]
    feats, pairs, span, width = keep_ref.shape
    unit = span // 4
    bit = bit_ref[0]
    for m in range(pairs):
        for slot in range(4):
            for ref, which in ((keep_ref, bit), (send_ref, 1 - bit)):
                patch = 2 * m + which
                row = (patch * 3 + slot) * unit if slot < 3 else 3 * latent + patch * unit
                block = total[pl.ds(pl.multiple_of(row, unit), unit), :]
                for f in range(feats):
                    ref[f, m, slot * unit : (slot + 1) * unit, :] = block[:, f * width : (f + 1) * width].astype(
                        ref.dtype
                    )


def pack_call(bit, psum, edge_grad, out_grad, patch_sum, low, high, tables, feats, patches):
    latent, hidden = edge_grad.shape
    shape = (feats, patches // 2, 4 * latent // patches, hidden // feats)
    vmem = pl.BlockSpec(memory_space=pltpu.VMEM)
    return launch(
        lambda *refs: pack_kernel(len(tables), *refs),
        in_specs=[pl.BlockSpec(memory_space=pltpu.SMEM)] + [vmem] * (6 + len(tables)),
        out_shape=[jax.ShapeDtypeStruct(shape, F32), jax.ShapeDtypeStruct(shape, BF16)],
        scratch_shapes=[pltpu.VMEM((4 * latent, hidden), F32)],
        compiler_params=params(),
        cost_estimate=cost(0.5),
        name="pack_grads",
    )(bit, psum, edge_grad, out_grad, patch_sum, low, high, *tables)


def coarse_sum_kernel(ids_ref, lat_ref, cot_ref, bit_ref, mine_ref, other_ref):
    latent = lat_ref.shape[1]
    half = mine_ref.shape[0]
    for ref, bit in ((mine_ref, bit_ref[0]), (other_ref, 1 - bit_ref[0])):
        places = lax.broadcasted_iota(jnp.int32, (half, ids_ref.shape[1]), 0) + bit * half
        live = jnp.where(places == ids_ref[...], 1.0, 0.0)
        hot = live.astype(BF16)
        ref[:, :latent] = dot(hot, lat_ref[...])
        ref[:, latent : 2 * latent] = dot(hot, cot_ref[...])
        ref[:, 2 * latent :] = jnp.broadcast_to(jnp.sum(live, axis=1, keepdims=True), (half, 128))


def coarse_sum_call(ids, lat, cot, bit, coarse):
    vmem = pl.BlockSpec(memory_space=pltpu.VMEM)
    half = jax.ShapeDtypeStruct((coarse // 2, 2 * lat.shape[1] + 128), F32)
    return launch(
        coarse_sum_kernel,
        in_specs=[vmem, vmem, vmem, pl.BlockSpec(memory_space=pltpu.SMEM)],
        out_shape=[half, half],
        compiler_params=params(),
        cost_estimate=cost(1),
        name="coarse_sums",
    )(ids, lat, cot, bit)


def add_pair_kernel(a_ref, b_ref, out_ref):
    out_ref[...] = (a_ref[...].astype(F32) + b_ref[...].astype(F32)).astype(out_ref.dtype)


def add_pair_call(a, b):
    return launch(
        add_pair_kernel,
        out_shape=jax.ShapeDtypeStruct(a.shape, a.dtype),
        compiler_params=params(),
        cost_estimate=cost(1.0),
        name="add_pair",
    )(a, b)


def far_sum_kernel(own_ref, sent_ref, got_ref, far_ref, coarse_ref):
    size = own_ref.shape[0]
    far_ref[...] = (own_ref[...].astype(F32) + got_ref[:size].astype(F32)).astype(BF16)
    coarse_ref[...] = sent_ref[size:].astype(F32) + got_ref[size:].astype(F32)


def far_sum_call(own, sent, got):
    size, width = own.shape
    return launch(
        far_sum_kernel,
        out_shape=[
            jax.ShapeDtypeStruct((size, width), BF16),
            jax.ShapeDtypeStruct((sent.shape[0] - size, width), F32),
        ],
        compiler_params=params(),
        cost_estimate=cost(1.0),
        name="far_sum",
    )(own, sent, got)


def add_split_kernel(bit_ref, keep_ref, got_ref, mine_ref, other_ref):
    bit = bit_ref[0]
    for ref, which in ((mine_ref, bit), (other_ref, 1 - bit)):
        for a in range(keep_ref.shape[0]):
            ref[a] = (keep_ref[a, which] + got_ref[a, which].astype(F32)).astype(ref.dtype)


def add_split_call(bit, keep, got, send_type):
    vmem = pl.BlockSpec(memory_space=pltpu.VMEM)
    shape = keep.shape[:1] + keep.shape[2:]
    return launch(
        add_split_kernel,
        in_specs=[pl.BlockSpec(memory_space=pltpu.SMEM), vmem, vmem],
        out_shape=[jax.ShapeDtypeStruct(shape, F32), jax.ShapeDtypeStruct(shape, send_type)],
        compiler_params=params(),
        cost_estimate=cost(1.0),
        name="add_split",
    )(bit, keep, got)


def last_grads_kernel(scale, keep_ref, got_ref, in_ref, out_ref):
    rows_in = in_ref.shape[0]
    in_ref[...] = (keep_ref[:rows_in] + got_ref[:rows_in].astype(F32)) * scale
    out_ref[...] = (keep_ref[rows_in:] + got_ref[rows_in:].astype(F32)) * scale


def last_grads_call(scale, keep, got, rows_in):
    span, width = keep.shape
    return launch(
        lambda *refs: last_grads_kernel(scale, *refs),
        out_shape=[
            jax.ShapeDtypeStruct((rows_in, width), F32),
            jax.ShapeDtypeStruct((span - rows_in, width), F32),
        ],
        compiler_params=params(),
        cost_estimate=cost(1.5),
        name="last_grads",
    )(keep, got)


def node_kernel(place_ref, ids_ref, lat_ref, cot_ref, agg_ref, back_ref, *refs):
    pieces, (new_ref, grad_ref, total) = refs[:-3], refs[-3:]
    latent = lat_ref.shape[1]
    for j, piece in enumerate(pieces):
        size = piece.shape[0] // 3
        here = pl.ds(pl.multiple_of(place_ref[j] * size, size), size)
        total[here, :latent] = piece[:size]
        total[here, latent : 2 * latent] = piece[size : 2 * size]
        total[here, 2 * latent :] = 64.0 * piece[2 * size :, :128] + piece[2 * size :, 128:256]
    sums = total[...]
    means = sums[:, : 2 * latent] / jnp.maximum(sums[:, 2 * latent : 2 * latent + 1], 1.0)
    places = lax.broadcasted_iota(jnp.int32, (sums.shape[0], ids_ref.shape[1]), 0)
    hot = jnp.where(places == ids_ref[...], 1.0, 0.0).astype(BF16)
    high = means.astype(BF16)
    low = (means - high.astype(F32)).astype(BF16)
    pooled = lax.dot_general(hot, high, ROWS, preferred_element_type=F32)
    pooled = pooled + lax.dot_general(hot, low, ROWS, preferred_element_type=F32)
    new_ref[...] = (lat_ref[...].astype(F32) + agg_ref[...] + pooled[:, :latent]).astype(BF16)
    grad_ref[...] = (cot_ref[...].astype(F32) + back_ref[...] + pooled[:, latent:]).astype(BF16)


def node_call(place, ids, lat, cot, agg, back, pieces):
    vmem = pl.BlockSpec(memory_space=pltpu.VMEM)
    coarse = sum(piece.shape[0] // 3 for piece in pieces)
    width = 2 * lat.shape[1] + 128
    return launch(
        node_kernel,
        in_specs=[pl.BlockSpec(memory_space=pltpu.SMEM)] + [vmem] * (5 + len(pieces)),
        scratch_shapes=[pltpu.VMEM((coarse, width), F32)],
        out_shape=[jax.ShapeDtypeStruct(lat.shape, BF16)] * 2,
        compiler_params=params(),
        cost_estimate=cost(2.0),
        name="node_outputs",
    )(place, ids, lat, cot, streamed(agg), back, *pieces)


def node_back_kernel(own_ref, far_ref, near_ref, psum_ref, weight_ref, out_ref):
    latent = own_ref.shape[1]
    total = own_ref[...].astype(F32) + far_ref[...].astype(F32) + near_ref[...].astype(F32)
    back = lax.dot_general(
        total.astype(BF16), weight_ref[latent : 2 * latent], COLS, preferred_element_type=F32
    )
    own = lax.dot_general(psum_ref[...], weight_ref[2 * latent :], COLS, preferred_element_type=F32)
    out_ref[...] = back + own


def node_back_call(own, far, near, psum, weight_in):
    return launch(
        node_back_kernel,
        out_shape=jax.ShapeDtypeStruct(own.shape, F32),
        compiler_params=params(),
        cost_estimate=cost(15.0),
        name="grad_node",
    )(own, far, near, psum, weight_in)


def xor_swap(value, axis, distance):
    size = lax.axis_size(axis)
    return lax.ppermute(value, axis, [(i, i ^ distance) for i in range(size)])


def bits_of(size):
    return [1 << b for b in range(size.bit_length() - 1)]


def split(value, dim, bit):
    mine = lax.dynamic_index_in_dim(value, bit, dim, keepdims=False)
    other = lax.dynamic_index_in_dim(value, 1 - bit, dim, keepdims=False)
    return mine, other


def coarse_reduce(sums, other, patch):
    width = sums.shape[1]
    bits = bits_of(lax.axis_size("patch"))
    sums = sums + xor_swap(other, "patch", 1)
    for distance in bits[1:]:
        mine, other = split(sums.reshape(2, -1, width), 0, (patch // distance) % 2)
        sums = mine + xor_swap(other, "patch", distance)
    for distance in bits_of(lax.axis_size("feat")):
        sums = sums + xor_swap(sums, "feat", distance)
    for distance in reversed(bits):
        got = xor_swap(sums, "patch", distance)
        first = (patch // distance) % 2 == 0
        sums = jnp.concatenate([jnp.where(first, sums, got), jnp.where(first, got, sums)], axis=0)
    return sums


def shards(
    node_lat,
    edge_lat,
    neighbours,
    send_rows,
    coarse_of,
    weight_in,
    bias_in,
    weight_out,
    norm_gain,
    edge_cotangent,
    node_cotangent,
):
    Order.token = None
    node_count, latent = node_lat.shape
    degree = edge_lat.shape[1]
    edge_count = node_count * degree
    rim_rows = send_rows.shape[0] // 2
    feat_count = lax.axis_size("feat")
    patch_count = lax.axis_size("patch")
    patch_total = feat_count * node_count
    coarse_total = COARSE_DEV * patch_count * feat_count
    feat = lax.axis_index("feat")
    patch = lax.axis_index("patch")
    block = min(512, edge_count)
    ring_up = [(i, (i + 1) % patch_count) for i in range(patch_count)]
    ring_down = [(j, i) for i, j in ring_up]

    def relative(ids):
        moved = ((ids // node_count) ^ feat) * node_count + ids % node_count
        return jnp.where(ids < patch_total, moved, ids)

    flat_edges = edge_lat.reshape(edge_count, latent)
    flat_cots = edge_cotangent.reshape(edge_count, latent)
    ids = relative(neighbours).T.reshape(edge_count)
    ids_col = ids[:, None]
    ids_row = ids[None, :]
    send_rel = relative(send_rows)
    bias = bias_in[None, :]
    gain = norm_gain[None, :]
    coarse_row = coarse_of[None, :]

    core_bit = (patch % 2).astype(jnp.int32).reshape(1)
    whole_step = feat_count == 4 and patch_count == 4

    if feat_count == 4:
        far = xor_swap(node_lat, "feat", 2)
        near = xor_swap(node_lat, "feat", 1)
        last = xor_swap(far, "feat", 1)
        pieces = [node_lat, near, far, last]
    else:
        pieces = [node_lat]
        for distance in bits_of(feat_count):
            pieces = pieces + [xor_swap(piece, "feat", distance) for piece in pieces]

    coarse, coarse_other = coarse_sum_call(coarse_row, node_lat, node_cotangent, core_bit, coarse_total)
    if whole_step:
        got = xor_swap(coarse_other, "patch", 1)
        high_bit = (patch // 2).astype(jnp.int32).reshape(1)
        halves = (1, 2, coarse.shape[0] // 2, coarse.shape[1])
        coarse, coarse_other = add_split_call(high_bit, coarse.reshape(halves), got.reshape(halves), F32)
        coarse, coarse_other = coarse[0], coarse_other[0]
        got = xor_swap(coarse_other, "patch", 2)
    else:
        coarse = coarse_reduce(coarse, coarse_other, patch)
        got = jnp.zeros_like(coarse)
    base = base_call(flat_edges, node_lat, ids_col, weight_in, bias, pieces[:-1], block)
    to_lower, to_upper = select_call(send_rel[:, None], pieces)
    from_lower = lax.ppermute(to_upper, "patch", ring_up)
    from_upper = lax.ppermute(to_lower, "patch", ring_down)
    coarse = add_pair_call(coarse, got)
    got = xor_swap(coarse, "feat", 2) if whole_step else jnp.zeros_like(coarse)

    edge_new, aggregate, hidden_act, grad_proj, grad_pre, pre_sum, grad_edge = edge_call(
        base,
        ids_col,
        pieces[-1],
        from_lower,
        from_upper,
        flat_edges,
        flat_cots,
        node_cotangent,
        weight_in,
        weight_out,
        gain,
        patch_total - node_count,
        block)

    rim_low, rim_high = rim_sum_call(ids_row, grad_pre, patch_total, 2 * rim_rows)
    back_upper = lax.ppermute(rim_low, "patch", ring_down)
    back_lower = lax.ppermute(rim_high, "patch", ring_up)
    patch_sum = patch_sum_call(ids_row, grad_pre, patch_total, node_count)
    edge_grad, out_grad = edge_grads_call(flat_edges, grad_pre, hidden_act, grad_proj)
    tables = pieces + [from_lower, from_upper]
    keep, send = pack_call(
        core_bit, pre_sum, edge_grad, out_grad, patch_sum, rim_low, rim_high, tables, feat_count, patch_count
    )
    got_core = xor_swap(send, "patch", 1)
    sums = add_rim_call(
        send_rel[None, :], back_lower, back_upper, patch_sum, coarse, got, node_count, whole_step
    )
    span, width = keep.shape[2:]
    steps = [("patch", d) for d in bits_of(patch_count)[1:]] + [("feat", d) for d in bits_of(feat_count)]

    def fold(step, keep, received):
        axis, distance = steps[step]
        index = patch if axis == "patch" else feat
        bit = ((index // distance) % 2).astype(jnp.int32).reshape(1)
        shape = (-1, 2, span, width)
        keep, send = add_split_call(bit, keep.reshape(shape), received.reshape(shape), BF16)
        return keep, xor_swap(send, axis, distance)

    keep, received = fold(0, keep, got_core)
    if feat_count == 4:
        relay = xor_swap(sums[3], "feat", 1)
        if whole_step:
            far_sum, coarse_all = far_sum_call(sums[2], sums[3], relay)
        else:
            far_sum = add_pair_call(sums[2], relay)
        got_far = xor_swap(far_sum, "feat", 2)
        got_near = xor_swap(sums[1], "feat", 1)
        own = [sums[0], got_far, got_near]
    else:
        parts = sums
        for distance in reversed(bits_of(feat_count)):
            arrived = [xor_swap(part, "feat", distance) for part in parts[distance:]]
            parts = [add_pair_call(a, b) for a, b in zip(parts[:distance], arrived)]
        own = [parts[0], jnp.zeros_like(parts[0]), jnp.zeros_like(parts[0])]
    keep, received = fold(1, keep, received)
    back = node_back_call(*own, pre_sum, weight_in)
    keep, received = fold(2, keep, received)
    if whole_step:
        parts = [coarse_all] + [xor_swap(coarse_all, "patch", j) for j in range(1, 4)]
        place = jnp.stack([((patch ^ j) % 2) * 2 + (patch ^ j) // 2 for j in range(4)]).astype(jnp.int32)
    else:
        counts = jnp.pad(coarse[:, 2 * latent :], ((0, 0), (128, latent - 256)))
        parts = [jnp.concatenate([coarse[:, :latent], coarse[:, latent : 2 * latent], counts], axis=0)]
        place = jnp.zeros((1,), jnp.int32)
    node_new, grad_node = node_call(
        place, coarse_row, node_lat, node_cotangent, aggregate, back, parts
    )
    for step in range(3, len(steps)):
        keep, received = fold(step, keep, received)
    scale = 1.0 / math.sqrt(edge_count * patch_count * feat_count)
    in_rows = 3 * latent // patch_count
    grads_in, grads_out = last_grads_call(scale, keep.reshape(span, width), received.reshape(span, width), in_rows)
    return (
        edge_new.reshape(edge_lat.shape),
        node_new,
        grad_edge.reshape(edge_lat.shape),
        grad_node,
        grads_in,
        grads_out,
    )


def solution(mesh):
    return jax.shard_map(
        shards,
        mesh=mesh,
        in_specs=(
            P(("groups", "patch", "feat"), None),
            P(("groups", "patch", "feat"), None, None),
            P(None, ("patch", "feat")),
            P("patch"),
            P(("patch", "feat")),
            P(),
            P(),
            P(),
            P(),
            P(("groups", "patch", "feat"), None, None),
            P(("groups", "patch", "feat"), None),
        ),
        out_specs=(
            P(("groups", "patch", "feat"), None, None),
            P(("groups", "patch", "feat"), None),
            P(("groups", "patch", "feat"), None, None),
            P(("groups", "patch", "feat"), None),
            P(("groups", "patch"), "feat"),
            P(("groups", "patch"), "feat"),
        ),
        check_vma=False,
    )
```

```python
import functools
import math

import jax
import jax.numpy as jnp
from jax import lax
from jax.experimental import pallas as pl
from jax.experimental.pallas import tpu as pltpu
from jax.sharding import PartitionSpec as P

COARSE_DEV = 4
LAYER_EPS = 1e-05
F32 = jnp.float32
BF16 = jnp.bfloat16
VMEM_LIMIT = 24 * 1024 * 1024
EDGE_LIMIT = 24 * 1024 * 1024
COLS = (((1,), (1,)), ((), ()))
ROWS = (((0,), (0,)), ((), ()))


def dot(a, b):
    return jnp.dot(a, b, preferred_element_type=F32)


def params(limit=None):
    return pltpu.CompilerParams(vmem_limit_bytes=limit or VMEM_LIMIT)


COST = {
    "base_terms": 15,
    "select_rows": 2,
    "add_pair": 1,
    "edge_block": 36,
    "rim_sums": 2.4,
    "patch_sums": 0.3,
    "edge_grads": 0.3,
    "add_rim_sums": 0.3,
    "pack_grads": 0.3,
    "far_sum": 30,
    "node_outputs": 2,
    "grad_node": 30,
    "last_grads": 1.5,
    "coarse_sums": 1,
    "coarse_split": 1,
    "fold0": 0.3,
    "fold1": 0.3,
    "fold2": 0.3,
}


def cost(name):
    micros = COST[name]
    return pl.CostEstimate(flops=int(micros * 1.15e9), bytes_accessed=1 << 20, transcendentals=0)


class Order:
    token = None


def launch(kernel, out_shape, in_specs=None, out_specs=None, grid=None, **settings):
    outs = list(out_shape) if isinstance(out_shape, (list, tuple)) else [out_shape]
    mark = jax.ShapeDtypeStruct((8, 128), F32)

    def call(*args):
        count = len(args)
        late = [] if Order.token is None else [Order.token]
        vmem = pl.BlockSpec(memory_space=pltpu.VMEM)
        specs = list(in_specs or [vmem] * count) + [pl.BlockSpec(memory_space=pl.ANY)] * len(late)
        end = count + len(late) + len(outs)

        def body(*refs):
            refs[end][...] = jnp.zeros((8, 128), F32)
            kernel(*refs[:count], *refs[count + len(late) : end], *refs[end + 1 :])

        if grid is None:
            places, more = [vmem] * (len(outs) + 1), {}
        else:
            places = list(out_specs) if isinstance(out_specs, (list, tuple)) else [out_specs]
            places, more = places + [pl.BlockSpec((8, 128), lambda i: (0, 0))], {"grid": grid}
        results = pl.pallas_call(
            body, out_shape=outs + [mark], in_specs=specs, out_specs=places, **more, **settings
        )(*args, *late)
        Order.token = results[-1]
        return results[:-1] if isinstance(out_shape, (list, tuple)) else results[0]

    return call


def streamed(array):
    return pltpu.with_memory_space_constraint(array, pltpu.HBM)


def held(array):
    return pltpu.with_memory_space_constraint(array, pltpu.VMEM)


def whole(array):
    zeros = (0,) * array.ndim
    return pl.BlockSpec(array.shape, lambda i: zeros)


def rows(array, block):
    rest = (0,) * (array.ndim - 1)
    return pl.BlockSpec((block,) + array.shape[1:], lambda i: (i,) + rest)


def one_hot(ids, first, count):
    lanes = lax.broadcasted_iota(jnp.int32, (ids.shape[0], count), 1) + first
    return jnp.where(ids == lanes, 1.0, 0.0).astype(BF16)


def fill_table(table, pieces, weight_ref):
    latent = pieces[0].shape[1]
    at = 0
    for piece in pieces:
        size = piece.shape[0]
        table[at : at + size] = dot(piece[...], weight_ref[latent : 2 * latent]).astype(BF16)
        at += size


def base_kernel(degree, edge_ref, node_ref, ids_ref, weight_ref, bias_ref, *refs):
    pieces, (out_ref, table) = refs[:-2], refs[-2:]
    latent = edge_ref.shape[1]

    @pl.when(pl.program_id(0) == 0)
    def _():
        fill_table(table, pieces, weight_ref)

    edges = edge_ref.shape[0]
    term = dot(node_ref[...], weight_ref[2 * latent :]) + bias_ref[...]
    total = dot(edge_ref[...], weight_ref[:latent])
    total = total + dot(one_hot(ids_ref[...], 0, table.shape[0]), table[...])
    hidden = total.shape[1]
    total = total.reshape(edges // degree, degree, hidden) + term[:, None, :]
    out_ref[...] = total.reshape(edges, hidden)


def base_call(edges, nodes, ids, weight_in, bias, early, pieces, block):
    count, latent = edges.shape
    hidden = weight_in.shape[1]
    degree = count // nodes.shape[0]
    size = sum(piece.shape[0] for piece in pieces)
    return launch(
        lambda *refs: base_kernel(degree, *refs[:5], *refs[5 + len(early) :]),
        grid=(count // block,),
        in_specs=[
            rows(edges, block),
            rows(nodes, block // degree),
            rows(ids, block),
            whole(weight_in),
            whole(bias),
        ]
        + [pl.BlockSpec(memory_space=pl.ANY)] * len(early)
        + [whole(piece) for piece in pieces],
        out_specs=pl.BlockSpec((block, hidden), lambda i: (i, 0)),
        out_shape=jax.ShapeDtypeStruct((count, hidden), F32),
        scratch_shapes=[pltpu.VMEM((size, hidden), BF16)],
        compiler_params=params(),
        cost_estimate=cost("base_terms"),
        name="base_terms",
    )(streamed(edges), nodes, ids, weight_in, bias, *early, *pieces)


def edge_kernel(
    first,
    degree,
    base_ref,
    ids_ref,
    last_ref,
    low_ref,
    high_ref,
    edge_ref,
    cot_ref,
    ncot_ref,
    weight_ref,
    out_w_ref,
    gain_ref,
    new_ref,
    agg_ref,
    hid_ref,
    gproj_ref,
    gpre_ref,
    psum_ref,
    gedge_ref,
    table,
):
    latent = low_ref.shape[1]

    @pl.when(pl.program_id(0) == 0)
    def _():
        fill_table(table, (last_ref, low_ref, high_ref), weight_ref)

    ids = ids_ref[...]
    edges = ids.shape[0]
    nodes = edges // degree
    limit = first + table.shape[0]
    live = jnp.where(ids < limit, 1.0, 0.0)
    value = base_ref[...] + dot(one_hot(ids, first, table.shape[0]), table[...])
    sig = 0.5 + 0.5 * jnp.tanh(0.5 * value)
    act = value * sig
    slope = sig + act * (1.0 - sig)
    hid = act.astype(BF16)
    hid_ref[...] = hid
    projected = dot(hid, out_w_ref[...])
    centre = projected - jnp.mean(projected, axis=1, keepdims=True)
    inverse = lax.rsqrt(jnp.mean(centre * centre, axis=1, keepdims=True) + LAYER_EPS)
    normed = centre * inverse
    gain = gain_ref[...]
    message = normed * gain
    new_ref[...] = (edge_ref[...].astype(F32) + message).astype(BF16)
    pick = lax.broadcasted_iota(jnp.int32, (nodes, edges), 1) // degree
    pick = jnp.where(pick == lax.broadcasted_iota(jnp.int32, (nodes, edges), 0), 1.0, 0.0).astype(BF16)
    agg_ref[...] = dot(pick, (message * live).astype(BF16))
    ncot = jnp.broadcast_to(ncot_ref[...].astype(F32)[:, None, :], (nodes, degree, latent))
    cot = cot_ref[...].astype(F32)
    scaled = (cot + live * ncot.reshape(edges, latent)) * gain
    mean_a = jnp.mean(scaled, axis=1, keepdims=True)
    mean_b = jnp.mean(scaled * normed, axis=1, keepdims=True)
    gproj = (inverse * (scaled - mean_a - normed * mean_b)).astype(BF16)
    gproj_ref[...] = gproj
    gpre = (lax.dot_general(gproj, out_w_ref[...], COLS, preferred_element_type=F32) * slope).astype(BF16)
    gpre_ref[...] = gpre
    psum_ref[...] = dot(pick, gpre).astype(BF16)
    back = lax.dot_general(gpre, weight_ref[:latent], COLS, preferred_element_type=F32)
    gedge_ref[...] = (cot + back).astype(BF16)


def edge_call(base, ids, last, low, high, edges, cots, ncot, weight_in, weight_out, gain, first, block):
    count, latent = edges.shape
    hidden = weight_in.shape[1]
    degree = count // ncot.shape[0]
    blocks = count // block
    small = block // degree

    def like(width, dtype, size, total):
        return (
            pl.BlockSpec((size, width), lambda i: (i, 0)),
            jax.ShapeDtypeStruct((total, width), dtype),
        )

    outs = [
        like(latent, BF16, block, count),
        like(latent, F32, small, count // degree),
        like(hidden, BF16, block, count),
        like(latent, BF16, block, count),
        like(hidden, BF16, block, count),
        like(hidden, BF16, small, count // degree),
        like(latent, BF16, block, count),
    ]
    return launch(
        lambda *refs: edge_kernel(first, degree, *refs),
        grid=(blocks,),
        in_specs=[
            rows(base, block),
            rows(ids, block),
            whole(last),
            whole(low),
            whole(high),
            rows(edges, block),
            rows(cots, block),
            rows(ncot, small),
            whole(weight_in),
            whole(weight_out),
            whole(gain),
        ],
        out_specs=[spec for spec, _ in outs],
        out_shape=[shape for _, shape in outs],
        scratch_shapes=[pltpu.VMEM((last.shape[0] + 2 * low.shape[0], hidden), BF16)],
        compiler_params=params(EDGE_LIMIT),
        cost_estimate=cost("edge_block"),
        name="edge_block",
    )(base, ids, last, low, high, streamed(edges), streamed(cots), ncot, weight_in, weight_out, gain)


def select_kernel(ids_ref, *refs):
    pieces, (low_ref, high_ref) = refs[:-2], refs[-2:]
    total, at = None, 0
    for piece in pieces:
        term = dot(one_hot(ids_ref[...], at, piece.shape[0]), piece[...])
        total = term if total is None else total + term
        at += piece.shape[0]
    half = low_ref.shape[0]
    low_ref[...] = total[:half].astype(BF16)
    high_ref[...] = total[half:].astype(BF16)


def select_call(ids, pieces):
    count, width = ids.shape[0], pieces[0].shape[1]
    half = jax.ShapeDtypeStruct((count // 2, width), BF16)
    return launch(
        select_kernel,
        out_shape=[half, half],
        compiler_params=params(),
        cost_estimate=cost("select_rows"),
        name="select_rows",
    )(ids, *pieces)


def rim_sum_kernel(first, ids_ref, values_ref, mine_ref, got_ref, low_ref, high_ref, sum_ref):
    sum_ref[...] = mine_ref[...] + got_ref[...]
    half = low_ref.shape[0]
    places = lax.broadcasted_iota(jnp.int32, (2 * half, ids_ref.shape[1]), 0) + first
    hot = jnp.where(places == ids_ref[...], 1.0, 0.0).astype(BF16)
    total = dot(hot, values_ref[...])
    low_ref[...] = total[:half].astype(BF16)
    high_ref[...] = total[half:].astype(BF16)


def rim_sum_call(ids, values, mine, got, first, count):
    half = jax.ShapeDtypeStruct((count // 2, values.shape[1]), BF16)
    return launch(
        lambda *refs: rim_sum_kernel(first, *refs),
        out_shape=[half, half, jax.ShapeDtypeStruct(mine.shape, F32)],
        compiler_params=params(),
        cost_estimate=cost("rim_sums"),
        name="rim_sums",
    )(ids, values, mine, got)


def patch_sum_kernel(ids_ref, values_ref, out_ref):
    size = out_ref.shape[0]
    places = lax.broadcasted_iota(jnp.int32, (size, ids_ref.shape[1]), 0) + pl.program_id(0) * size
    hot = jnp.where(places == ids_ref[...], 1.0, 0.0).astype(BF16)
    out_ref[...] = dot(hot, values_ref[...])


def patch_sum_call(ids, values, count, block):
    width = values.shape[1]
    return launch(
        patch_sum_kernel,
        grid=(count // block,),
        in_specs=[whole(ids), whole(values)],
        out_specs=pl.BlockSpec((block, width), lambda i: (i, 0)),
        out_shape=jax.ShapeDtypeStruct((count, width), F32),
        compiler_params=params(),
        cost_estimate=cost("patch_sums"),
        name="patch_sums",
    )(ids, values)


def add_rim_kernel(ids_ref, low_ref, high_ref, start_ref, coarse_ref, *outs):
    half = low_ref.shape[0]
    size = outs[0].shape[0]
    latent = start_ref.shape[1]
    coarse = coarse_ref[...]
    few = coarse.shape[0]
    counts = coarse[:, 2 * latent :]
    high = jnp.floor(counts * (1.0 / 64.0))
    for j, out in enumerate(outs):
        places = lax.broadcasted_iota(jnp.int32, (size, 2 * half), 0) + j * size
        hot = jnp.where(places == ids_ref[...], 1.0, 0.0).astype(BF16)
        total = start_ref[j * size : (j + 1) * size] + dot(hot[:, :half], low_ref[...])
        total = total + dot(hot[:, half:], high_ref[...])
        out[:size] = total.astype(BF16)
        if out.shape[0] > size:
            out[size : size + few] = coarse[:, :latent].astype(BF16)
            out[size + few : size + 2 * few] = coarse[:, latent : 2 * latent].astype(BF16)
            out[size + 2 * few :] = jnp.zeros((few, latent), BF16)
            out[size + 2 * few :, :128] = high.astype(BF16)
            out[size + 2 * few :, 128:256] = (counts - 64.0 * high).astype(BF16)


def add_rim_call(ids, low, high, start, coarse, size, extended):
    count, width = start.shape
    pieces = count // size
    extra = [3 * coarse.shape[0] if extended and j == pieces - 1 else 0 for j in range(pieces)]
    return launch(
        add_rim_kernel,
        out_shape=[jax.ShapeDtypeStruct((size + more, width), BF16) for more in extra],
        compiler_params=params(),
        cost_estimate=cost("add_rim_sums"),
        name="add_rim_sums",
    )(ids, low, high, start, coarse)


def edge_grads_kernel(edge_ref, gpre_ref, hid_ref, gproj_ref, in_ref, out_ref):
    in_ref[...] = lax.dot_general(edge_ref[...], gpre_ref[...], ROWS, preferred_element_type=F32)
    out_ref[...] = lax.dot_general(hid_ref[...], gproj_ref[...], ROWS, preferred_element_type=F32)


def edge_grads_call(edges, gpre, hid, gproj):
    latent, hidden = edges.shape[1], gpre.shape[1]
    return launch(
        edge_grads_kernel,
        out_shape=[
            jax.ShapeDtypeStruct((latent, hidden), F32),
            jax.ShapeDtypeStruct((hidden, latent), F32),
        ],
        compiler_params=params(),
        cost_estimate=cost("edge_grads"),
        name="edge_grads",
    )(edges, gpre, hid, gproj)


def pack_kernel(pieces, where_ref, psum_ref, edge_ref, out_ref, patch_ref, low_ref, high_ref, *refs):
    tables = refs[:pieces]
    keep_ref, send_ref, total = refs[pieces:]
    latent = tables[0].shape[1]
    size = tables[0].shape[0]
    parts = [patch_ref[j * size : (j + 1) * size].astype(BF16) for j in range(pieces - 2)]
    grad = None
    for table, part in zip(tables, parts + [low_ref[...], high_ref[...]]):
        term = lax.dot_general(table[...], part, ROWS, preferred_element_type=F32)
        grad = term if grad is None else grad + term
    total[:latent] = edge_ref[...]
    total[latent : 2 * latent] = grad
    total[2 * latent : 3 * latent] = lax.dot_general(
        tables[0][...], psum_ref[...], ROWS, preferred_element_type=F32
    )
    total[3 * latent :] = out_ref[...]
    feats, pairs, span, width = keep_ref.shape
    unit = span // 4
    bit = where_ref[0] & 1
    for m in range(pairs):
        for slot in range(4):
            for ref, which in ((keep_ref, bit), (send_ref, 1 - bit)):
                patch = 2 * m + which
                row = (patch * 3 + slot) * unit if slot < 3 else 3 * latent + patch * unit
                block = total[pl.ds(pl.multiple_of(row, unit), unit), :]
                for f in range(feats):
                    ref[f, m, slot * unit : (slot + 1) * unit, :] = block[:, f * width : (f + 1) * width].astype(
                        ref.dtype
                    )


def pack_call(where, psum, edge_grad, out_grad, patch_sum, low, high, tables, feats, patches):
    latent, hidden = edge_grad.shape
    shape = (feats, patches // 2, 4 * latent // patches, hidden // feats)
    vmem = pl.BlockSpec(memory_space=pltpu.VMEM)
    return launch(
        lambda *refs: pack_kernel(len(tables), *refs),
        in_specs=[pl.BlockSpec(memory_space=pltpu.SMEM)] + [vmem] * (6 + len(tables)),
        out_shape=[jax.ShapeDtypeStruct(shape, F32), jax.ShapeDtypeStruct(shape, BF16)],
        scratch_shapes=[pltpu.VMEM((4 * latent, hidden), F32)],
        compiler_params=params(),
        cost_estimate=cost("pack_grads"),
        name="pack_grads",
    )(where, psum, edge_grad, out_grad, patch_sum, low, high, *tables)


def coarse_sum_kernel(ids_ref, lat_ref, cot_ref, where_ref, mine_ref, other_ref):
    latent = lat_ref.shape[1]
    half = mine_ref.shape[0]
    core = where_ref[0] & 1
    for ref, bit in ((mine_ref, core), (other_ref, 1 - core)):
        places = lax.broadcasted_iota(jnp.int32, (half, ids_ref.shape[1]), 0) + bit * half
        live = jnp.where(places == ids_ref[...], 1.0, 0.0)
        hot = live.astype(BF16)
        ref[:, :latent] = dot(hot, lat_ref[...])
        ref[:, latent : 2 * latent] = dot(hot, cot_ref[...])
        ref[:, 2 * latent :] = jnp.broadcast_to(jnp.sum(live, axis=1, keepdims=True), (half, 128))


def coarse_sum_call(ids, lat, cot, where, coarse):
    vmem = pl.BlockSpec(memory_space=pltpu.VMEM)
    half = jax.ShapeDtypeStruct((coarse // 2, 2 * lat.shape[1] + 128), F32)
    return launch(
        coarse_sum_kernel,
        in_specs=[vmem, vmem, vmem, pl.BlockSpec(memory_space=pltpu.SMEM)],
        out_shape=[half, half],
        compiler_params=params(),
        cost_estimate=cost("coarse_sums"),
        name="coarse_sums",
    )(ids, lat, cot, where)


def add_pair_kernel(a_ref, b_ref, out_ref):
    out_ref[...] = (a_ref[...].astype(F32) + b_ref[...].astype(F32)).astype(out_ref.dtype)


def add_pair_call(a, b):
    return launch(
        add_pair_kernel,
        out_shape=jax.ShapeDtypeStruct(a.shape, a.dtype),
        compiler_params=params(),
        cost_estimate=cost("add_pair"),
        name="add_pair",
    )(a, b)


def far_sum_kernel(own_ref, sent_ref, got_ref, far_ref, coarse_ref):
    size = own_ref.shape[0]
    far_ref[...] = (own_ref[...].astype(F32) + got_ref[:size].astype(F32)).astype(BF16)
    coarse_ref[...] = (sent_ref[size:].astype(F32) + got_ref[size:].astype(F32)).astype(BF16)


def far_sum_call(own, sent, got):
    size, width = own.shape
    return launch(
        far_sum_kernel,
        out_shape=[
            jax.ShapeDtypeStruct((size, width), BF16),
            jax.ShapeDtypeStruct((sent.shape[0] - size, width), BF16),
        ],
        compiler_params=params(),
        cost_estimate=cost("far_sum"),
        name="far_sum",
    )(own, sent, got)


def add_split_kernel(axis, shift, where_ref, keep_ref, got_ref, mine_ref, other_ref):
    bit = (where_ref[axis] >> shift) & 1
    for ref, which in ((mine_ref, bit), (other_ref, 1 - bit)):
        for a in range(keep_ref.shape[0]):
            ref[a] = (keep_ref[a, which] + got_ref[a, which].astype(F32)).astype(ref.dtype)


def add_split_call(name, where, axis, distance, keep, got, send_type):
    vmem = pl.BlockSpec(memory_space=pltpu.VMEM)
    shape = keep.shape[:1] + keep.shape[2:]
    return launch(
        functools.partial(add_split_kernel, axis, distance.bit_length() - 1),
        in_specs=[pl.BlockSpec(memory_space=pltpu.SMEM), vmem, vmem],
        out_shape=[jax.ShapeDtypeStruct(shape, F32), jax.ShapeDtypeStruct(shape, send_type)],
        compiler_params=params(),
        cost_estimate=cost(name),
        name=name,
    )(where, keep, got)


def last_grads_kernel(scale, keep_ref, got_ref, in_ref, out_ref):
    rows_in = in_ref.shape[0]
    in_ref[...] = (keep_ref[:rows_in] + got_ref[:rows_in].astype(F32)) * scale
    out_ref[...] = (keep_ref[rows_in:] + got_ref[rows_in:].astype(F32)) * scale


def last_grads_call(scale, keep, got, rows_in):
    span, width = keep.shape
    return launch(
        lambda *refs: last_grads_kernel(scale, *refs),
        out_shape=[
            jax.ShapeDtypeStruct((rows_in, width), F32),
            jax.ShapeDtypeStruct((span - rows_in, width), F32),
        ],
        compiler_params=params(),
        cost_estimate=cost("last_grads"),
        name="last_grads",
    )(keep, got)


def node_kernel(where_ref, ids_ref, lat_ref, cot_ref, agg_ref, back_ref, *refs):
    pieces, (new_ref, grad_ref, total) = refs[:-3], refs[-3:]
    latent = lat_ref.shape[1]
    for j, piece in enumerate(pieces):
        size = piece.shape[0] // 3
        owner = where_ref[0] ^ j
        place = (owner & 1) * 2 + (owner >> 1) if len(pieces) == 4 else j
        here = pl.ds(pl.multiple_of(place * size, size), size)
        total[here, :latent] = piece[:size].astype(F32)
        total[here, latent : 2 * latent] = piece[size : 2 * size].astype(F32)
        counts = piece[2 * size :].astype(F32)
        total[here, 2 * latent :] = 64.0 * counts[:, :128] + counts[:, 128:256]
    sums = total[...]
    means = sums[:, : 2 * latent] / jnp.maximum(sums[:, 2 * latent : 2 * latent + 1], 1.0)
    places = lax.broadcasted_iota(jnp.int32, (sums.shape[0], ids_ref.shape[1]), 0)
    hot = jnp.where(places == ids_ref[...], 1.0, 0.0).astype(BF16)
    high = means.astype(BF16)
    low = (means - high.astype(F32)).astype(BF16)
    pooled = lax.dot_general(hot, high, ROWS, preferred_element_type=F32)
    pooled = pooled + lax.dot_general(hot, low, ROWS, preferred_element_type=F32)
    new_ref[...] = (lat_ref[...].astype(F32) + agg_ref[...] + pooled[:, :latent]).astype(BF16)
    grad_ref[...] = (cot_ref[...].astype(F32) + back_ref[...] + pooled[:, latent:]).astype(BF16)


def node_call(where, ids, lat, cot, agg, back, pieces):
    vmem = pl.BlockSpec(memory_space=pltpu.VMEM)
    coarse = sum(piece.shape[0] // 3 for piece in pieces)
    width = 2 * lat.shape[1] + 128
    return launch(
        node_kernel,
        in_specs=[pl.BlockSpec(memory_space=pltpu.SMEM)] + [vmem] * (5 + len(pieces)),
        scratch_shapes=[pltpu.VMEM((coarse, width), F32)],
        out_shape=[jax.ShapeDtypeStruct(lat.shape, BF16)] * 2,
        compiler_params=params(),
        cost_estimate=cost("node_outputs"),
        name="node_outputs",
    )(where, ids, lat, cot, agg, back, *pieces)


def node_back_kernel(own_ref, far_ref, near_ref, psum_ref, weight_ref, out_ref):
    latent = own_ref.shape[1]
    total = own_ref[...].astype(F32) + far_ref[...].astype(F32) + near_ref[...].astype(F32)
    back = lax.dot_general(
        total.astype(BF16), weight_ref[latent : 2 * latent], COLS, preferred_element_type=F32
    )
    own = lax.dot_general(psum_ref[...], weight_ref[2 * latent :], COLS, preferred_element_type=F32)
    out_ref[...] = back + own


def node_back_call(own, far, near, psum, weight_in):
    return launch(
        node_back_kernel,
        out_shape=jax.ShapeDtypeStruct(own.shape, F32),
        compiler_params=params(),
        cost_estimate=cost("grad_node"),
        name="grad_node",
    )(own, far, near, psum, weight_in)


def xor_swap(value, axis, distance):
    size = lax.axis_size(axis)
    return lax.ppermute(value, axis, [(i, i ^ distance) for i in range(size)])


def bits_of(size):
    return [1 << b for b in range(size.bit_length() - 1)]


def split(value, dim, bit):
    mine = lax.dynamic_index_in_dim(value, bit, dim, keepdims=False)
    other = lax.dynamic_index_in_dim(value, 1 - bit, dim, keepdims=False)
    return mine, other


def coarse_reduce(sums, other, patch):
    width = sums.shape[1]
    bits = bits_of(lax.axis_size("patch"))
    sums = sums + xor_swap(other, "patch", 1)
    for distance in bits[1:]:
        mine, other = split(sums.reshape(2, -1, width), 0, (patch // distance) % 2)
        sums = mine + xor_swap(other, "patch", distance)
    for distance in bits_of(lax.axis_size("feat")):
        sums = sums + xor_swap(sums, "feat", distance)
    for distance in reversed(bits):
        got = xor_swap(sums, "patch", distance)
        first = (patch // distance) % 2 == 0
        sums = jnp.concatenate([jnp.where(first, sums, got), jnp.where(first, got, sums)], axis=0)
    return sums


def shards(
    node_lat,
    edge_lat,
    neighbours,
    send_rows,
    coarse_of,
    weight_in,
    bias_in,
    weight_out,
    norm_gain,
    edge_cotangent,
    node_cotangent,
):
    Order.token = None
    node_count, latent = node_lat.shape
    degree = edge_lat.shape[1]
    edge_count = node_count * degree
    rim_rows = send_rows.shape[0] // 2
    feat_count = lax.axis_size("feat")
    patch_count = lax.axis_size("patch")
    patch_total = feat_count * node_count
    coarse_total = COARSE_DEV * patch_count * feat_count
    feat = lax.axis_index("feat")
    patch = lax.axis_index("patch")
    block = min(512, edge_count)
    ring_up = [(i, (i + 1) % patch_count) for i in range(patch_count)]
    ring_down = [(j, i) for i, j in ring_up]

    def relative(ids):
        moved = ((ids // node_count) ^ feat) * node_count + ids % node_count
        return jnp.where(ids < patch_total, moved, ids)

    flat_edges = edge_lat.reshape(edge_count, latent)
    flat_cots = edge_cotangent.reshape(edge_count, latent)
    ids = relative(neighbours).T.reshape(edge_count)
    ids_col = ids[:, None]
    ids_row = ids[None, :]
    send_rel = relative(send_rows)
    send_col = send_rel[:, None]
    send_row = send_rel[None, :]
    bias = bias_in[None, :]
    gain = norm_gain[None, :]
    coarse_row = coarse_of[None, :]

    where = jnp.stack([patch, feat]).astype(jnp.int32)
    whole_step = feat_count == 4 and patch_count == 4

    if feat_count == 4:
        far = xor_swap(node_lat, "feat", 2)
        near = xor_swap(node_lat, "feat", 1)
        last = xor_swap(far, "feat", 1)
        pieces = [node_lat, near, far, last]
    else:
        pieces = [node_lat]
        for distance in bits_of(feat_count):
            pieces = pieces + [xor_swap(piece, "feat", distance) for piece in pieces]

    coarse, coarse_other = coarse_sum_call(coarse_row, node_lat, node_cotangent, where, coarse_total)
    if whole_step:
        got = xor_swap(coarse_other, "patch", 1)
        halves = (1, 2, coarse.shape[0] // 2, coarse.shape[1])
        coarse, coarse_other = add_split_call("coarse_split", where, 0, 2, coarse.reshape(halves), got.reshape(halves), F32)
        coarse, coarse_other = coarse[0], coarse_other[0]
        got = xor_swap(coarse_other, "patch", 2)
    else:
        coarse = coarse_reduce(coarse, coarse_other, patch)
        got = jnp.zeros_like(coarse)
    base = base_call(
        flat_edges, node_lat, ids_col, weight_in, bias, (ids_row, send_col, send_row, coarse_row), pieces[:-1], block
    )
    to_lower, to_upper = select_call(send_col, pieces)
    from_lower = lax.ppermute(to_upper, "patch", ring_up)
    from_upper = lax.ppermute(to_lower, "patch", ring_down)
    coarse = add_pair_call(coarse, got)
    got = xor_swap(coarse, "feat", 2) if whole_step else jnp.zeros_like(coarse)

    edge_new, aggregate, hidden_act, grad_proj, grad_pre, pre_sum, grad_edge = edge_call(
        base,
        ids_col,
        pieces[-1],
        from_lower,
        from_upper,
        flat_edges,
        flat_cots,
        node_cotangent,
        weight_in,
        weight_out,
        gain,
        patch_total - node_count,
        block)

    rim_low, rim_high, coarse = rim_sum_call(ids_row, grad_pre, coarse, got, patch_total, 2 * rim_rows)
    back_upper = lax.ppermute(rim_low, "patch", ring_down)
    back_lower = lax.ppermute(rim_high, "patch", ring_up)
    patch_sum = patch_sum_call(ids_row, grad_pre, patch_total, node_count)
    span, width = 4 * latent // patch_count, latent // feat_count
    steps = [("patch", d) for d in bits_of(patch_count)[1:]] + [("feat", d) for d in bits_of(feat_count)]

    def fold(step, keep, received):
        axis, distance = steps[step]
        shape = (-1, 2, span, width)
        keep, send = add_split_call(
            f"fold{min(step, 2)}",
            where,
            int(axis == "feat"),
            distance,
            keep.reshape(shape),
            received.reshape(shape),
            BF16,
        )
        return keep, xor_swap(send, axis, distance)

    edge_grad, out_grad = edge_grads_call(flat_edges, grad_pre, hidden_act, grad_proj)
    sums = add_rim_call(
        send_row, back_lower, back_upper, patch_sum, coarse, node_count, whole_step
    )
    tables = pieces + [from_lower, from_upper]
    keep, send = pack_call(
        where, pre_sum, edge_grad, out_grad, patch_sum, rim_low, rim_high, tables, feat_count, patch_count
    )
    got_core = xor_swap(send, "patch", 1)
    keep, received = fold(0, keep, got_core)
    if feat_count == 4:
        relay = xor_swap(sums[3], "feat", 1)
        if whole_step:
            far_sum, coarse_all = far_sum_call(sums[2], sums[3], relay)
        else:
            far_sum = add_pair_call(sums[2], relay)
        got_far = xor_swap(far_sum, "feat", 2)
        got_near = xor_swap(sums[1], "feat", 1)
        own = [sums[0], got_far, got_near]
    else:
        parts = sums
        for distance in reversed(bits_of(feat_count)):
            arrived = [xor_swap(part, "feat", distance) for part in parts[distance:]]
            parts = [add_pair_call(a, b) for a, b in zip(parts[:distance], arrived)]
        own = [parts[0], jnp.zeros_like(parts[0]), jnp.zeros_like(parts[0])]
    keep, received = fold(1, keep, received)
    back = node_back_call(*own, pre_sum, weight_in)
    keep, received = fold(2, keep, received)
    if whole_step:
        parts = [coarse_all] + [xor_swap(coarse_all, "patch", j) for j in range(1, 4)]
    else:
        counts = jnp.pad(coarse[:, 2 * latent :], ((0, 0), (128, latent - 256)))
        parts = [jnp.concatenate([coarse[:, :latent], coarse[:, latent : 2 * latent], counts], axis=0)]
    node_new, grad_node = node_call(
        where, coarse_row, node_lat, node_cotangent, aggregate, back, parts
    )
    for step in range(3, len(steps)):
        keep, received = fold(step, keep, received)
    scale = 1.0 / math.sqrt(edge_count * patch_count * feat_count)
    in_rows = 3 * latent // patch_count
    grads_in, grads_out = last_grads_call(scale, keep.reshape(span, width), received.reshape(span, width), in_rows)
    return (
        edge_new.reshape(edge_lat.shape),
        node_new,
        grad_edge.reshape(edge_lat.shape),
        grad_node,
        grads_in,
        grads_out,
    )


def solution(mesh):
    return jax.shard_map(
        shards,
        mesh=mesh,
        in_specs=(
            P(("groups", "patch", "feat"), None),
            P(("groups", "patch", "feat"), None, None),
            P(None, ("patch", "feat")),
            P("patch"),
            P(("patch", "feat")),
            P(),
            P(),
            P(),
            P(),
            P(("groups", "patch", "feat"), None, None),
            P(("groups", "patch", "feat"), None),
        ),
        out_specs=(
            P(("groups", "patch", "feat"), None, None),
            P(("groups", "patch", "feat"), None),
            P(("groups", "patch", "feat"), None, None),
            P(("groups", "patch", "feat"), None),
            P(("groups", "patch"), "feat"),
            P(("groups", "patch"), "feat"),
        ),
        check_vma=False,
    )
```

```python
import functools
import math

import jax
import jax.numpy as jnp
from jax import lax
from jax.experimental import pallas as pl
from jax.experimental.pallas import tpu as pltpu
from jax.sharding import PartitionSpec as P

COARSE_DEV = 4
LAYER_EPS = 1e-05
F32 = jnp.float32
BF16 = jnp.bfloat16
VMEM_LIMIT = 24 * 1024 * 1024
EDGE_LIMIT = 24 * 1024 * 1024
COLS = (((1,), (1,)), ((), ()))
ROWS = (((0,), (0,)), ((), ()))


def dot(a, b):
    return jnp.dot(a, b, preferred_element_type=F32)


def params(limit=None):
    return pltpu.CompilerParams(vmem_limit_bytes=limit or VMEM_LIMIT)


COST = {
    "base_terms": 15,
    "select_rows": 2,
    "add_pair": 1,
    "edge_block": 36,
    "rim_sums": 2.4,
    "patch_sums": 0.3,
    "edge_grads": 0.3,
    "add_rim_sums": 0.3,
    "pack_grads": 0.3,
    "coarse_rows": 0.3,
    "far_sum": 30,
    "node_outputs": 2,
    "grad_node": .1,
    "last_grads": 1.5,
    "coarse_sums": 1,
    "coarse_split": 1,
    "fold0": 0.3,
    "fold1": 0.3,
    "fold3": 0.3,
    "fold2": 0.3,
}


def cost(name):
    micros = COST[name]
    return pl.CostEstimate(flops=int(micros * 1.15e9), bytes_accessed=1 << 20, transcendentals=0)


class Order:
    token = None


def launch(kernel, out_shape, in_specs=None, out_specs=None, grid=None, **settings):
    outs = list(out_shape) if isinstance(out_shape, (list, tuple)) else [out_shape]
    mark = jax.ShapeDtypeStruct((8, 128), F32)

    def call(*args):
        count = len(args)
        late = [] if Order.token is None else [Order.token]
        vmem = pl.BlockSpec(memory_space=pltpu.VMEM)
        specs = list(in_specs or [vmem] * count) + [pl.BlockSpec(memory_space=pl.ANY)] * len(late)
        end = count + len(late) + len(outs)

        def body(*refs):
            refs[end][...] = jnp.zeros((8, 128), F32)
            kernel(*refs[:count], *refs[count + len(late) : end], *refs[end + 1 :])

        if grid is None:
            places, more = [vmem] * (len(outs) + 1), {}
        else:
            places = list(out_specs) if isinstance(out_specs, (list, tuple)) else [out_specs]
            places, more = places + [pl.BlockSpec((8, 128), lambda i: (0, 0))], {"grid": grid}
        results = pl.pallas_call(
            body, out_shape=outs + [mark], in_specs=specs, out_specs=places, **more, **settings
        )(*args, *late)
        Order.token = results[-1]
        return results[:-1] if isinstance(out_shape, (list, tuple)) else results[0]

    return call


def streamed(array):
    return pltpu.with_memory_space_constraint(array, pltpu.HBM)


def held(array):
    return pltpu.with_memory_space_constraint(array, pltpu.VMEM)


def whole(array):
    zeros = (0,) * array.ndim
    return pl.BlockSpec(array.shape, lambda i: zeros)


def rows(array, block):
    rest = (0,) * (array.ndim - 1)
    return pl.BlockSpec((block,) + array.shape[1:], lambda i: (i,) + rest)


def one_hot(ids, first, count):
    lanes = lax.broadcasted_iota(jnp.int32, (ids.shape[0], count), 1) + first
    return jnp.where(ids == lanes, 1.0, 0.0).astype(BF16)


def fill_table(table, pieces, weight_ref):
    latent = pieces[0].shape[1]
    at = 0
    for piece in pieces:
        size = piece.shape[0]
        table[at : at + size] = dot(piece[...], weight_ref[latent : 2 * latent]).astype(BF16)
        at += size


def base_kernel(degree, edge_ref, node_ref, ids_ref, weight_ref, bias_ref, *refs):
    pieces, (out_ref, table) = refs[:-2], refs[-2:]
    latent = edge_ref.shape[1]

    @pl.when(pl.program_id(0) == 0)
    def _():
        fill_table(table, pieces, weight_ref)

    edges = edge_ref.shape[0]
    term = dot(node_ref[...], weight_ref[2 * latent :]) + bias_ref[...]
    total = dot(edge_ref[...], weight_ref[:latent])
    total = total + dot(one_hot(ids_ref[...], 0, table.shape[0]), table[...])
    hidden = total.shape[1]
    total = total.reshape(edges // degree, degree, hidden) + term[:, None, :]
    out_ref[...] = total.reshape(edges, hidden)


def base_call(edges, nodes, ids, weight_in, bias, early, pieces, block):
    count, latent = edges.shape
    hidden = weight_in.shape[1]
    degree = count // nodes.shape[0]
    size = sum(piece.shape[0] for piece in pieces)
    return launch(
        lambda *refs: base_kernel(degree, *refs[:5], *refs[5 + len(early) :]),
        grid=(count // block,),
        in_specs=[
            rows(edges, block),
            rows(nodes, block // degree),
            rows(ids, block),
            whole(weight_in),
            whole(bias),
        ]
        + [pl.BlockSpec(memory_space=pl.ANY)] * len(early)
        + [whole(piece) for piece in pieces],
        out_specs=pl.BlockSpec((block, hidden), lambda i: (i, 0)),
        out_shape=jax.ShapeDtypeStruct((count, hidden), F32),
        scratch_shapes=[pltpu.VMEM((size, hidden), BF16)],
        compiler_params=params(),
        cost_estimate=cost("base_terms"),
        name="base_terms",
    )(streamed(edges), nodes, ids, weight_in, bias, *early, *pieces)


def edge_kernel(
    first,
    degree,
    base_ref,
    ids_ref,
    last_ref,
    low_ref,
    high_ref,
    edge_ref,
    cot_ref,
    ncot_ref,
    weight_ref,
    out_w_ref,
    gain_ref,
    new_ref,
    agg_ref,
    hid_ref,
    gproj_ref,
    gpre_ref,
    psum_ref,
    gedge_ref,
    table,
):
    latent = low_ref.shape[1]

    @pl.when(pl.program_id(0) == 0)
    def _():
        fill_table(table, (last_ref, low_ref, high_ref), weight_ref)

    ids = ids_ref[...]
    edges = ids.shape[0]
    nodes = edges // degree
    limit = first + table.shape[0]
    live = jnp.where(ids < limit, 1.0, 0.0)
    value = base_ref[...] + dot(one_hot(ids, first, table.shape[0]), table[...])
    sig = 0.5 + 0.5 * jnp.tanh(0.5 * value)
    act = value * sig
    slope = sig + act * (1.0 - sig)
    hid = act.astype(BF16)
    hid_ref[...] = hid
    projected = dot(hid, out_w_ref[...])
    centre = projected - jnp.mean(projected, axis=1, keepdims=True)
    inverse = lax.rsqrt(jnp.mean(centre * centre, axis=1, keepdims=True) + LAYER_EPS)
    normed = centre * inverse
    gain = gain_ref[...]
    message = normed * gain
    new_ref[...] = (edge_ref[...].astype(F32) + message).astype(BF16)
    pick = lax.broadcasted_iota(jnp.int32, (nodes, edges), 1) // degree
    pick = jnp.where(pick == lax.broadcasted_iota(jnp.int32, (nodes, edges), 0), 1.0, 0.0).astype(BF16)
    agg_ref[...] = dot(pick, (message * live).astype(BF16))
    ncot = jnp.broadcast_to(ncot_ref[...].astype(F32)[:, None, :], (nodes, degree, latent))
    cot = cot_ref[...].astype(F32)
    scaled = (cot + live * ncot.reshape(edges, latent)) * gain
    mean_a = jnp.mean(scaled, axis=1, keepdims=True)
    mean_b = jnp.mean(scaled * normed, axis=1, keepdims=True)
    gproj = (inverse * (scaled - mean_a - normed * mean_b)).astype(BF16)
    gproj_ref[...] = gproj
    gpre = (lax.dot_general(gproj, out_w_ref[...], COLS, preferred_element_type=F32) * slope).astype(BF16)
    gpre_ref[...] = gpre
    psum_ref[...] = dot(pick, gpre).astype(BF16)
    back = lax.dot_general(gpre, weight_ref[:latent], COLS, preferred_element_type=F32)
    gedge_ref[...] = (cot + back).astype(BF16)


def edge_call(base, ids, last, low, high, edges, cots, ncot, weight_in, weight_out, gain, first, block):
    count, latent = edges.shape
    hidden = weight_in.shape[1]
    degree = count // ncot.shape[0]
    blocks = count // block
    small = block // degree

    def like(width, dtype, size, total):
        return (
            pl.BlockSpec((size, width), lambda i: (i, 0)),
            jax.ShapeDtypeStruct((total, width), dtype),
        )

    outs = [
        like(latent, BF16, block, count),
        like(latent, F32, small, count // degree),
        like(hidden, BF16, block, count),
        like(latent, BF16, block, count),
        like(hidden, BF16, block, count),
        like(hidden, BF16, small, count // degree),
        like(latent, BF16, block, count),
    ]
    return launch(
        lambda *refs: edge_kernel(first, degree, *refs),
        grid=(blocks,),
        in_specs=[
            rows(base, block),
            rows(ids, block),
            whole(last),
            whole(low),
            whole(high),
            rows(edges, block),
            rows(cots, block),
            rows(ncot, small),
            whole(weight_in),
            whole(weight_out),
            whole(gain),
        ],
        out_specs=[spec for spec, _ in outs],
        out_shape=[shape for _, shape in outs],
        scratch_shapes=[pltpu.VMEM((last.shape[0] + 2 * low.shape[0], hidden), BF16)],
        compiler_params=params(EDGE_LIMIT),
        cost_estimate=cost("edge_block"),
        name="edge_block",
    )(base, ids, last, low, high, streamed(edges), streamed(cots), ncot, weight_in, weight_out, gain)


def select_kernel(ids_ref, *refs):
    pieces, (low_ref, high_ref) = refs[:-2], refs[-2:]
    total, at = None, 0
    for piece in pieces:
        term = dot(one_hot(ids_ref[...], at, piece.shape[0]), piece[...])
        total = term if total is None else total + term
        at += piece.shape[0]
    half = low_ref.shape[0]
    low_ref[...] = total[:half].astype(BF16)
    high_ref[...] = total[half:].astype(BF16)


def select_call(ids, pieces):
    count, width = ids.shape[0], pieces[0].shape[1]
    half = jax.ShapeDtypeStruct((count // 2, width), BF16)
    return launch(
        select_kernel,
        out_shape=[half, half],
        compiler_params=params(),
        cost_estimate=cost("select_rows"),
        name="select_rows",
    )(ids, *pieces)


def rim_sum_kernel(first, ids_ref, values_ref, mine_ref, got_ref, low_ref, high_ref, sum_ref):
    sum_ref[...] = mine_ref[...] + got_ref[...]
    half = low_ref.shape[0]
    places = lax.broadcasted_iota(jnp.int32, (2 * half, ids_ref.shape[1]), 0) + first
    hot = jnp.where(places == ids_ref[...], 1.0, 0.0).astype(BF16)
    total = dot(hot, values_ref[...])
    low_ref[...] = total[:half].astype(BF16)
    high_ref[...] = total[half:].astype(BF16)


def rim_sum_call(ids, values, mine, got, first, count):
    half = jax.ShapeDtypeStruct((count // 2, values.shape[1]), BF16)
    return launch(
        lambda *refs: rim_sum_kernel(first, *refs),
        out_shape=[half, half, jax.ShapeDtypeStruct(mine.shape, F32)],
        compiler_params=params(),
        cost_estimate=cost("rim_sums"),
        name="rim_sums",
    )(ids, values, mine, got)


def patch_sum_kernel(ids_ref, values_ref, out_ref):
    size = out_ref.shape[0]
    places = lax.broadcasted_iota(jnp.int32, (size, ids_ref.shape[1]), 0) + pl.program_id(0) * size
    hot = jnp.where(places == ids_ref[...], 1.0, 0.0).astype(BF16)
    out_ref[...] = dot(hot, values_ref[...])


def patch_sum_call(ids, values, count, block):
    width = values.shape[1]
    return launch(
        patch_sum_kernel,
        grid=(count // block,),
        in_specs=[whole(ids), whole(values)],
        out_specs=pl.BlockSpec((block, width), lambda i: (i, 0)),
        out_shape=jax.ShapeDtypeStruct((count, width), F32),
        compiler_params=params(),
        cost_estimate=cost("patch_sums"),
        name="patch_sums",
    )(ids, values)


def add_rim_kernel(ids_ref, low_ref, high_ref, start_ref, coarse_ref, *outs):
    half = low_ref.shape[0]
    size = outs[0].shape[0]
    latent = start_ref.shape[1]
    coarse = coarse_ref[...]
    few = coarse.shape[0]
    counts = coarse[:, 2 * latent :]
    high = jnp.floor(counts * (1.0 / 64.0))
    for j, out in enumerate(outs):
        places = lax.broadcasted_iota(jnp.int32, (size, 2 * half), 0) + j * size
        hot = jnp.where(places == ids_ref[...], 1.0, 0.0).astype(BF16)
        total = start_ref[j * size : (j + 1) * size] + dot(hot[:, :half], low_ref[...])
        total = total + dot(hot[:, half:], high_ref[...])
        out[:size] = total.astype(BF16)
        if out.shape[0] > size:
            out[size : size + few] = coarse[:, :latent].astype(BF16)
            out[size + few : size + 2 * few] = coarse[:, latent : 2 * latent].astype(BF16)
            out[size + 2 * few :] = jnp.zeros((few, latent), BF16)
            out[size + 2 * few :, :128] = high.astype(BF16)
            out[size + 2 * few :, 128:256] = (counts - 64.0 * high).astype(BF16)


def add_rim_call(ids, low, high, start, coarse, size, extended):
    count, width = start.shape
    pieces = count // size
    extra = [3 * coarse.shape[0] if extended and j == pieces - 1 else 0 for j in range(pieces)]
    return launch(
        add_rim_kernel,
        out_shape=[jax.ShapeDtypeStruct((size + more, width), BF16) for more in extra],
        compiler_params=params(),
        cost_estimate=cost("add_rim_sums"),
        name="add_rim_sums",
    )(ids, low, high, start, coarse)


def edge_grads_kernel(edge_ref, gpre_ref, hid_ref, gproj_ref, in_ref, out_ref):
    in_ref[...] = lax.dot_general(edge_ref[...], gpre_ref[...], ROWS, preferred_element_type=F32)
    out_ref[...] = lax.dot_general(hid_ref[...], gproj_ref[...], ROWS, preferred_element_type=F32)


def edge_grads_call(edges, gpre, hid, gproj):
    latent, hidden = edges.shape[1], gpre.shape[1]
    return launch(
        edge_grads_kernel,
        out_shape=[
            jax.ShapeDtypeStruct((latent, hidden), F32),
            jax.ShapeDtypeStruct((hidden, latent), F32),
        ],
        compiler_params=params(),
        cost_estimate=cost("edge_grads"),
        name="edge_grads",
    )(edges, gpre, hid, gproj)


def pack_kernel(pieces, where_ref, psum_ref, edge_ref, out_ref, patch_ref, low_ref, high_ref, *refs):
    tables = refs[:pieces]
    keep_ref, send_ref, total = refs[pieces:]
    latent = tables[0].shape[1]
    size = tables[0].shape[0]
    parts = [patch_ref[j * size : (j + 1) * size].astype(BF16) for j in range(pieces - 2)]
    grad = None
    for table, part in zip(tables, parts + [low_ref[...], high_ref[...]]):
        term = lax.dot_general(table[...], part, ROWS, preferred_element_type=F32)
        grad = term if grad is None else grad + term
    total[:latent] = grad
    total[latent:] = lax.dot_general(tables[0][...], psum_ref[...], ROWS, preferred_element_type=F32)
    feats, pairs, span, width = keep_ref.shape
    unit = span // 4

    def block(patch, slot):
        row = (patch * 3 + slot) * unit if slot < 3 else 3 * latent + patch * unit
        for ref, start, end in ((edge_ref, 0, latent), (total, latent, 3 * latent), (out_ref, 3 * latent, 4 * latent)):
            if start <= row < end:
                return ref[row - start : row - start + unit]

    for bit in range(2):

        @pl.when((where_ref[0] & 1) == bit)
        def _():
            for m in range(pairs):
                for slot in range(4):
                    for ref, which in ((keep_ref, bit), (send_ref, 1 - bit)):
                        rows_in = block(2 * m + which, slot)
                        for f in range(feats):
                            ref[f, m, slot * unit : (slot + 1) * unit, :] = rows_in[
                                :, f * width : (f + 1) * width
                            ].astype(ref.dtype)


def pack_call(where, psum, edge_grad, out_grad, patch_sum, low, high, tables, feats, patches):
    latent, hidden = edge_grad.shape
    shape = (feats, patches // 2, 4 * latent // patches, hidden // feats)
    vmem = pl.BlockSpec(memory_space=pltpu.VMEM)
    return launch(
        lambda *refs: pack_kernel(len(tables), *refs),
        in_specs=[pl.BlockSpec(memory_space=pltpu.SMEM)] + [vmem] * (6 + len(tables)),
        out_shape=[jax.ShapeDtypeStruct(shape, F32), jax.ShapeDtypeStruct(shape, BF16)],
        scratch_shapes=[pltpu.VMEM((2 * latent, hidden), F32)],
        compiler_params=params(),
        cost_estimate=cost("pack_grads"),
        name="pack_grads",
    )(where, psum, edge_grad, out_grad, patch_sum, low, high, *tables)


def coarse_sum_kernel(ids_ref, lat_ref, cot_ref, where_ref, mine_ref, other_ref):
    latent = lat_ref.shape[1]
    half = mine_ref.shape[0]
    core = where_ref[0] & 1
    for ref, bit in ((mine_ref, core), (other_ref, 1 - core)):
        places = lax.broadcasted_iota(jnp.int32, (half, ids_ref.shape[1]), 0) + bit * half
        live = jnp.where(places == ids_ref[...], 1.0, 0.0)
        hot = live.astype(BF16)
        ref[:, :latent] = dot(hot, lat_ref[...])
        ref[:, latent : 2 * latent] = dot(hot, cot_ref[...])
        ref[:, 2 * latent :] = jnp.broadcast_to(jnp.sum(live, axis=1, keepdims=True), (half, 128))


def coarse_sum_call(ids, lat, cot, where, coarse):
    vmem = pl.BlockSpec(memory_space=pltpu.VMEM)
    half = jax.ShapeDtypeStruct((coarse // 2, 2 * lat.shape[1] + 128), F32)
    return launch(
        coarse_sum_kernel,
        in_specs=[vmem, vmem, vmem, pl.BlockSpec(memory_space=pltpu.SMEM)],
        out_shape=[half, half],
        compiler_params=params(),
        cost_estimate=cost("coarse_sums"),
        name="coarse_sums",
    )(ids, lat, cot, where)


def add_pair_kernel(a_ref, b_ref, out_ref):
    out_ref[...] = (a_ref[...].astype(F32) + b_ref[...].astype(F32)).astype(out_ref.dtype)


def add_pair_call(a, b):
    return launch(
        add_pair_kernel,
        out_shape=jax.ShapeDtypeStruct(a.shape, a.dtype),
        compiler_params=params(),
        cost_estimate=cost("add_pair"),
        name="add_pair",
    )(a, b)


def coarse_rows_kernel(sent_ref, got_ref, out_ref):
    few = out_ref.shape[0]
    out_ref[...] = (sent_ref[-few:].astype(F32) + got_ref[-few:].astype(F32)).astype(BF16)


def coarse_rows_call(sent, got, few):
    return launch(
        coarse_rows_kernel,
        out_shape=jax.ShapeDtypeStruct((few, sent.shape[1]), BF16),
        compiler_params=params(),
        cost_estimate=cost("coarse_rows"),
        name="coarse_rows",
    )(sent, got)


def far_sum_kernel(own_ref, got_ref, out_ref):
    size = own_ref.shape[0]
    out_ref[...] = (own_ref[...].astype(F32) + got_ref[:size].astype(F32)).astype(BF16)


def far_sum_call(own, got):
    return launch(
        far_sum_kernel,
        out_shape=jax.ShapeDtypeStruct(own.shape, BF16),
        compiler_params=params(),
        cost_estimate=cost("far_sum"),
        name="far_sum",
    )(own, got)


def add_split_kernel(axis, shift, count, where_ref, *refs):
    keeps, gots = refs[:count], refs[count : 2 * count]
    outs = refs[2 * count :]
    parts = len(outs) // 2
    bit = (where_ref[axis] >> shift) & 1
    for refs_out, which in ((outs[:parts], bit), (outs[parts:], 1 - bit)):
        piece = refs_out[0].shape[1]
        for a in range(keeps[0].shape[0]):
            at = 0
            for keep, got in zip(keeps, gots):
                size = min(piece, keep.shape[2])
                for row in range(0, keep.shape[2], size):
                    rows_in = slice(row, row + size)
                    out, first = refs_out[at // piece], at % piece
                    total = keep[a, which, rows_in] + got[a, which, rows_in].astype(F32)
                    out[a, first : first + size] = total.astype(out.dtype)
                    at += size


def add_split_call(name, where, axis, distance, keeps, gots, parts, send_type):
    vmem = pl.BlockSpec(memory_space=pltpu.VMEM)
    total = sum(keep.shape[2] for keep in keeps)
    shape = keeps[0].shape[:1] + (total // parts,) + keeps[0].shape[3:]
    outs = launch(
        functools.partial(add_split_kernel, axis, distance.bit_length() - 1, len(keeps)),
        in_specs=[pl.BlockSpec(memory_space=pltpu.SMEM)] + [vmem] * (2 * len(keeps)),
        out_shape=[jax.ShapeDtypeStruct(shape, F32)] * parts + [jax.ShapeDtypeStruct(shape, send_type)] * parts,
        compiler_params=params(),
        cost_estimate=cost(name),
        name=name,
    )(where, *keeps, *gots)
    return outs[:parts], outs[parts:]


def last_grads_kernel(scale, keep_ref, got_ref, in_ref, out_ref):
    rows_in = in_ref.shape[0]
    in_ref[...] = (keep_ref[:rows_in] + got_ref[:rows_in].astype(F32)) * scale
    out_ref[...] = (keep_ref[rows_in:] + got_ref[rows_in:].astype(F32)) * scale


def last_grads_call(scale, keep, got, rows_in):
    span, width = keep.shape
    return launch(
        lambda *refs: last_grads_kernel(scale, *refs),
        out_shape=[
            jax.ShapeDtypeStruct((rows_in, width), F32),
            jax.ShapeDtypeStruct((span - rows_in, width), F32),
        ],
        compiler_params=params(),
        cost_estimate=cost("last_grads"),
        name="last_grads",
    )(keep, got)


def node_kernel(where_ref, ids_ref, lat_ref, cot_ref, agg_ref, back_ref, *refs):
    pieces, (new_ref, grad_ref, total) = refs[:-3], refs[-3:]
    latent = lat_ref.shape[1]
    for j, piece in enumerate(pieces):
        size = piece.shape[0] // 3
        owner = where_ref[0] ^ j
        place = (owner & 1) * 2 + (owner >> 1) if len(pieces) == 4 else j
        here = pl.ds(pl.multiple_of(place * size, size), size)
        total[here, :latent] = piece[:size].astype(F32)
        total[here, latent : 2 * latent] = piece[size : 2 * size].astype(F32)
        counts = piece[2 * size :].astype(F32)
        total[here, 2 * latent :] = 64.0 * counts[:, :128] + counts[:, 128:256]
    sums = total[...]
    means = sums[:, : 2 * latent] / jnp.maximum(sums[:, 2 * latent : 2 * latent + 1], 1.0)
    places = lax.broadcasted_iota(jnp.int32, (sums.shape[0], ids_ref.shape[1]), 0)
    hot = jnp.where(places == ids_ref[...], 1.0, 0.0).astype(BF16)
    high = means.astype(BF16)
    low = (means - high.astype(F32)).astype(BF16)
    pooled = lax.dot_general(hot, high, ROWS, preferred_element_type=F32)
    pooled = pooled + lax.dot_general(hot, low, ROWS, preferred_element_type=F32)
    new_ref[...] = (lat_ref[...].astype(F32) + agg_ref[...] + pooled[:, :latent]).astype(BF16)
    grad_ref[...] = (cot_ref[...].astype(F32) + back_ref[...] + pooled[:, latent:]).astype(BF16)


def node_call(where, ids, lat, cot, agg, back, pieces):
    vmem = pl.BlockSpec(memory_space=pltpu.VMEM)
    coarse = sum(piece.shape[0] // 3 for piece in pieces)
    width = 2 * lat.shape[1] + 128
    return launch(
        node_kernel,
        in_specs=[pl.BlockSpec(memory_space=pltpu.SMEM)] + [vmem] * (5 + len(pieces)),
        scratch_shapes=[pltpu.VMEM((coarse, width), F32)],
        out_shape=[jax.ShapeDtypeStruct(lat.shape, BF16)] * 2,
        compiler_params=params(),
        cost_estimate=cost("node_outputs"),
        name="node_outputs",
    )(where, ids, lat, cot, agg, back, *pieces)


def node_back_kernel(own_ref, far_ref, near_ref, psum_ref, weight_ref, out_ref):
    latent = own_ref.shape[1]
    total = own_ref[...].astype(F32) + far_ref[...].astype(F32) + near_ref[...].astype(F32)
    back = lax.dot_general(
        total.astype(BF16), weight_ref[latent : 2 * latent], COLS, preferred_element_type=F32
    )
    own = lax.dot_general(psum_ref[...], weight_ref[2 * latent :], COLS, preferred_element_type=F32)
    out_ref[...] = back + own


def node_back_call(own, far, near, psum, weight_in):
    return launch(
        node_back_kernel,
        out_shape=jax.ShapeDtypeStruct(own.shape, F32),
        compiler_params=params(),
        cost_estimate=cost("grad_node"),
        name="grad_node",
    )(own, far, near, psum, weight_in)


def xor_swap(value, axis, distance):
    size = lax.axis_size(axis)
    return lax.ppermute(value, axis, [(i, i ^ distance) for i in range(size)])


def bits_of(size):
    return [1 << b for b in range(size.bit_length() - 1)]


def split(value, dim, bit):
    mine = lax.dynamic_index_in_dim(value, bit, dim, keepdims=False)
    other = lax.dynamic_index_in_dim(value, 1 - bit, dim, keepdims=False)
    return mine, other


def coarse_reduce(sums, other, patch):
    width = sums.shape[1]
    bits = bits_of(lax.axis_size("patch"))
    sums = sums + xor_swap(other, "patch", 1)
    for distance in bits[1:]:
        mine, other = split(sums.reshape(2, -1, width), 0, (patch // distance) % 2)
        sums = mine + xor_swap(other, "patch", distance)
    for distance in bits_of(lax.axis_size("feat")):
        sums = sums + xor_swap(sums, "feat", distance)
    for distance in reversed(bits):
        got = xor_swap(sums, "patch", distance)
        first = (patch // distance) % 2 == 0
        sums = jnp.concatenate([jnp.where(first, sums, got), jnp.where(first, got, sums)], axis=0)
    return sums


def shards(
    node_lat,
    edge_lat,
    neighbours,
    send_rows,
    coarse_of,
    weight_in,
    bias_in,
    weight_out,
    norm_gain,
    edge_cotangent,
    node_cotangent,
):
    Order.token = None
    node_count, latent = node_lat.shape
    degree = edge_lat.shape[1]
    edge_count = node_count * degree
    rim_rows = send_rows.shape[0] // 2
    feat_count = lax.axis_size("feat")
    patch_count = lax.axis_size("patch")
    patch_total = feat_count * node_count
    coarse_total = COARSE_DEV * patch_count * feat_count
    feat = lax.axis_index("feat")
    patch = lax.axis_index("patch")
    block = min(512, edge_count)
    ring_up = [(i, (i + 1) % patch_count) for i in range(patch_count)]
    ring_down = [(j, i) for i, j in ring_up]

    def relative(ids):
        moved = ((ids // node_count) ^ feat) * node_count + ids % node_count
        return jnp.where(ids < patch_total, moved, ids)

    flat_edges = edge_lat.reshape(edge_count, latent)
    flat_cots = edge_cotangent.reshape(edge_count, latent)
    ids = relative(neighbours).T.reshape(edge_count)
    ids_col = ids[:, None]
    ids_row = ids[None, :]
    send_rel = relative(send_rows)
    send_col = send_rel[:, None]
    send_row = send_rel[None, :]
    bias = bias_in[None, :]
    gain = norm_gain[None, :]
    coarse_row = coarse_of[None, :]

    where = jnp.stack([patch, feat]).astype(jnp.int32)
    whole_step = feat_count == 4 and patch_count == 4

    if feat_count == 4:
        far = xor_swap(node_lat, "feat", 2)
        near = xor_swap(node_lat, "feat", 1)
        last = xor_swap(far, "feat", 1)
        pieces = [node_lat, near, far, last]
    else:
        pieces = [node_lat]
        for distance in bits_of(feat_count):
            pieces = pieces + [xor_swap(piece, "feat", distance) for piece in pieces]

    coarse, coarse_other = coarse_sum_call(coarse_row, node_lat, node_cotangent, where, coarse_total)
    if whole_step:
        got = xor_swap(coarse_other, "patch", 1)
        halves = (1, 2, coarse.shape[0] // 2, coarse.shape[1])
        (coarse,), (coarse_other,) = add_split_call(
            "coarse_split", where, 0, 2, [coarse.reshape(halves)], [got.reshape(halves)], 1, F32
        )
        coarse, coarse_other = coarse[0], coarse_other[0]
        got = xor_swap(coarse_other, "patch", 2)
    else:
        coarse = coarse_reduce(coarse, coarse_other, patch)
        got = jnp.zeros_like(coarse)
    base = base_call(
        flat_edges, node_lat, ids_col, weight_in, bias, (ids_row, send_col, send_row, coarse_row), pieces[:-1], block
    )
    to_lower, to_upper = select_call(send_col, pieces)
    from_lower = lax.ppermute(to_upper, "patch", ring_up)
    from_upper = lax.ppermute(to_lower, "patch", ring_down)
    coarse = add_pair_call(coarse, got)
    got = xor_swap(coarse, "feat", 2) if whole_step else jnp.zeros_like(coarse)

    edge_new, aggregate, hidden_act, grad_proj, grad_pre, pre_sum, grad_edge = edge_call(
        base,
        ids_col,
        pieces[-1],
        from_lower,
        from_upper,
        flat_edges,
        flat_cots,
        node_cotangent,
        weight_in,
        weight_out,
        gain,
        patch_total - node_count,
        block)

    rim_low, rim_high, coarse = rim_sum_call(ids_row, grad_pre, coarse, got, patch_total, 2 * rim_rows)
    back_upper = lax.ppermute(rim_low, "patch", ring_down)
    back_lower = lax.ppermute(rim_high, "patch", ring_up)
    patch_sum = patch_sum_call(ids_row, grad_pre, patch_total, node_count)
    span, width = 4 * latent // patch_count, latent // feat_count
    steps = [("patch", d) for d in bits_of(patch_count)[1:]] + [("feat", d) for d in bits_of(feat_count)]

    def fold(name, step, keeps, gots, parts):
        axis, distance = steps[step]
        shape = lambda x: (-1, 2) + x.shape[-2:]
        keeps, sends = add_split_call(
            name,
            where,
            int(axis == "feat"),
            distance,
            [x.reshape(shape(x)) for x in keeps],
            [x.reshape(shape(x)) for x in gots],
            parts,
            BF16,
        )
        return keeps, [xor_swap(x, axis, distance) for x in sends]

    def fold_half(name, keep, got):
        for step in range(1, len(steps) - 1):
            (keep,), (got,) = fold(name, step, [keep], [got], 1)
        return keep, got

    sums = add_rim_call(
        send_row, back_lower, back_upper, patch_sum, coarse, node_count, whole_step
    )
    edge_grad, out_grad = edge_grads_call(flat_edges, grad_pre, hidden_act, grad_proj)
    tables = pieces + [from_lower, from_upper]
    keep, send = pack_call(
        where, pre_sum, edge_grad, out_grad, patch_sum, rim_low, rim_high, tables, feat_count, patch_count
    )
    got_core = xor_swap(send, "patch", 1)
    if feat_count == 4:
        relay = xor_swap(sums[3], "feat", 1)
        far_sum = far_sum_call(sums[2], relay)
        got_far = xor_swap(far_sum, "feat", 2)
        got_near = xor_swap(sums[1], "feat", 1)
        own = [sums[0], got_far, got_near]
    else:
        parts = sums
        for distance in reversed(bits_of(feat_count)):
            arrived = [xor_swap(part, "feat", distance) for part in parts[distance:]]
            parts = [add_pair_call(a, b) for a, b in zip(parts[:distance], arrived)]
        own = [parts[0], jnp.zeros_like(parts[0]), jnp.zeros_like(parts[0])]
    (keep_a, keep_b), (got_a, got_b) = fold("fold0", 0, [keep], [got_core], 2)
    keep_a, got_a = fold_half("fold1", keep_a, got_a)
    keep_b, got_b = fold_half("fold3", keep_b, got_b)
    if whole_step:
        coarse_all = coarse_rows_call(sums[3], relay, 3 * coarse.shape[0])
        parts = [coarse_all] + [xor_swap(coarse_all, "patch", j) for j in range(1, 4)]
    else:
        counts = jnp.pad(coarse[:, 2 * latent :], ((0, 0), (128, latent - 256)))
        parts = [jnp.concatenate([coarse[:, :latent], coarse[:, latent : 2 * latent], counts], axis=0)]
    back = node_back_call(*own, pre_sum, weight_in)
    (keep,), (received,) = fold("fold2", len(steps) - 1, [keep_a, keep_b], [got_a, got_b], 1)
    node_new, grad_node = node_call(
        where, coarse_row, node_lat, node_cotangent, aggregate, back, parts
    )
    scale = 1.0 / math.sqrt(edge_count * patch_count * feat_count)
    in_rows = 3 * latent // patch_count
    grads_in, grads_out = last_grads_call(scale, keep.reshape(span, width), received.reshape(span, width), in_rows)
    return (
        edge_new.reshape(edge_lat.shape),
        node_new,
        grad_edge.reshape(edge_lat.shape),
        grad_node,
        grads_in,
        grads_out,
    )


def solution(mesh):
    return jax.shard_map(
        shards,
        mesh=mesh,
        in_specs=(
            P(("groups", "patch", "feat"), None),
            P(("groups", "patch", "feat"), None, None),
            P(None, ("patch", "feat")),
            P("patch"),
            P(("patch", "feat")),
            P(),
            P(),
            P(),
            P(),
            P(("groups", "patch", "feat"), None, None),
            P(("groups", "patch", "feat"), None),
        ),
        out_specs=(
            P(("groups", "patch", "feat"), None, None),
            P(("groups", "patch", "feat"), None),
            P(("groups", "patch", "feat"), None, None),
            P(("groups", "patch", "feat"), None),
            P(("groups", "patch"), "feat"),
            P(("groups", "patch"), "feat"),
        ),
        check_vma=False,
    )
```

```python
import functools
import math

import jax
import jax.numpy as jnp
from jax import lax
from jax.experimental import pallas as pl
from jax.experimental.pallas import tpu as pltpu
from jax.sharding import PartitionSpec as P

COARSE_DEV = 4
LAYER_EPS = 1e-05
F32 = jnp.float32
BF16 = jnp.bfloat16
VMEM_LIMIT = 24 * 1024 * 1024
EDGE_LIMIT = 24 * 1024 * 1024
COLS = (((1,), (1,)), ((), ()))
ROWS = (((0,), (0,)), ((), ()))


def dot(a, b):
    return jnp.dot(a, b, preferred_element_type=F32)


def params(limit=None):
    return pltpu.CompilerParams(vmem_limit_bytes=limit or VMEM_LIMIT)


COST = {
    "base_terms": 15,
    "select_rows": 2,
    "add_pair": 1,
    "edge_block": 36,
    "rim_sums": 2.4,
    "patch_sums": 0.3,
    "edge_grads": 0.3,
    "add_rim_sums": 0.3,
    "pack_grads": 0.3,
    "coarse_rows": 0.3,
    "far_sum": 30,
    "node_outputs": 2,
    "grad_node": .1,
    "last_grads": 1.5,
    "coarse_sums": 1,
    "coarse_split": 1,
    "fold0": 0.3,
    "fold1": 0.3,
    "fold3": 0.3,
    "fold2": 0.3,
}


def cost(name):
    micros = COST[name]
    return pl.CostEstimate(flops=int(micros * 1.15e9), bytes_accessed=1 << 20, transcendentals=0)


class Order:
    token = None


def launch(kernel, out_shape, in_specs=None, out_specs=None, grid=None, **settings):
    outs = list(out_shape) if isinstance(out_shape, (list, tuple)) else [out_shape]
    mark = jax.ShapeDtypeStruct((8, 128), F32)

    def call(*args):
        count = len(args)
        late = [] if Order.token is None else [Order.token]
        vmem = pl.BlockSpec(memory_space=pltpu.VMEM)
        specs = list(in_specs or [vmem] * count) + [pl.BlockSpec(memory_space=pl.ANY)] * len(late)
        end = count + len(late) + len(outs)

        def body(*refs):
            refs[end][...] = jnp.zeros((8, 128), F32)
            kernel(*refs[:count], *refs[count + len(late) : end], *refs[end + 1 :])

        if grid is None:
            places, more = [vmem] * (len(outs) + 1), {}
        else:
            places = list(out_specs) if isinstance(out_specs, (list, tuple)) else [out_specs]
            places, more = places + [pl.BlockSpec((8, 128), lambda i: (0, 0))], {"grid": grid}
        results = pl.pallas_call(
            body, out_shape=outs + [mark], in_specs=specs, out_specs=places, **more, **settings
        )(*args, *late)
        Order.token = results[-1]
        return results[:-1] if isinstance(out_shape, (list, tuple)) else results[0]

    return call


def streamed(array):
    return pltpu.with_memory_space_constraint(array, pltpu.HBM)


def held(array):
    return pltpu.with_memory_space_constraint(array, pltpu.VMEM)


def whole(array):
    zeros = (0,) * array.ndim
    return pl.BlockSpec(array.shape, lambda i: zeros)


def rows(array, block):
    rest = (0,) * (array.ndim - 1)
    return pl.BlockSpec((block,) + array.shape[1:], lambda i: (i,) + rest)


def one_hot(ids, first, count):
    lanes = lax.broadcasted_iota(jnp.int32, (ids.shape[0], count), 1) + first
    return jnp.where(ids == lanes, 1.0, 0.0).astype(BF16)


def fill_table(table, pieces, weight_ref):
    latent = pieces[0].shape[1]
    at = 0
    for piece in pieces:
        size = piece.shape[0]
        table[at : at + size] = dot(piece[...], weight_ref[latent : 2 * latent]).astype(BF16)
        at += size


def base_kernel(degree, edge_ref, node_ref, ids_ref, weight_ref, bias_ref, *refs):
    pieces, (out_ref, table) = refs[:-2], refs[-2:]
    latent = edge_ref.shape[1]

    @pl.when(pl.program_id(0) == 0)
    def _():
        fill_table(table, pieces, weight_ref)

    edges = edge_ref.shape[0]
    term = dot(node_ref[...], weight_ref[2 * latent :]) + bias_ref[...]
    total = dot(edge_ref[...], weight_ref[:latent])
    total = total + dot(one_hot(ids_ref[...], 0, table.shape[0]), table[...])
    hidden = total.shape[1]
    total = total.reshape(edges // degree, degree, hidden) + term[:, None, :]
    out_ref[...] = total.reshape(edges, hidden)


def base_call(edges, nodes, ids, weight_in, bias, early, pieces, block):
    count, latent = edges.shape
    hidden = weight_in.shape[1]
    degree = count // nodes.shape[0]
    size = sum(piece.shape[0] for piece in pieces)
    return launch(
        lambda *refs: base_kernel(degree, *refs[:5], *refs[5 + len(early) :]),
        grid=(count // block,),
        in_specs=[
            rows(edges, block),
            rows(nodes, block // degree),
            rows(ids, block),
            whole(weight_in),
            whole(bias),
        ]
        + [pl.BlockSpec(memory_space=pl.ANY)] * len(early)
        + [whole(piece) for piece in pieces],
        out_specs=pl.BlockSpec((block, hidden), lambda i: (i, 0)),
        out_shape=jax.ShapeDtypeStruct((count, hidden), F32),
        scratch_shapes=[pltpu.VMEM((size, hidden), BF16)],
        compiler_params=params(),
        cost_estimate=cost("base_terms"),
        name="base_terms",
    )(streamed(edges), nodes, ids, weight_in, bias, *early, *pieces)


def edge_kernel(
    first,
    degree,
    base_ref,
    ids_ref,
    last_ref,
    low_ref,
    high_ref,
    edge_ref,
    cot_ref,
    ncot_ref,
    weight_ref,
    out_w_ref,
    gain_ref,
    new_ref,
    agg_ref,
    hid_ref,
    gproj_ref,
    gpre_ref,
    psum_ref,
    gedge_ref,
    table,
):
    latent = low_ref.shape[1]

    @pl.when(pl.program_id(0) == 0)
    def _():
        fill_table(table, (last_ref, low_ref, high_ref), weight_ref)

    ids = ids_ref[...]
    edges = ids.shape[0]
    nodes = edges // degree
    limit = first + table.shape[0]
    live = jnp.where(ids < limit, 1.0, 0.0)
    value = base_ref[...] + dot(one_hot(ids, first, table.shape[0]), table[...])
    sig = 0.5 + 0.5 * jnp.tanh(0.5 * value)
    act = value * sig
    slope = sig + act * (1.0 - sig)
    hid = act.astype(BF16)
    hid_ref[...] = hid
    projected = dot(hid, out_w_ref[...])
    centre = projected - jnp.mean(projected, axis=1, keepdims=True)
    inverse = lax.rsqrt(jnp.mean(centre * centre, axis=1, keepdims=True) + LAYER_EPS)
    normed = centre * inverse
    gain = gain_ref[...]
    message = normed * gain
    new_ref[...] = (edge_ref[...].astype(F32) + message).astype(BF16)
    pick = lax.broadcasted_iota(jnp.int32, (nodes, edges), 1) // degree
    pick = jnp.where(pick == lax.broadcasted_iota(jnp.int32, (nodes, edges), 0), 1.0, 0.0).astype(BF16)
    agg_ref[...] = dot(pick, (message * live).astype(BF16))
    ncot = jnp.broadcast_to(ncot_ref[...].astype(F32)[:, None, :], (nodes, degree, latent))
    cot = cot_ref[...].astype(F32)
    scaled = (cot + live * ncot.reshape(edges, latent)) * gain
    mean_a = jnp.mean(scaled, axis=1, keepdims=True)
    mean_b = jnp.mean(scaled * normed, axis=1, keepdims=True)
    gproj = (inverse * (scaled - mean_a - normed * mean_b)).astype(BF16)
    gproj_ref[...] = gproj
    gpre = (lax.dot_general(gproj, out_w_ref[...], COLS, preferred_element_type=F32) * slope).astype(BF16)
    gpre_ref[...] = gpre
    psum_ref[...] = dot(pick, gpre).astype(BF16)
    back = lax.dot_general(gpre, weight_ref[:latent], COLS, preferred_element_type=F32)
    gedge_ref[...] = (cot + back).astype(BF16)


def edge_call(base, ids, last, low, high, edges, cots, ncot, weight_in, weight_out, gain, first, block):
    count, latent = edges.shape
    hidden = weight_in.shape[1]
    degree = count // ncot.shape[0]
    blocks = count // block
    small = block // degree

    def like(width, dtype, size, total):
        return (
            pl.BlockSpec((size, width), lambda i: (i, 0)),
            jax.ShapeDtypeStruct((total, width), dtype),
        )

    outs = [
        like(latent, BF16, block, count),
        like(latent, F32, small, count // degree),
        like(hidden, BF16, block, count),
        like(latent, BF16, block, count),
        like(hidden, BF16, block, count),
        like(hidden, BF16, small, count // degree),
        like(latent, BF16, block, count),
    ]
    return launch(
        lambda *refs: edge_kernel(first, degree, *refs),
        grid=(blocks,),
        in_specs=[
            rows(base, block),
            rows(ids, block),
            whole(last),
            whole(low),
            whole(high),
            rows(edges, block),
            rows(cots, block),
            rows(ncot, small),
            whole(weight_in),
            whole(weight_out),
            whole(gain),
        ],
        out_specs=[spec for spec, _ in outs],
        out_shape=[shape for _, shape in outs],
        scratch_shapes=[pltpu.VMEM((last.shape[0] + 2 * low.shape[0], hidden), BF16)],
        compiler_params=params(EDGE_LIMIT),
        cost_estimate=cost("edge_block"),
        name="edge_block",
    )(base, ids, last, low, high, streamed(edges), streamed(cots), ncot, weight_in, weight_out, gain)


def select_kernel(ids_ref, *refs):
    pieces, (low_ref, high_ref) = refs[:-2], refs[-2:]
    total, at = None, 0
    for piece in pieces:
        term = dot(one_hot(ids_ref[...], at, piece.shape[0]), piece[...])
        total = term if total is None else total + term
        at += piece.shape[0]
    half = low_ref.shape[0]
    low_ref[...] = total[:half].astype(BF16)
    high_ref[...] = total[half:].astype(BF16)


def select_call(ids, pieces):
    count, width = ids.shape[0], pieces[0].shape[1]
    half = jax.ShapeDtypeStruct((count // 2, width), BF16)
    return launch(
        select_kernel,
        out_shape=[half, half],
        compiler_params=params(),
        cost_estimate=cost("select_rows"),
        name="select_rows",
    )(ids, *pieces)


def rim_sum_kernel(first, ids_ref, values_ref, mine_ref, got_ref, low_ref, high_ref, sum_ref):
    sum_ref[...] = mine_ref[...] + got_ref[...]
    half = low_ref.shape[0]
    places = lax.broadcasted_iota(jnp.int32, (2 * half, ids_ref.shape[1]), 0) + first
    hot = jnp.where(places == ids_ref[...], 1.0, 0.0).astype(BF16)
    total = dot(hot, values_ref[...])
    low_ref[...] = total[:half].astype(BF16)
    high_ref[...] = total[half:].astype(BF16)


def rim_sum_call(ids, values, mine, got, first, count):
    half = jax.ShapeDtypeStruct((count // 2, values.shape[1]), BF16)
    return launch(
        lambda *refs: rim_sum_kernel(first, *refs),
        out_shape=[half, half, jax.ShapeDtypeStruct(mine.shape, F32)],
        compiler_params=params(),
        cost_estimate=cost("rim_sums"),
        name="rim_sums",
    )(ids, values, mine, got)


def patch_sum_kernel(ids_ref, values_ref, out_ref):
    size = out_ref.shape[0]
    places = lax.broadcasted_iota(jnp.int32, (size, ids_ref.shape[1]), 0) + pl.program_id(0) * size
    hot = jnp.where(places == ids_ref[...], 1.0, 0.0).astype(BF16)
    out_ref[...] = dot(hot, values_ref[...])


def patch_sum_call(ids, values, count, block):
    width = values.shape[1]
    return launch(
        patch_sum_kernel,
        grid=(count // block,),
        in_specs=[whole(ids), whole(values)],
        out_specs=pl.BlockSpec((block, width), lambda i: (i, 0)),
        out_shape=jax.ShapeDtypeStruct((count, width), F32),
        compiler_params=params(),
        cost_estimate=cost("patch_sums"),
        name="patch_sums",
    )(ids, values)


def add_rim_kernel(ids_ref, low_ref, high_ref, start_ref, coarse_ref, *outs):
    half = low_ref.shape[0]
    size = outs[0].shape[0]
    latent = start_ref.shape[1]
    coarse = coarse_ref[...]
    few = coarse.shape[0]
    counts = coarse[:, 2 * latent :]
    high = jnp.floor(counts * (1.0 / 64.0))
    for j, out in enumerate(outs):
        places = lax.broadcasted_iota(jnp.int32, (size, 2 * half), 0) + j * size
        hot = jnp.where(places == ids_ref[...], 1.0, 0.0).astype(BF16)
        total = start_ref[j * size : (j + 1) * size] + dot(hot[:, :half], low_ref[...])
        total = total + dot(hot[:, half:], high_ref[...])
        out[:size] = total.astype(BF16)
        if out.shape[0] > size:
            out[size : size + few] = coarse[:, :latent].astype(BF16)
            out[size + few : size + 2 * few] = coarse[:, latent : 2 * latent].astype(BF16)
            out[size + 2 * few :] = jnp.zeros((few, latent), BF16)
            out[size + 2 * few :, :128] = high.astype(BF16)
            out[size + 2 * few :, 128:256] = (counts - 64.0 * high).astype(BF16)


def add_rim_call(ids, low, high, start, coarse, size, extended):
    count, width = start.shape
    pieces = count // size
    extra = [3 * coarse.shape[0] if extended and j == pieces - 1 else 0 for j in range(pieces)]
    return launch(
        add_rim_kernel,
        out_shape=[jax.ShapeDtypeStruct((size + more, width), BF16) for more in extra],
        compiler_params=params(),
        cost_estimate=cost("add_rim_sums"),
        name="add_rim_sums",
    )(ids, low, high, start, coarse)


def edge_grads_kernel(edge_ref, gpre_ref, hid_ref, gproj_ref, in_ref, out_ref):
    in_ref[...] = lax.dot_general(edge_ref[...], gpre_ref[...], ROWS, preferred_element_type=F32)
    out_ref[...] = lax.dot_general(hid_ref[...], gproj_ref[...], ROWS, preferred_element_type=F32)


def edge_grads_call(edges, gpre, hid, gproj):
    latent, hidden = edges.shape[1], gpre.shape[1]
    return launch(
        edge_grads_kernel,
        out_shape=[
            jax.ShapeDtypeStruct((latent, hidden), F32),
            jax.ShapeDtypeStruct((hidden, latent), F32),
        ],
        compiler_params=params(),
        cost_estimate=cost("edge_grads"),
        name="edge_grads",
    )(edges, gpre, hid, gproj)


def pack_kernel(pieces, where_ref, psum_ref, edge_ref, out_ref, patch_ref, low_ref, high_ref, *refs):
    tables = refs[:pieces]
    keep_ref, send_ref, total = refs[pieces:]
    latent = tables[0].shape[1]
    size = tables[0].shape[0]
    parts = [patch_ref[j * size : (j + 1) * size].astype(BF16) for j in range(pieces - 2)]
    grad = None
    for table, part in zip(tables, parts + [low_ref[...], high_ref[...]]):
        term = lax.dot_general(table[...], part, ROWS, preferred_element_type=F32)
        grad = term if grad is None else grad + term
    total[:latent] = grad
    total[latent:] = lax.dot_general(tables[0][...], psum_ref[...], ROWS, preferred_element_type=F32)
    feats, pairs, span, width = keep_ref.shape
    unit = span // 4

    def block(patch, slot):
        row = (patch * 3 + slot) * unit if slot < 3 else 3 * latent + patch * unit
        for ref, start, end in ((edge_ref, 0, latent), (total, latent, 3 * latent), (out_ref, 3 * latent, 4 * latent)):
            if start <= row < end:
                return ref[row - start : row - start + unit]

    for bit in range(2):

        @pl.when((where_ref[0] & 1) == bit)
        def _():
            for m in range(pairs):
                for slot in range(4):
                    for ref, which in ((keep_ref, bit), (send_ref, 1 - bit)):
                        rows_in = block(2 * m + which, slot)
                        for f in range(feats):
                            ref[f, m, slot * unit : (slot + 1) * unit, :] = rows_in[
                                :, f * width : (f + 1) * width
                            ].astype(ref.dtype)


def pack_call(where, psum, edge_grad, out_grad, patch_sum, low, high, tables, feats, patches):
    latent, hidden = edge_grad.shape
    shape = (feats, patches // 2, 4 * latent // patches, hidden // feats)
    vmem = pl.BlockSpec(memory_space=pltpu.VMEM)
    return launch(
        lambda *refs: pack_kernel(len(tables), *refs),
        in_specs=[pl.BlockSpec(memory_space=pltpu.SMEM)] + [vmem] * (6 + len(tables)),
        out_shape=[jax.ShapeDtypeStruct(shape, F32), jax.ShapeDtypeStruct(shape, BF16)],
        scratch_shapes=[pltpu.VMEM((2 * latent, hidden), F32)],
        compiler_params=params(),
        cost_estimate=cost("pack_grads"),
        name="pack_grads",
    )(where, psum, edge_grad, out_grad, patch_sum, low, high, *tables)


def coarse_sum_kernel(ids_ref, lat_ref, cot_ref, where_ref, mine_ref, other_ref):
    latent = lat_ref.shape[1]
    half = mine_ref.shape[0]
    core = where_ref[0] & 1
    for ref, bit in ((mine_ref, core), (other_ref, 1 - core)):
        places = lax.broadcasted_iota(jnp.int32, (half, ids_ref.shape[1]), 0) + bit * half
        live = jnp.where(places == ids_ref[...], 1.0, 0.0)
        hot = live.astype(BF16)
        ref[:, :latent] = dot(hot, lat_ref[...])
        ref[:, latent : 2 * latent] = dot(hot, cot_ref[...])
        ref[:, 2 * latent :] = jnp.broadcast_to(jnp.sum(live, axis=1, keepdims=True), (half, 128))


def coarse_sum_call(ids, lat, cot, where, coarse):
    vmem = pl.BlockSpec(memory_space=pltpu.VMEM)
    half = jax.ShapeDtypeStruct((coarse // 2, 2 * lat.shape[1] + 128), F32)
    return launch(
        coarse_sum_kernel,
        in_specs=[vmem, vmem, vmem, pl.BlockSpec(memory_space=pltpu.SMEM)],
        out_shape=[half, half],
        compiler_params=params(),
        cost_estimate=cost("coarse_sums"),
        name="coarse_sums",
    )(ids, lat, cot, where)


def add_pair_kernel(a_ref, b_ref, out_ref):
    out_ref[...] = (a_ref[...].astype(F32) + b_ref[...].astype(F32)).astype(out_ref.dtype)


def add_pair_call(a, b):
    return launch(
        add_pair_kernel,
        out_shape=jax.ShapeDtypeStruct(a.shape, a.dtype),
        compiler_params=params(),
        cost_estimate=cost("add_pair"),
        name="add_pair",
    )(a, b)


def coarse_rows_kernel(sent_ref, got_ref, out_ref):
    few = out_ref.shape[0]
    out_ref[...] = (sent_ref[-few:].astype(F32) + got_ref[-few:].astype(F32)).astype(BF16)


def coarse_rows_call(sent, got, few):
    return launch(
        coarse_rows_kernel,
        out_shape=jax.ShapeDtypeStruct((few, sent.shape[1]), BF16),
        compiler_params=params(),
        cost_estimate=cost("coarse_rows"),
        name="coarse_rows",
    )(sent, got)


def far_sum_kernel(own_ref, got_ref, out_ref):
    size = own_ref.shape[0]
    out_ref[...] = (own_ref[...].astype(F32) + got_ref[:size].astype(F32)).astype(BF16)


def far_sum_call(own, got):
    return launch(
        far_sum_kernel,
        out_shape=jax.ShapeDtypeStruct(own.shape, BF16),
        compiler_params=params(),
        cost_estimate=cost("far_sum"),
        name="far_sum",
    )(own, got)


def add_split_kernel(axis, shift, count, where_ref, *refs):
    keeps, gots = refs[:count], refs[count : 2 * count]
    outs = refs[2 * count :]
    parts = len(outs) // 2
    bit = (where_ref[axis] >> shift) & 1
    for refs_out, which in ((outs[:parts], bit), (outs[parts:], 1 - bit)):
        piece = refs_out[0].shape[1]
        for a in range(keeps[0].shape[0]):
            at = 0
            for keep, got in zip(keeps, gots):
                size = min(piece, keep.shape[2])
                for row in range(0, keep.shape[2], size):
                    rows_in = slice(row, row + size)
                    out, first = refs_out[at // piece], at % piece
                    total = keep[a, which, rows_in] + got[a, which, rows_in].astype(F32)
                    out[a, first : first + size] = total.astype(out.dtype)
                    at += size


def add_split_call(name, where, axis, distance, keeps, gots, parts, send_type):
    vmem = pl.BlockSpec(memory_space=pltpu.VMEM)
    total = sum(keep.shape[2] for keep in keeps)
    shape = keeps[0].shape[:1] + (total // parts,) + keeps[0].shape[3:]
    outs = launch(
        functools.partial(add_split_kernel, axis, distance.bit_length() - 1, len(keeps)),
        in_specs=[pl.BlockSpec(memory_space=pltpu.SMEM)] + [vmem] * (2 * len(keeps)),
        out_shape=[jax.ShapeDtypeStruct(shape, F32)] * parts + [jax.ShapeDtypeStruct(shape, send_type)] * parts,
        compiler_params=params(),
        cost_estimate=cost(name),
        name=name,
    )(where, *keeps, *gots)
    return outs[:parts], outs[parts:]


def last_grads_kernel(scale, keep_ref, got_ref, in_ref, out_ref):
    rows_in = in_ref.shape[0]
    in_ref[...] = (keep_ref[:rows_in] + got_ref[:rows_in].astype(F32)) * scale
    out_ref[...] = (keep_ref[rows_in:] + got_ref[rows_in:].astype(F32)) * scale


def last_grads_call(scale, keep, got, rows_in):
    span, width = keep.shape
    return launch(
        lambda *refs: last_grads_kernel(scale, *refs),
        out_shape=[
            jax.ShapeDtypeStruct((rows_in, width), F32),
            jax.ShapeDtypeStruct((span - rows_in, width), F32),
        ],
        compiler_params=params(),
        cost_estimate=cost("last_grads"),
        name="last_grads",
    )(keep, got)


def node_kernel(where_ref, ids_ref, lat_ref, cot_ref, agg_ref, back_ref, *refs):
    pieces, (new_ref, grad_ref, total) = refs[:-3], refs[-3:]
    latent = lat_ref.shape[1]
    for j, piece in enumerate(pieces):
        size = piece.shape[0] // 3
        owner = where_ref[0] ^ j
        place = (owner & 1) * 2 + (owner >> 1) if len(pieces) == 4 else j
        here = pl.ds(pl.multiple_of(place * size, size), size)
        total[here, :latent] = piece[:size].astype(F32)
        total[here, latent : 2 * latent] = piece[size : 2 * size].astype(F32)
        counts = piece[2 * size :].astype(F32)
        total[here, 2 * latent :] = 64.0 * counts[:, :128] + counts[:, 128:256]
    sums = total[...]
    means = sums[:, : 2 * latent] / jnp.maximum(sums[:, 2 * latent : 2 * latent + 1], 1.0)
    places = lax.broadcasted_iota(jnp.int32, (sums.shape[0], ids_ref.shape[1]), 0)
    hot = jnp.where(places == ids_ref[...], 1.0, 0.0).astype(BF16)
    high = means.astype(BF16)
    low = (means - high.astype(F32)).astype(BF16)
    pooled = lax.dot_general(hot, high, ROWS, preferred_element_type=F32)
    pooled = pooled + lax.dot_general(hot, low, ROWS, preferred_element_type=F32)
    new_ref[...] = (lat_ref[...].astype(F32) + agg_ref[...] + pooled[:, :latent]).astype(BF16)
    grad_ref[...] = (cot_ref[...].astype(F32) + back_ref[...] + pooled[:, latent:]).astype(BF16)


def node_call(where, ids, lat, cot, agg, back, pieces):
    vmem = pl.BlockSpec(memory_space=pltpu.VMEM)
    coarse = sum(piece.shape[0] // 3 for piece in pieces)
    width = 2 * lat.shape[1] + 128
    return launch(
        node_kernel,
        in_specs=[pl.BlockSpec(memory_space=pltpu.SMEM)] + [vmem] * (5 + len(pieces)),
        scratch_shapes=[pltpu.VMEM((coarse, width), F32)],
        out_shape=[jax.ShapeDtypeStruct(lat.shape, BF16)] * 2,
        compiler_params=params(),
        cost_estimate=cost("node_outputs"),
        name="node_outputs",
    )(where, ids, lat, cot, agg, back, *pieces)


def node_back_kernel(own_ref, far_ref, near_ref, psum_ref, weight_ref, out_ref):
    latent = own_ref.shape[1]
    total = own_ref[...].astype(F32) + far_ref[...].astype(F32) + near_ref[...].astype(F32)
    back = lax.dot_general(
        total.astype(BF16), weight_ref[latent : 2 * latent], COLS, preferred_element_type=F32
    )
    own = lax.dot_general(psum_ref[...], weight_ref[2 * latent :], COLS, preferred_element_type=F32)
    out_ref[...] = back + own


def node_back_call(own, far, near, psum, weight_in):
    return launch(
        node_back_kernel,
        out_shape=jax.ShapeDtypeStruct(own.shape, F32),
        compiler_params=params(),
        cost_estimate=cost("grad_node"),
        name="grad_node",
    )(own, far, near, psum, weight_in)


def xor_swap(value, axis, distance):
    size = lax.axis_size(axis)
    return lax.ppermute(value, axis, [(i, i ^ distance) for i in range(size)])


def bits_of(size):
    return [1 << b for b in range(size.bit_length() - 1)]


def split(value, dim, bit):
    mine = lax.dynamic_index_in_dim(value, bit, dim, keepdims=False)
    other = lax.dynamic_index_in_dim(value, 1 - bit, dim, keepdims=False)
    return mine, other


def coarse_reduce(sums, other, patch):
    width = sums.shape[1]
    bits = bits_of(lax.axis_size("patch"))
    sums = sums + xor_swap(other, "patch", 1)
    for distance in bits[1:]:
        mine, other = split(sums.reshape(2, -1, width), 0, (patch // distance) % 2)
        sums = mine + xor_swap(other, "patch", distance)
    for distance in bits_of(lax.axis_size("feat")):
        sums = sums + xor_swap(sums, "feat", distance)
    for distance in reversed(bits):
        got = xor_swap(sums, "patch", distance)
        first = (patch // distance) % 2 == 0
        sums = jnp.concatenate([jnp.where(first, sums, got), jnp.where(first, got, sums)], axis=0)
    return sums


def shards(
    node_lat,
    edge_lat,
    neighbours,
    send_rows,
    coarse_of,
    weight_in,
    bias_in,
    weight_out,
    norm_gain,
    edge_cotangent,
    node_cotangent,
):
    Order.token = None
    node_count, latent = node_lat.shape
    degree = edge_lat.shape[1]
    edge_count = node_count * degree
    rim_rows = send_rows.shape[0] // 2
    feat_count = lax.axis_size("feat")
    patch_count = lax.axis_size("patch")
    patch_total = feat_count * node_count
    coarse_total = COARSE_DEV * patch_count * feat_count
    feat = lax.axis_index("feat")
    patch = lax.axis_index("patch")
    block = min(512, edge_count)
    ring_up = [(i, (i + 1) % patch_count) for i in range(patch_count)]
    ring_down = [(j, i) for i, j in ring_up]

    def relative(ids):
        moved = ((ids // node_count) ^ feat) * node_count + ids % node_count
        return jnp.where(ids < patch_total, moved, ids)

    flat_edges = edge_lat.reshape(edge_count, latent)
    flat_cots = edge_cotangent.reshape(edge_count, latent)
    ids = relative(neighbours).T.reshape(edge_count)
    ids_col = ids[:, None]
    ids_row = ids[None, :]
    send_rel = relative(send_rows)
    send_col = send_rel[:, None]
    send_row = send_rel[None, :]
    bias = bias_in[None, :]
    gain = norm_gain[None, :]
    coarse_row = coarse_of[None, :]

    where = jnp.stack([patch, feat]).astype(jnp.int32)
    whole_step = feat_count == 4 and patch_count == 4

    if feat_count == 4:
        far = xor_swap(node_lat, "feat", 2)
        near = xor_swap(node_lat, "feat", 1)
        last = xor_swap(far, "feat", 1)
        pieces = [node_lat, near, far, last]
    else:
        pieces = [node_lat]
        for distance in bits_of(feat_count):
            pieces = pieces + [xor_swap(piece, "feat", distance) for piece in pieces]

    coarse, coarse_other = coarse_sum_call(coarse_row, node_lat, node_cotangent, where, coarse_total)
    if whole_step:
        got = xor_swap(coarse_other, "patch", 1)
        halves = (1, 2, coarse.shape[0] // 2, coarse.shape[1])
        (coarse,), (coarse_other,) = add_split_call(
            "coarse_split", where, 0, 2, [coarse.reshape(halves)], [got.reshape(halves)], 1, F32
        )
        coarse, coarse_other = coarse[0], coarse_other[0]
        got = xor_swap(coarse_other, "patch", 2)
    else:
        coarse = coarse_reduce(coarse, coarse_other, patch)
        got = jnp.zeros_like(coarse)
    base = base_call(
        flat_edges, node_lat, ids_col, weight_in, bias, (ids_row, send_col, send_row, coarse_row), pieces[:-1], block
    )
    to_lower, to_upper = select_call(send_col, pieces)
    from_lower = lax.ppermute(to_upper, "patch", ring_up)
    from_upper = lax.ppermute(to_lower, "patch", ring_down)
    coarse = add_pair_call(coarse, got)
    got = xor_swap(coarse, "feat", 2) if whole_step else jnp.zeros_like(coarse)

    edge_new, aggregate, hidden_act, grad_proj, grad_pre, pre_sum, grad_edge = edge_call(
        base,
        ids_col,
        pieces[-1],
        from_lower,
        from_upper,
        flat_edges,
        flat_cots,
        node_cotangent,
        weight_in,
        weight_out,
        gain,
        patch_total - node_count,
        block)

    rim_low, rim_high, coarse = rim_sum_call(ids_row, grad_pre, coarse, got, patch_total, 2 * rim_rows)
    back_upper = lax.ppermute(rim_low, "patch", ring_down)
    back_lower = lax.ppermute(rim_high, "patch", ring_up)
    patch_sum = patch_sum_call(ids_row, grad_pre, patch_total, 2 * node_count)
    span, width = 4 * latent // patch_count, latent // feat_count
    steps = [("patch", d) for d in bits_of(patch_count)[1:]] + [("feat", d) for d in bits_of(feat_count)]

    def fold(name, step, keeps, gots, parts):
        axis, distance = steps[step]
        shape = lambda x: (-1, 2) + x.shape[-2:]
        keeps, sends = add_split_call(
            name,
            where,
            int(axis == "feat"),
            distance,
            [x.reshape(shape(x)) for x in keeps],
            [x.reshape(shape(x)) for x in gots],
            parts,
            BF16,
        )
        return keeps, [xor_swap(x, axis, distance) for x in sends]

    def fold_half(name, keep, got):
        for step in range(1, len(steps) - 1):
            (keep,), (got,) = fold(name, step, [keep], [got], 1)
        return keep, got

    sums = add_rim_call(
        send_row, back_lower, back_upper, patch_sum, coarse, node_count, whole_step
    )
    edge_grad, out_grad = edge_grads_call(flat_edges, grad_pre, hidden_act, grad_proj)
    tables = pieces + [from_lower, from_upper]
    keep, send = pack_call(
        where, pre_sum, edge_grad, out_grad, patch_sum, rim_low, rim_high, tables, feat_count, patch_count
    )
    got_core = xor_swap(send, "patch", 1)
    if feat_count == 4:
        relay = xor_swap(sums[3], "feat", 1)
        far_sum = far_sum_call(sums[2], relay)
        got_far = xor_swap(far_sum, "feat", 2)
        got_near = xor_swap(sums[1], "feat", 1)
        own = [sums[0], got_far, got_near]
    else:
        parts = sums
        for distance in reversed(bits_of(feat_count)):
            arrived = [xor_swap(part, "feat", distance) for part in parts[distance:]]
            parts = [add_pair_call(a, b) for a, b in zip(parts[:distance], arrived)]
        own = [parts[0], jnp.zeros_like(parts[0]), jnp.zeros_like(parts[0])]
    (keep_a,), (got_a,) = fold("fold0", 0, [keep], [got_core], 1)
    keep_a, got_a = fold_half("fold1", keep_a, got_a)
    if whole_step:
        coarse_all = coarse_rows_call(sums[3], relay, 3 * coarse.shape[0])
        parts = [coarse_all] + [xor_swap(coarse_all, "patch", j) for j in range(1, 4)]
    else:
        counts = jnp.pad(coarse[:, 2 * latent :], ((0, 0), (128, latent - 256)))
        parts = [jnp.concatenate([coarse[:, :latent], coarse[:, latent : 2 * latent], counts], axis=0)]
    back = node_back_call(*own, pre_sum, weight_in)
    (keep,), (received,) = fold("fold2", len(steps) - 1, [keep_a], [got_a], 1)
    node_new, grad_node = node_call(
        where, coarse_row, node_lat, node_cotangent, aggregate, back, parts
    )
    scale = 1.0 / math.sqrt(edge_count * patch_count * feat_count)
    in_rows = 3 * latent // patch_count
    grads_in, grads_out = last_grads_call(scale, keep.reshape(span, width), received.reshape(span, width), in_rows)
    return (
        edge_new.reshape(edge_lat.shape),
        node_new,
        grad_edge.reshape(edge_lat.shape),
        grad_node,
        grads_in,
        grads_out,
    )


def solution(mesh):
    return jax.shard_map(
        shards,
        mesh=mesh,
        in_specs=(
            P(("groups", "patch", "feat"), None),
            P(("groups", "patch", "feat"), None, None),
            P(None, ("patch", "feat")),
            P("patch"),
            P(("patch", "feat")),
            P(),
            P(),
            P(),
            P(),
            P(("groups", "patch", "feat"), None, None),
            P(("groups", "patch", "feat"), None),
        ),
        out_specs=(
            P(("groups", "patch", "feat"), None, None),
            P(("groups", "patch", "feat"), None),
            P(("groups", "patch", "feat"), None, None),
            P(("groups", "patch", "feat"), None),
            P(("groups", "patch"), "feat"),
            P(("groups", "patch"), "feat"),
        ),
        check_vma=False,
    )
```

```python
import functools
import math

import jax
import jax.numpy as jnp
from jax import lax
from jax.experimental import pallas as pl
from jax.experimental.pallas import tpu as pltpu
from jax.sharding import PartitionSpec as P

COARSE_DEV = 4
LAYER_EPS = 1e-05
F32 = jnp.float32
BF16 = jnp.bfloat16
VMEM_LIMIT = 24 * 1024 * 1024
EDGE_LIMIT = 24 * 1024 * 1024
COLS = (((1,), (1,)), ((), ()))
ROWS = (((0,), (0,)), ((), ()))


def dot(a, b):
    return jnp.dot(a, b, preferred_element_type=F32)


def params(limit=None):
    return pltpu.CompilerParams(vmem_limit_bytes=limit or VMEM_LIMIT)


COST = {
    "base_terms": 15,
    "select_rows": 2,
    "add_pair": 1,
    "edge_block": 36,
    "rim_sums": 2.4,
    "patch_sums": 0.3,
    "edge_grads": 0.3,
    "add_rim_sums": 0.3,
    "pack_grads": 0.3,
    "coarse_rows": 0.3,
    "near_sum": 0.3,
    "far_sum": 30,
    "node_outputs": 2,
    "grad_node": .1,
    "last_grads": 1.5,
    "coarse_sums": 1,
    "coarse_split": 1,
    "fold0": 0.3,
    "fold1": 0.3,
    "fold3": 0.3,
    "fold2": 0.3,
}


def cost(name):
    micros = COST[name]
    return pl.CostEstimate(flops=int(micros * 1.15e9), bytes_accessed=1 << 20, transcendentals=0)


class Order:
    token = None


def launch(kernel, out_shape, in_specs=None, out_specs=None, grid=None, **settings):
    outs = list(out_shape) if isinstance(out_shape, (list, tuple)) else [out_shape]
    mark = jax.ShapeDtypeStruct((8, 128), F32)

    def call(*args):
        count = len(args)
        late = [] if Order.token is None else [Order.token]
        vmem = pl.BlockSpec(memory_space=pltpu.VMEM)
        specs = list(in_specs or [vmem] * count) + [pl.BlockSpec(memory_space=pl.ANY)] * len(late)
        end = count + len(late) + len(outs)

        def body(*refs):
            refs[end][...] = jnp.zeros((8, 128), F32)
            kernel(*refs[:count], *refs[count + len(late) : end], *refs[end + 1 :])

        if grid is None:
            places, more = [vmem] * (len(outs) + 1), {}
        else:
            places = list(out_specs) if isinstance(out_specs, (list, tuple)) else [out_specs]
            places, more = places + [pl.BlockSpec((8, 128), lambda i: (0, 0))], {"grid": grid}
        results = pl.pallas_call(
            body, out_shape=outs + [mark], in_specs=specs, out_specs=places, **more, **settings
        )(*args, *late)
        Order.token = results[-1]
        return results[:-1] if isinstance(out_shape, (list, tuple)) else results[0]

    return call


def streamed(array):
    return pltpu.with_memory_space_constraint(array, pltpu.HBM)


def held(array):
    return pltpu.with_memory_space_constraint(array, pltpu.VMEM)


def whole(array):
    zeros = (0,) * array.ndim
    return pl.BlockSpec(array.shape, lambda i: zeros)


def rows(array, block):
    rest = (0,) * (array.ndim - 1)
    return pl.BlockSpec((block,) + array.shape[1:], lambda i: (i,) + rest)


def one_hot(ids, first, count):
    lanes = lax.broadcasted_iota(jnp.int32, (ids.shape[0], count), 1) + first
    return jnp.where(ids == lanes, 1.0, 0.0).astype(BF16)


def fill_table(table, pieces, weight_ref):
    latent = pieces[0].shape[1]
    at = 0
    for piece in pieces:
        size = piece.shape[0]
        table[at : at + size] = dot(piece[...], weight_ref[latent : 2 * latent]).astype(BF16)
        at += size


def base_kernel(degree, edge_ref, node_ref, ids_ref, weight_ref, bias_ref, *refs):
    pieces, (out_ref, table) = refs[:-2], refs[-2:]
    latent = edge_ref.shape[1]

    @pl.when(pl.program_id(0) == 0)
    def _():
        fill_table(table, pieces, weight_ref)

    edges = edge_ref.shape[0]
    term = dot(node_ref[...], weight_ref[2 * latent :]) + bias_ref[...]
    total = dot(edge_ref[...], weight_ref[:latent])
    total = total + dot(one_hot(ids_ref[...], 0, table.shape[0]), table[...])
    hidden = total.shape[1]
    total = total.reshape(edges // degree, degree, hidden) + term[:, None, :]
    out_ref[...] = total.reshape(edges, hidden)


def base_call(edges, nodes, ids, weight_in, bias, early, pieces, block):
    count, latent = edges.shape
    hidden = weight_in.shape[1]
    degree = count // nodes.shape[0]
    size = sum(piece.shape[0] for piece in pieces)
    return launch(
        lambda *refs: base_kernel(degree, *refs[:5], *refs[5 + len(early) :]),
        grid=(count // block,),
        in_specs=[
            rows(edges, block),
            rows(nodes, block // degree),
            rows(ids, block),
            whole(weight_in),
            whole(bias),
        ]
        + [pl.BlockSpec(memory_space=pl.ANY)] * len(early)
        + [whole(piece) for piece in pieces],
        out_specs=pl.BlockSpec((block, hidden), lambda i: (i, 0)),
        out_shape=jax.ShapeDtypeStruct((count, hidden), F32),
        scratch_shapes=[pltpu.VMEM((size, hidden), BF16)],
        compiler_params=params(),
        cost_estimate=cost("base_terms"),
        name="base_terms",
    )(streamed(edges), nodes, ids, weight_in, bias, *early, *pieces)


def edge_kernel(
    first,
    degree,
    base_ref,
    ids_ref,
    last_ref,
    low_ref,
    high_ref,
    edge_ref,
    cot_ref,
    ncot_ref,
    weight_ref,
    out_w_ref,
    gain_ref,
    new_ref,
    agg_ref,
    hid_ref,
    gproj_ref,
    gpre_ref,
    psum_ref,
    gedge_ref,
    table,
):
    latent = low_ref.shape[1]

    @pl.when(pl.program_id(0) == 0)
    def _():
        fill_table(table, (last_ref, low_ref, high_ref), weight_ref)

    ids = ids_ref[...]
    edges = ids.shape[0]
    nodes = edges // degree
    limit = first + table.shape[0]
    live = jnp.where(ids < limit, 1.0, 0.0)
    value = base_ref[...] + dot(one_hot(ids, first, table.shape[0]), table[...])
    sig = 0.5 + 0.5 * jnp.tanh(0.5 * value)
    act = value * sig
    slope = sig + act * (1.0 - sig)
    hid = act.astype(BF16)
    hid_ref[...] = hid
    projected = dot(hid, out_w_ref[...])
    centre = projected - jnp.mean(projected, axis=1, keepdims=True)
    inverse = lax.rsqrt(jnp.mean(centre * centre, axis=1, keepdims=True) + LAYER_EPS)
    normed = centre * inverse
    gain = gain_ref[...]
    message = normed * gain
    new_ref[...] = (edge_ref[...].astype(F32) + message).astype(BF16)
    pick = lax.broadcasted_iota(jnp.int32, (nodes, edges), 1) // degree
    pick = jnp.where(pick == lax.broadcasted_iota(jnp.int32, (nodes, edges), 0), 1.0, 0.0).astype(BF16)
    agg_ref[...] = dot(pick, (message * live).astype(BF16))
    ncot = jnp.broadcast_to(ncot_ref[...].astype(F32)[:, None, :], (nodes, degree, latent))
    cot = cot_ref[...].astype(F32)
    scaled = (cot + live * ncot.reshape(edges, latent)) * gain
    mean_a = jnp.mean(scaled, axis=1, keepdims=True)
    mean_b = jnp.mean(scaled * normed, axis=1, keepdims=True)
    gproj = (inverse * (scaled - mean_a - normed * mean_b)).astype(BF16)
    gproj_ref[...] = gproj
    gpre = (lax.dot_general(gproj, out_w_ref[...], COLS, preferred_element_type=F32) * slope).astype(BF16)
    gpre_ref[...] = gpre
    psum_ref[...] = dot(pick, gpre).astype(BF16)
    back = lax.dot_general(gpre, weight_ref[:latent], COLS, preferred_element_type=F32)
    gedge_ref[...] = (cot + back).astype(BF16)


def edge_call(base, ids, last, low, high, edges, cots, ncot, weight_in, weight_out, gain, first, block):
    count, latent = edges.shape
    hidden = weight_in.shape[1]
    degree = count // ncot.shape[0]
    blocks = count // block
    small = block // degree

    def like(width, dtype, size, total):
        return (
            pl.BlockSpec((size, width), lambda i: (i, 0)),
            jax.ShapeDtypeStruct((total, width), dtype),
        )

    outs = [
        like(latent, BF16, block, count),
        like(latent, F32, small, count // degree),
        like(hidden, BF16, block, count),
        like(latent, BF16, block, count),
        like(hidden, BF16, block, count),
        like(hidden, BF16, small, count // degree),
        like(latent, BF16, block, count),
    ]
    return launch(
        lambda *refs: edge_kernel(first, degree, *refs),
        grid=(blocks,),
        in_specs=[
            rows(base, block),
            rows(ids, block),
            whole(last),
            whole(low),
            whole(high),
            rows(edges, block),
            rows(cots, block),
            rows(ncot, small),
            whole(weight_in),
            whole(weight_out),
            whole(gain),
        ],
        out_specs=[spec for spec, _ in outs],
        out_shape=[shape for _, shape in outs],
        scratch_shapes=[pltpu.VMEM((last.shape[0] + 2 * low.shape[0], hidden), BF16)],
        compiler_params=params(EDGE_LIMIT),
        cost_estimate=cost("edge_block"),
        name="edge_block",
    )(base, ids, last, low, high, streamed(edges), streamed(cots), ncot, weight_in, weight_out, gain)


def select_kernel(ids_ref, *refs):
    pieces, (low_ref, high_ref) = refs[:-2], refs[-2:]
    total, at = None, 0
    for piece in pieces:
        term = dot(one_hot(ids_ref[...], at, piece.shape[0]), piece[...])
        total = term if total is None else total + term
        at += piece.shape[0]
    half = low_ref.shape[0]
    low_ref[...] = total[:half].astype(BF16)
    high_ref[...] = total[half:].astype(BF16)


def select_call(ids, pieces):
    count, width = ids.shape[0], pieces[0].shape[1]
    half = jax.ShapeDtypeStruct((count // 2, width), BF16)
    return launch(
        select_kernel,
        out_shape=[half, half],
        compiler_params=params(),
        cost_estimate=cost("select_rows"),
        name="select_rows",
    )(ids, *pieces)


def rim_sum_kernel(first, ids_ref, values_ref, mine_ref, got_ref, low_ref, high_ref, sum_ref):
    sum_ref[...] = mine_ref[...] + got_ref[...]
    half = low_ref.shape[0]
    places = lax.broadcasted_iota(jnp.int32, (2 * half, ids_ref.shape[1]), 0) + first
    hot = jnp.where(places == ids_ref[...], 1.0, 0.0).astype(BF16)
    total = dot(hot, values_ref[...])
    low_ref[...] = total[:half].astype(BF16)
    high_ref[...] = total[half:].astype(BF16)


def rim_sum_call(ids, values, mine, got, first, count):
    half = jax.ShapeDtypeStruct((count // 2, values.shape[1]), BF16)
    return launch(
        lambda *refs: rim_sum_kernel(first, *refs),
        out_shape=[half, half, jax.ShapeDtypeStruct(mine.shape, F32)],
        compiler_params=params(),
        cost_estimate=cost("rim_sums"),
        name="rim_sums",
    )(ids, values, mine, got)


def patch_sum_kernel(ids_ref, values_ref, out_ref):
    size = out_ref.shape[0]
    places = lax.broadcasted_iota(jnp.int32, (size, ids_ref.shape[1]), 0) + pl.program_id(0) * size
    hot = jnp.where(places == ids_ref[...], 1.0, 0.0).astype(BF16)
    out_ref[...] = dot(hot, values_ref[...])


def patch_sum_call(ids, values, count, block):
    width = values.shape[1]
    return launch(
        patch_sum_kernel,
        grid=(count // block,),
        in_specs=[whole(ids), whole(values)],
        out_specs=pl.BlockSpec((block, width), lambda i: (i, 0)),
        out_shape=jax.ShapeDtypeStruct((count, width), F32),
        compiler_params=params(),
        cost_estimate=cost("patch_sums"),
        name="patch_sums",
    )(ids, values)


def add_rim_kernel(ids_ref, low_ref, high_ref, start_ref, coarse_ref, *outs):
    half = low_ref.shape[0]
    size = outs[0].shape[0]
    latent = start_ref.shape[1]
    coarse = coarse_ref[...]
    few = coarse.shape[0]
    counts = coarse[:, 2 * latent :]
    high = jnp.floor(counts * (1.0 / 64.0))
    for j, out in enumerate(outs):
        places = lax.broadcasted_iota(jnp.int32, (size, 2 * half), 0) + j * size
        hot = jnp.where(places == ids_ref[...], 1.0, 0.0).astype(BF16)
        total = start_ref[j * size : (j + 1) * size] + dot(hot[:, :half], low_ref[...])
        total = total + dot(hot[:, half:], high_ref[...])
        out[:size] = total.astype(BF16)
        if out.shape[0] > size:
            out[size : size + few] = coarse[:, :latent].astype(BF16)
            out[size + few : size + 2 * few] = coarse[:, latent : 2 * latent].astype(BF16)
            out[size + 2 * few :] = jnp.zeros((few, latent), BF16)
            out[size + 2 * few :, :128] = high.astype(BF16)
            out[size + 2 * few :, 128:256] = (counts - 64.0 * high).astype(BF16)


def add_rim_call(ids, low, high, start, coarse, size, extended):
    count, width = start.shape
    pieces = count // size
    extra = [3 * coarse.shape[0] if extended and j == pieces - 1 else 0 for j in range(pieces)]
    return launch(
        add_rim_kernel,
        out_shape=[jax.ShapeDtypeStruct((size + more, width), BF16) for more in extra],
        compiler_params=params(),
        cost_estimate=cost("add_rim_sums"),
        name="add_rim_sums",
    )(ids, low, high, start, coarse)


def edge_grads_kernel(edge_ref, gpre_ref, hid_ref, gproj_ref, in_ref, out_ref):
    in_ref[...] = lax.dot_general(edge_ref[...], gpre_ref[...], ROWS, preferred_element_type=F32)
    out_ref[...] = lax.dot_general(hid_ref[...], gproj_ref[...], ROWS, preferred_element_type=F32)


def edge_grads_call(edges, gpre, hid, gproj):
    latent, hidden = edges.shape[1], gpre.shape[1]
    return launch(
        edge_grads_kernel,
        out_shape=[
            jax.ShapeDtypeStruct((latent, hidden), F32),
            jax.ShapeDtypeStruct((hidden, latent), F32),
        ],
        compiler_params=params(),
        cost_estimate=cost("edge_grads"),
        name="edge_grads",
    )(edges, gpre, hid, gproj)


def pack_kernel(pieces, where_ref, psum_ref, edge_ref, out_ref, patch_ref, low_ref, high_ref, *refs):
    tables = refs[:pieces]
    keep_ref, send_ref, total = refs[pieces:]
    latent = tables[0].shape[1]
    size = tables[0].shape[0]
    parts = [patch_ref[j * size : (j + 1) * size].astype(BF16) for j in range(pieces - 2)]
    grad = None
    for table, part in zip(tables, parts + [low_ref[...], high_ref[...]]):
        term = lax.dot_general(table[...], part, ROWS, preferred_element_type=F32)
        grad = term if grad is None else grad + term
    total[:latent] = grad
    total[latent:] = lax.dot_general(tables[0][...], psum_ref[...], ROWS, preferred_element_type=F32)
    feats, pairs, span, width = keep_ref.shape
    unit = span // 4

    def block(patch, slot):
        row = (patch * 3 + slot) * unit if slot < 3 else 3 * latent + patch * unit
        for ref, start, end in ((edge_ref, 0, latent), (total, latent, 3 * latent), (out_ref, 3 * latent, 4 * latent)):
            if start <= row < end:
                return ref[row - start : row - start + unit]

    for bit in range(2):

        @pl.when((where_ref[0] & 1) == bit)
        def _():
            for m in range(pairs):
                for slot in range(4):
                    for ref, which in ((keep_ref, bit), (send_ref, 1 - bit)):
                        rows_in = block(2 * m + which, slot)
                        for f in range(feats):
                            ref[f, m, slot * unit : (slot + 1) * unit, :] = rows_in[
                                :, f * width : (f + 1) * width
                            ].astype(ref.dtype)


def pack_call(where, psum, edge_grad, out_grad, patch_sum, low, high, tables, feats, patches):
    latent, hidden = edge_grad.shape
    shape = (feats, patches // 2, 4 * latent // patches, hidden // feats)
    vmem = pl.BlockSpec(memory_space=pltpu.VMEM)
    return launch(
        lambda *refs: pack_kernel(len(tables), *refs),
        in_specs=[pl.BlockSpec(memory_space=pltpu.SMEM)] + [vmem] * (6 + len(tables)),
        out_shape=[jax.ShapeDtypeStruct(shape, F32), jax.ShapeDtypeStruct(shape, BF16)],
        scratch_shapes=[pltpu.VMEM((2 * latent, hidden), F32)],
        compiler_params=params(),
        cost_estimate=cost("pack_grads"),
        name="pack_grads",
    )(where, psum, edge_grad, out_grad, patch_sum, low, high, *tables)


def coarse_sum_kernel(ids_ref, lat_ref, cot_ref, where_ref, mine_ref, other_ref):
    latent = lat_ref.shape[1]
    half = mine_ref.shape[0]
    core = where_ref[0] & 1
    for ref, bit in ((mine_ref, core), (other_ref, 1 - core)):
        places = lax.broadcasted_iota(jnp.int32, (half, ids_ref.shape[1]), 0) + bit * half
        live = jnp.where(places == ids_ref[...], 1.0, 0.0)
        hot = live.astype(BF16)
        ref[:, :latent] = dot(hot, lat_ref[...])
        ref[:, latent : 2 * latent] = dot(hot, cot_ref[...])
        ref[:, 2 * latent :] = jnp.broadcast_to(jnp.sum(live, axis=1, keepdims=True), (half, 128))


def coarse_sum_call(ids, lat, cot, where, coarse):
    vmem = pl.BlockSpec(memory_space=pltpu.VMEM)
    half = jax.ShapeDtypeStruct((coarse // 2, 2 * lat.shape[1] + 128), F32)
    return launch(
        coarse_sum_kernel,
        in_specs=[vmem, vmem, vmem, pl.BlockSpec(memory_space=pltpu.SMEM)],
        out_shape=[half, half],
        compiler_params=params(),
        cost_estimate=cost("coarse_sums"),
        name="coarse_sums",
    )(ids, lat, cot, where)


def add_pair_kernel(a_ref, b_ref, out_ref):
    out_ref[...] = (a_ref[...].astype(F32) + b_ref[...].astype(F32)).astype(out_ref.dtype)


def add_pair_call(a, b):
    return launch(
        add_pair_kernel,
        out_shape=jax.ShapeDtypeStruct(a.shape, a.dtype),
        compiler_params=params(),
        cost_estimate=cost("add_pair"),
        name="add_pair",
    )(a, b)


def coarse_rows_kernel(sent_ref, got_ref, out_ref):
    few = out_ref.shape[0]
    out_ref[...] = (sent_ref[-few:].astype(F32) + got_ref[-few:].astype(F32)).astype(BF16)


def coarse_rows_call(sent, got, few):
    return launch(
        coarse_rows_kernel,
        out_shape=jax.ShapeDtypeStruct((few, sent.shape[1]), BF16),
        compiler_params=params(),
        cost_estimate=cost("coarse_rows"),
        name="coarse_rows",
    )(sent, got)


def far_sum_kernel(own_ref, got_ref, out_ref):
    size = own_ref.shape[0]
    out_ref[...] = (own_ref[...].astype(F32) + got_ref[:size].astype(F32)).astype(BF16)


def far_sum_call(own, got):
    return launch(
        far_sum_kernel,
        out_shape=jax.ShapeDtypeStruct(own.shape, BF16),
        compiler_params=params(),
        cost_estimate=cost("far_sum"),
        name="far_sum",
    )(own, got)


def near_sum_kernel(own_ref, got_ref, out_ref):
    out_ref[...] = own_ref[...].astype(F32) + got_ref[...].astype(F32)


def near_sum_call(own, got):
    return launch(
        near_sum_kernel,
        out_shape=jax.ShapeDtypeStruct(own.shape, F32),
        compiler_params=params(),
        cost_estimate=cost("near_sum"),
        name="near_sum",
    )(own, got)


def add_split_kernel(axis, shift, count, where_ref, *refs):
    keeps, gots = refs[:count], refs[count : 2 * count]
    outs = refs[2 * count :]
    parts = len(outs) // 2
    bit = (where_ref[axis] >> shift) & 1
    for refs_out, which in ((outs[:parts], bit), (outs[parts:], 1 - bit)):
        piece = refs_out[0].shape[1]
        for a in range(keeps[0].shape[0]):
            at = 0
            for keep, got in zip(keeps, gots):
                size = min(piece, keep.shape[2])
                for row in range(0, keep.shape[2], size):
                    rows_in = slice(row, row + size)
                    out, first = refs_out[at // piece], at % piece
                    total = keep[a, which, rows_in] + got[a, which, rows_in].astype(F32)
                    out[a, first : first + size] = total.astype(out.dtype)
                    at += size


def add_split_call(name, where, axis, distance, keeps, gots, parts, send_type):
    vmem = pl.BlockSpec(memory_space=pltpu.VMEM)
    total = sum(keep.shape[2] for keep in keeps)
    shape = keeps[0].shape[:1] + (total // parts,) + keeps[0].shape[3:]
    outs = launch(
        functools.partial(add_split_kernel, axis, distance.bit_length() - 1, len(keeps)),
        in_specs=[pl.BlockSpec(memory_space=pltpu.SMEM)] + [vmem] * (2 * len(keeps)),
        out_shape=[jax.ShapeDtypeStruct(shape, F32)] * parts + [jax.ShapeDtypeStruct(shape, send_type)] * parts,
        compiler_params=params(),
        cost_estimate=cost(name),
        name=name,
    )(where, *keeps, *gots)
    return outs[:parts], outs[parts:]


def last_grads_kernel(scale, keep_ref, got_ref, in_ref, out_ref):
    rows_in = in_ref.shape[0]
    in_ref[...] = (keep_ref[:rows_in] + got_ref[:rows_in].astype(F32)) * scale
    out_ref[...] = (keep_ref[rows_in:] + got_ref[rows_in:].astype(F32)) * scale


def last_grads_call(scale, keep, got, rows_in):
    span, width = keep.shape
    return launch(
        lambda *refs: last_grads_kernel(scale, *refs),
        out_shape=[
            jax.ShapeDtypeStruct((rows_in, width), F32),
            jax.ShapeDtypeStruct((span - rows_in, width), F32),
        ],
        compiler_params=params(),
        cost_estimate=cost("last_grads"),
        name="last_grads",
    )(keep, got)


def node_kernel(where_ref, ids_ref, lat_ref, cot_ref, agg_ref, back_ref, *refs):
    pieces, (new_ref, grad_ref, total) = refs[:-3], refs[-3:]
    latent = lat_ref.shape[1]
    for j, piece in enumerate(pieces):
        size = piece.shape[0] // 3
        owner = where_ref[0] ^ j
        place = (owner & 1) * 2 + (owner >> 1) if len(pieces) == 4 else j
        here = pl.ds(pl.multiple_of(place * size, size), size)
        total[here, :latent] = piece[:size].astype(F32)
        total[here, latent : 2 * latent] = piece[size : 2 * size].astype(F32)
        counts = piece[2 * size :].astype(F32)
        total[here, 2 * latent :] = 64.0 * counts[:, :128] + counts[:, 128:256]
    sums = total[...]
    means = sums[:, : 2 * latent] / jnp.maximum(sums[:, 2 * latent : 2 * latent + 1], 1.0)
    places = lax.broadcasted_iota(jnp.int32, (sums.shape[0], ids_ref.shape[1]), 0)
    hot = jnp.where(places == ids_ref[...], 1.0, 0.0).astype(BF16)
    high = means.astype(BF16)
    low = (means - high.astype(F32)).astype(BF16)
    pooled = lax.dot_general(hot, high, ROWS, preferred_element_type=F32)
    pooled = pooled + lax.dot_general(hot, low, ROWS, preferred_element_type=F32)
    new_ref[...] = (lat_ref[...].astype(F32) + agg_ref[...] + pooled[:, :latent]).astype(BF16)
    grad_ref[...] = (cot_ref[...].astype(F32) + back_ref[...] + pooled[:, latent:]).astype(BF16)


def node_call(where, ids, lat, cot, agg, back, pieces):
    vmem = pl.BlockSpec(memory_space=pltpu.VMEM)
    coarse = sum(piece.shape[0] // 3 for piece in pieces)
    width = 2 * lat.shape[1] + 128
    return launch(
        node_kernel,
        in_specs=[pl.BlockSpec(memory_space=pltpu.SMEM)] + [vmem] * (5 + len(pieces)),
        scratch_shapes=[pltpu.VMEM((coarse, width), F32)],
        out_shape=[jax.ShapeDtypeStruct(lat.shape, BF16)] * 2,
        compiler_params=params(),
        cost_estimate=cost("node_outputs"),
        name="node_outputs",
    )(where, ids, lat, cot, agg, back, *pieces)


def node_back_kernel(own_ref, far_ref, psum_ref, weight_ref, out_ref):
    latent = own_ref.shape[1]
    total = own_ref[...] + far_ref[...].astype(F32)
    back = lax.dot_general(
        total.astype(BF16), weight_ref[latent : 2 * latent], COLS, preferred_element_type=F32
    )
    own = lax.dot_general(psum_ref[...], weight_ref[2 * latent :], COLS, preferred_element_type=F32)
    out_ref[...] = back + own


def node_back_call(own, far, psum, weight_in):
    return launch(
        node_back_kernel,
        out_shape=jax.ShapeDtypeStruct(own.shape, F32),
        compiler_params=params(),
        cost_estimate=cost("grad_node"),
        name="grad_node",
    )(own, far, psum, weight_in)


def xor_swap(value, axis, distance):
    size = lax.axis_size(axis)
    return lax.ppermute(value, axis, [(i, i ^ distance) for i in range(size)])


def bits_of(size):
    return [1 << b for b in range(size.bit_length() - 1)]


def split(value, dim, bit):
    mine = lax.dynamic_index_in_dim(value, bit, dim, keepdims=False)
    other = lax.dynamic_index_in_dim(value, 1 - bit, dim, keepdims=False)
    return mine, other


def coarse_reduce(sums, other, patch):
    width = sums.shape[1]
    bits = bits_of(lax.axis_size("patch"))
    sums = sums + xor_swap(other, "patch", 1)
    for distance in bits[1:]:
        mine, other = split(sums.reshape(2, -1, width), 0, (patch // distance) % 2)
        sums = mine + xor_swap(other, "patch", distance)
    for distance in bits_of(lax.axis_size("feat")):
        sums = sums + xor_swap(sums, "feat", distance)
    for distance in reversed(bits):
        got = xor_swap(sums, "patch", distance)
        first = (patch // distance) % 2 == 0
        sums = jnp.concatenate([jnp.where(first, sums, got), jnp.where(first, got, sums)], axis=0)
    return sums


def shards(
    node_lat,
    edge_lat,
    neighbours,
    send_rows,
    coarse_of,
    weight_in,
    bias_in,
    weight_out,
    norm_gain,
    edge_cotangent,
    node_cotangent,
):
    Order.token = None
    node_count, latent = node_lat.shape
    degree = edge_lat.shape[1]
    edge_count = node_count * degree
    rim_rows = send_rows.shape[0] // 2
    feat_count = lax.axis_size("feat")
    patch_count = lax.axis_size("patch")
    patch_total = feat_count * node_count
    coarse_total = COARSE_DEV * patch_count * feat_count
    feat = lax.axis_index("feat")
    patch = lax.axis_index("patch")
    block = min(512, edge_count)
    ring_up = [(i, (i + 1) % patch_count) for i in range(patch_count)]
    ring_down = [(j, i) for i, j in ring_up]

    def relative(ids):
        moved = ((ids // node_count) ^ feat) * node_count + ids % node_count
        return jnp.where(ids < patch_total, moved, ids)

    flat_edges = edge_lat.reshape(edge_count, latent)
    flat_cots = edge_cotangent.reshape(edge_count, latent)
    ids = relative(neighbours).T.reshape(edge_count)
    ids_col = ids[:, None]
    ids_row = ids[None, :]
    send_rel = relative(send_rows)
    send_col = send_rel[:, None]
    send_row = send_rel[None, :]
    bias = bias_in[None, :]
    gain = norm_gain[None, :]
    coarse_row = coarse_of[None, :]

    where = jnp.stack([patch, feat]).astype(jnp.int32)
    whole_step = feat_count == 4 and patch_count == 4

    if feat_count == 4:
        far = xor_swap(node_lat, "feat", 2)
        near = xor_swap(node_lat, "feat", 1)
        last = xor_swap(far, "feat", 1)
        pieces = [node_lat, near, far, last]
    else:
        pieces = [node_lat]
        for distance in bits_of(feat_count):
            pieces = pieces + [xor_swap(piece, "feat", distance) for piece in pieces]

    coarse, coarse_other = coarse_sum_call(coarse_row, node_lat, node_cotangent, where, coarse_total)
    if whole_step:
        got = xor_swap(coarse_other, "patch", 1)
        halves = (1, 2, coarse.shape[0] // 2, coarse.shape[1])
        (coarse,), (coarse_other,) = add_split_call(
            "coarse_split", where, 0, 2, [coarse.reshape(halves)], [got.reshape(halves)], 1, F32
        )
        coarse, coarse_other = coarse[0], coarse_other[0]
        got = xor_swap(coarse_other, "patch", 2)
    else:
        coarse = coarse_reduce(coarse, coarse_other, patch)
        got = jnp.zeros_like(coarse)
    base = base_call(
        flat_edges, node_lat, ids_col, weight_in, bias, (ids_row, send_col, send_row, coarse_row), pieces[:-1], block
    )
    to_lower, to_upper = select_call(send_col, pieces)
    from_lower = lax.ppermute(to_upper, "patch", ring_up)
    from_upper = lax.ppermute(to_lower, "patch", ring_down)
    coarse = add_pair_call(coarse, got)
    got = xor_swap(coarse, "feat", 2) if whole_step else jnp.zeros_like(coarse)

    edge_new, aggregate, hidden_act, grad_proj, grad_pre, pre_sum, grad_edge = edge_call(
        base,
        ids_col,
        pieces[-1],
        from_lower,
        from_upper,
        flat_edges,
        flat_cots,
        node_cotangent,
        weight_in,
        weight_out,
        gain,
        patch_total - node_count,
        block)

    rim_low, rim_high, coarse = rim_sum_call(ids_row, grad_pre, coarse, got, patch_total, 2 * rim_rows)
    back_upper = lax.ppermute(rim_low, "patch", ring_down)
    back_lower = lax.ppermute(rim_high, "patch", ring_up)
    patch_sum = patch_sum_call(ids_row, grad_pre, patch_total, 2 * node_count)
    span, width = 4 * latent // patch_count, latent // feat_count
    steps = [("patch", d) for d in bits_of(patch_count)[1:]] + [("feat", d) for d in bits_of(feat_count)]

    def fold(name, step, keeps, gots, parts):
        axis, distance = steps[step]
        shape = lambda x: (-1, 2) + x.shape[-2:]
        keeps, sends = add_split_call(
            name,
            where,
            int(axis == "feat"),
            distance,
            [x.reshape(shape(x)) for x in keeps],
            [x.reshape(shape(x)) for x in gots],
            parts,
            BF16,
        )
        return keeps, [xor_swap(x, axis, distance) for x in sends]

    def fold_half(name, keep, got):
        for step in range(1, len(steps) - 1):
            (keep,), (got,) = fold(name, step, [keep], [got], 1)
        return keep, got

    sums = add_rim_call(
        send_row, back_lower, back_upper, patch_sum, coarse, node_count, whole_step
    )
    edge_grad, out_grad = edge_grads_call(flat_edges, grad_pre, hidden_act, grad_proj)
    tables = pieces + [from_lower, from_upper]
    keep, send = pack_call(
        where, pre_sum, edge_grad, out_grad, patch_sum, rim_low, rim_high, tables, feat_count, patch_count
    )
    got_core = xor_swap(send, "patch", 1)
    if feat_count == 4:
        relay = xor_swap(sums[3], "feat", 1)
        far_sum = far_sum_call(sums[2], relay)
        got_far = xor_swap(far_sum, "feat", 2)
        got_near = xor_swap(sums[1], "feat", 1)
        own = [got_near, got_far]
    else:
        parts = sums
        for distance in reversed(bits_of(feat_count)):
            arrived = [xor_swap(part, "feat", distance) for part in parts[distance:]]
            parts = [add_pair_call(a, b) for a, b in zip(parts[:distance], arrived)]
        sums = parts
        own = [jnp.zeros_like(parts[0]), jnp.zeros_like(parts[0])]
    (keep_a,), (got_a,) = fold("fold0", 0, [keep], [got_core], 1)
    own_sum = near_sum_call(sums[0], own[0])
    keep_a, got_a = fold_half("fold1", keep_a, got_a)
    if whole_step:
        coarse_all = coarse_rows_call(sums[3], relay, 3 * coarse.shape[0])
        parts = [coarse_all] + [xor_swap(coarse_all, "patch", j) for j in range(1, 4)]
    else:
        counts = jnp.pad(coarse[:, 2 * latent :], ((0, 0), (128, latent - 256)))
        parts = [jnp.concatenate([coarse[:, :latent], coarse[:, latent : 2 * latent], counts], axis=0)]
    back = node_back_call(own_sum, own[1], pre_sum, weight_in)
    (keep,), (received,) = fold("fold2", len(steps) - 1, [keep_a], [got_a], 1)
    node_new, grad_node = node_call(
        where, coarse_row, node_lat, node_cotangent, aggregate, back, parts
    )
    scale = 1.0 / math.sqrt(edge_count * patch_count * feat_count)
    in_rows = 3 * latent // patch_count
    grads_in, grads_out = last_grads_call(scale, keep.reshape(span, width), received.reshape(span, width), in_rows)
    return (
        edge_new.reshape(edge_lat.shape),
        node_new,
        grad_edge.reshape(edge_lat.shape),
        grad_node,
        grads_in,
        grads_out,
    )


def solution(mesh):
    return jax.shard_map(
        shards,
        mesh=mesh,
        in_specs=(
            P(("groups", "patch", "feat"), None),
            P(("groups", "patch", "feat"), None, None),
            P(None, ("patch", "feat")),
            P("patch"),
            P(("patch", "feat")),
            P(),
            P(),
            P(),
            P(),
            P(("groups", "patch", "feat"), None, None),
            P(("groups", "patch", "feat"), None),
        ),
        out_specs=(
            P(("groups", "patch", "feat"), None, None),
            P(("groups", "patch", "feat"), None),
            P(("groups", "patch", "feat"), None, None),
            P(("groups", "patch", "feat"), None),
            P(("groups", "patch"), "feat"),
            P(("groups", "patch"), "feat"),
        ),
        check_vma=False,
    )
```
